256 devices in a mesh: tm: 32 (over x, y, core), patch: 8 (over z).
Axes of the slice: x: 4, y: 4, z: 8, core: 2. Of those that a mesh axis runs over, the one named last changes fastest.
Arguments:
- stream: bfloat16 [256, 128, 2048], P('patch', 'tm'), may hold values from -6 to 6
- spatial_gain: float32 [2048], replicated, may hold values from 0.1 to 1.9
- spatial_qkv: bfloat16 [2048, 3, 2048], P(None, None, 'patch')
- spatial_out: bfloat16 [2048, 2048], P('patch'), may hold values from -1 to 1
- temporal_gain: float32 [2048], replicated, may hold values from 0.1 to 1.9
- temporal_qkv: bfloat16 [2048, 3, 2048], P(None, None, 'patch')
- temporal_out: bfloat16 [2048, 2048], P('patch'), may hold values from -0.125 to 0.125
- starts: int32 [2], replicated, may hold values from 1 to 63
Outputs:
- block_out: bfloat16 [256, 128, 2048], P('patch', 'tm')
The draws below stay inside these ranges and needn't reach their ends.
All inputs are finite; a program needn't handle non-finite values.
Results may differ from the reference program's by a relative error of at most 0.02.
Values may be sent and summed in bfloat16 or wider, within the bound.
No kernel may reach another device: no remote copies, remote signals or barrier semaphores. Data moves between devices by JAX's collectives and lax.ppermute only.
A program may use at most 128 MiB of HBM per device.

```python
import math
import jax
import jax.numpy as jnp
from jax import lax

D = 2048
HEADS = 16
E = 128
P_SIZE = 256
SEQ = 64
FRAMES = 128
EPISODES = 2
N_PATCH = 8


def draw_projection(key):
    base_key = jax.random.fold_in(key, 0)
    base = jax.random.normal(base_key, (D, 3, HEADS * E), jnp.float32) / math.sqrt(D)
    query_part = base[:, 0]
    return jnp.stack([query_part, base[:, 1], base[:, 2]], axis=1).astype(jnp.bfloat16)


def draw_spatial_qkv(key, part):
    key = jax.random.fold_in(key, 7)
    return draw_projection(key)


def draw_temporal_qkv(key, part):
    key = jax.random.fold_in(key, 13)
    return draw_projection(key)


def level_of(stream_key, extent, cuts, smallest, largest):
    factor_of, own = 1.0, jax.random.fold_in(stream_key, 6)
    for dim, shards_of in cuts:
        draws = jnp.exp(jax.random.uniform(jax.random.fold_in(own, dim), (shards_of,), jnp.float32, smallest / len(cuts), largest / len(cuts)))
        factor_of = factor_of * jnp.repeat(draws, extent[dim] // shards_of).reshape([-1 if axis == dim else 1 for axis in range(len(extent))])
    return factor_of


def centred(key, dims, scale, limit, cuts=(), kind=jnp.bfloat16):
    result = jax.random.normal(key, dims, jnp.float32) * scale
    if len(cuts) > 0:
        result = level_of(key, dims, cuts, -0.22, 0.18) * result
    return jnp.clip(result, min=-limit, max=limit).astype(kind)


def setup_inputs(seed: int = 0) -> dict:
    keys = jax.random.split(jax.random.key(seed), 9)
    stream = centred(keys[0], (P_SIZE, FRAMES, D), 1.0, 6.0, ((0, 8), (1, 32)))
    spatial_gain = jnp.clip(1.0 + 0.18 * jax.random.normal(keys[1], (D,), jnp.float32), 0.1, 1.9)
    spatial_qkv = draw_spatial_qkv(jax.random.fold_in(keys[8], 71), 0)
    spatial_out = centred(keys[3], (HEADS * E, D), (max(1, HEADS * E // 64)) ** -0.5, 1.0, ((0, 8),))
    temporal_gain = jnp.clip(1.0 + 0.18 * jax.random.normal(keys[4], (D,), jnp.float32), 0.1, 1.9)
    temporal_qkv = draw_temporal_qkv(jax.random.fold_in(keys[8], 71), 0)
    temporal_out = centred(keys[6], (HEADS * E, D), (HEADS * E) ** -0.5, 0.125, ((0, 8),))
    starts = jax.random.randint(keys[7], (EPISODES,), 1, SEQ).astype(jnp.int32)
    return {"stream": stream, "spatial_gain": spatial_gain, "spatial_qkv": spatial_qkv, "spatial_out": spatial_out, "temporal_gain": temporal_gain, "temporal_qkv": temporal_qkv, "temporal_out": temporal_out, "starts": starts}


def rms_norm(stream, gain):
    values = stream.astype(jnp.float32)
    scaled = values * lax.rsqrt(lax.optimization_barrier(jnp.mean(values * values, axis=-1, keepdims=True)) + 1e-05)
    return (scaled * gain).astype(jnp.bfloat16)

def project(normed, weight):
    flat_rows = normed.reshape(-1, D)
    output = jnp.dot(flat_rows, weight.reshape(D, -1), preferred_element_type=jnp.float32).astype(jnp.bfloat16)
    return output.reshape(normed.shape[:-1] + (3, HEADS, E))

def masked_softmax(scores, allowed):
    scores = jnp.where(allowed, scores, -1e+30)
    row_max = lax.optimization_barrier(jnp.max(scores, axis=-1, keepdims=True))
    shifted = jnp.exp(scores - row_max)
    return (shifted / lax.optimization_barrier(jnp.sum(shifted, axis=-1, keepdims=True))).astype(jnp.bfloat16)

def spatial_frame(block):
    query_rows = block[:, 0].astype(jnp.float32)
    key_rows = block[:, 1].astype(jnp.float32)
    value_rows = block[:, 2].astype(jnp.float32)
    scores = jnp.einsum('phe,qhe->hpq', query_rows, key_rows) * (1.0 / math.sqrt(E))
    attn_weights = masked_softmax(scores, True)
    return jnp.einsum('hpq,qhe->phe', attn_weights.astype(jnp.float32), value_rows).astype(jnp.bfloat16)

def out_project(mixed, weight):
    group_width = HEADS // N_PATCH * E
    summed = jnp.zeros((P_SIZE, FRAMES, D), jnp.float32)
    for group in range(N_PATCH):
        block = mixed[:, :, group * group_width:(group + 1) * group_width].reshape(-1, group_width)
        partial_sum = jnp.dot(block, weight[group * group_width:(group + 1) * group_width], preferred_element_type=jnp.float32).astype(jnp.bfloat16)
        partial_sum = lax.optimization_barrier(partial_sum)
        summed = summed + partial_sum.astype(jnp.float32).reshape(P_SIZE, FRAMES, D)
    return summed

def reference(stream, spatial_gain, spatial_qkv, spatial_out, temporal_gain, temporal_qkv, temporal_out, starts):
    spatial_rows = project(rms_norm(stream, spatial_gain), spatial_qkv)
    per_frame = lax.map(spatial_frame, jnp.moveaxis(spatial_rows, 1, 0))
    spatial_mix = jnp.moveaxis(per_frame, 0, 1).reshape(P_SIZE, FRAMES, HEADS * E)
    middle = (stream.astype(jnp.float32) + out_project(spatial_mix, spatial_out)).astype(jnp.bfloat16)
    temporal_rows = project(rms_norm(middle, temporal_gain), temporal_qkv).reshape(P_SIZE, EPISODES, SEQ, 3, HEADS, E)
    positions = jnp.arange(SEQ, dtype=jnp.int32)
    segment = positions[None, :] >= starts[:, None]
    allowed = (positions[None, :, None] >= positions[None, None, :]) & (segment[:, :, None] == segment[:, None, :])
    query_rows = temporal_rows[:, :, :, 0].astype(jnp.float32)
    key_rows = temporal_rows[:, :, :, 1].astype(jnp.float32)
    value_rows = temporal_rows[:, :, :, 2].astype(jnp.float32)
    scores = jnp.einsum('pbthe,pbuhe->pbhtu', query_rows, key_rows) * (1.0 / math.sqrt(E))
    attn_weights = masked_softmax(scores, allowed[None, :, None])
    temporal_mix = jnp.einsum('pbhtu,pbuhe->pbthe', attn_weights.astype(jnp.float32), value_rows).astype(jnp.bfloat16)
    temporal_mix = temporal_mix.reshape(P_SIZE, FRAMES, HEADS * E)
    return (middle.astype(jnp.float32) + out_project(temporal_mix, temporal_out)).astype(jnp.bfloat16)
```

```python
import functools
import math

import jax
import jax.numpy as jnp
from jax import lax
from jax.experimental import pallas as pl
from jax.experimental.pallas import tpu as pltpu
from jax.sharding import Mesh
from jax.sharding import PartitionSpec as P

E = 128
SEQ = 64
SCALE = 1.0 / math.sqrt(E)
BF = jnp.bfloat16
F32 = jnp.float32
NZ = 8
VMEM_LIMIT = 56 * 1024 * 1024
OFFSETS = (0, -1, 1, -2, 2, -3, 3, 4)


def params():
    return pltpu.CompilerParams(vmem_limit_bytes=VMEM_LIMIT)


def vmem():
    return pl.BlockSpec(memory_space=pltpu.VMEM)


def smem():
    return pl.BlockSpec(memory_space=pltpu.SMEM)


def normed(values, gain):
    scaled = values * lax.rsqrt(jnp.mean(values * values, axis=-1, keepdims=True) + 1e-05)
    return (scaled * gain).astype(BF)


def softmax(scores):
    shifted = jnp.exp(scores - jnp.max(scores, axis=-1, keepdims=True))
    return (shifted / jnp.sum(shifted, axis=-1, keepdims=True)).astype(BF)


def dot(a, b):
    return jnp.dot(a, b, preferred_element_type=F32)


def dot_t(a, b):
    return lax.dot_general(a, b, (((1,), (1,)), ((), ())), preferred_element_type=F32)


def norm_kernel(x_ref, gain_ref, a_ref, b_ref):
    gain = gain_ref[...]
    half = a_ref.shape[0]
    a_ref[...] = normed(x_ref[:half].astype(F32), gain)
    b_ref[...] = normed(x_ref[half:].astype(F32), gain)


def norm_rows(rows, gain):
    count, width = rows.shape
    half = jax.ShapeDtypeStruct((count // 2, width), BF)
    return pl.pallas_call(
        norm_kernel,
        out_shape=(half, half),
        in_specs=[vmem(), vmem()],
        out_specs=(vmem(), vmem()),
        compiler_params=params(),
        cost_estimate=pl.CostEstimate(
            flops=4 * count * width, bytes_accessed=4 * count * width, transcendentals=0
        ),
    )(rows, gain)


def spatial_kernel(place_ref, weight_ref, *refs):
    out_ref = refs[-1]
    pieces = refs[:-1]
    place = place_ref[0]
    for frame in range(4):
        part, inner = frame // 2, frame % 2
        rows = jnp.concatenate(
            [pieces[2 * k + part][32 * inner : 32 * inner + 32, :] for k in range(NZ)], axis=0
        )
        qkv = dot(rows, weight_ref[...]).astype(BF)
        for head in range(2):
            low = head * E
            query = qkv[:, low : low + E]
            key = qkv[:, 256 + low : 256 + low + E]
            value = qkv[:, 512 + low : 512 + low + E]
            weights = softmax(dot_t(query, key) * SCALE)
            mixed = dot(weights, value).astype(BF)
            for k in range(NZ):
                target = lax.rem(place + (OFFSETS[k] + NZ), NZ)
                out_ref[target, 32 * frame : 32 * frame + 32, low : low + E] = mixed[
                    32 * k : 32 * k + 32
                ]


def spatial_attend(place, weight, pieces):
    return pl.pallas_call(
        spatial_kernel,
        out_shape=jax.ShapeDtypeStruct((NZ, 128, 256), BF),
        in_specs=[smem(), vmem()] + [vmem()] * len(pieces),
        out_specs=vmem(),
        compiler_params=params(),
        cost_estimate=pl.CostEstimate(
            flops=2 * 1024 * 2048 * 768 * 2, bytes_accessed=8 << 20, transcendentals=8 * 65536
        ),
    )(place, weight, *pieces)


def middle_kernel(mix_ref, weight_ref, rows_ref, gain_ref, middle_ref, send_ref, total):
    step = pl.program_id(0)
    mix = jnp.concatenate([mix_ref[k] for k in range(NZ)], axis=1)
    blocks = weight_ref.shape[0]
    weight = jnp.concatenate([weight_ref[k] for k in range(blocks)], axis=1)
    width = blocks * E
    total[:, pl.ds(pl.multiple_of(step * width, width), width)] = dot(mix, weight)

    @pl.when(step == pl.num_programs(0) - 1)
    def _():
        middle = (total[...] + rows_ref[...].astype(F32)).astype(BF)
        middle_ref[...] = middle
        values = middle.astype(F32)
        scaled = values * lax.rsqrt(jnp.mean(values * values, axis=-1, keepdims=True) + 1e-05)
        scaled = scaled * gain_ref[...]
        for group in range(4):
            chunk = jnp.concatenate(
                [scaled[32 * f + 8 * group : 32 * f + 8 * group + 8] for f in range(4)], axis=0
            ).astype(BF)
            for y in range(4):
                send_ref[(group // 2) * 8 + y * 2 + group % 2] = chunk


def middle_rows(mix, weight, rows, gain):
    steps = 4
    width = rows.shape[1]
    return pl.pallas_call(
        middle_kernel,
        grid=(steps,),
        out_shape=(
            jax.ShapeDtypeStruct((128, width), BF),
            jax.ShapeDtypeStruct((16, 32, width), BF),
        ),
        in_specs=[
            pl.BlockSpec((NZ, 128, 256), lambda i: (0, 0, 0)),
            pl.BlockSpec((16 // steps, 2048, E), lambda i: (i, 0, 0)),
            pl.BlockSpec((128, width), lambda i: (0, 0)),
            pl.BlockSpec((1, width), lambda i: (0, 0)),
        ],
        out_specs=(
            pl.BlockSpec((128, width), lambda i: (0, 0)),
            pl.BlockSpec((16, 32, width), lambda i: (0, 0, 0)),
        ),
        scratch_shapes=[pltpu.VMEM((128, width), F32)],
        compiler_params=params(),
        cost_estimate=pl.CostEstimate(
            flops=2 * 128 * 2048 * 2048, bytes_accessed=12 << 20, transcendentals=0
        ),
    )(mix, weight, rows, gain)


def temporal_kernel(start_ref, rows_ref, weight_ref, out_ref, qkv, mix, total):
    step = pl.program_id(0)
    kind = lax.rem(step, 4)
    rows_count = rows_ref.shape[0]

    @pl.when(kind < 3)
    def _():
        weight = weight_ref[:, 0].reshape(2048, 256)
        part = dot(rows_ref[...], weight).astype(BF).astype(F32)
        qkv[2 * kind] = part[:, :E]
        qkv[2 * kind + 1] = part[:, E:]

    @pl.when(kind == 3)
    def _():
        start = start_ref[0]
        late = lax.broadcasted_iota(jnp.int32, (SEQ, SEQ), 0)
        early = lax.broadcasted_iota(jnp.int32, (SEQ, SEQ), 1)
        allowed = (early <= late) & ((early >= start) == (late >= start))
        for head in range(2):
            for patch in range(8):
                frames = pl.ds(patch, SEQ, stride=8)
                query = qkv[0 + head, frames, :].astype(BF)
                key = qkv[2 + head, frames, :].astype(BF)
                value = qkv[4 + head, frames, :].astype(BF)
                scores = jnp.where(allowed, dot_t(query, key) * SCALE, -1e30)
                mix[head, frames, :] = dot(softmax(scores), value)
        mixed = jnp.concatenate([mix[0], mix[1]], axis=1).astype(BF)
        for block in range(8):
            cols = slice(256 * block, 256 * block + 256)
            part = dot(mixed, weight_ref[block, 0])

            @pl.when(step == 3)
            def _():
                total[:, cols] = part

            @pl.when(step == 7)
            def _():
                out_ref[:, cols] = (total[:, cols] + part).astype(BF)


def temporal_attend(start, rows, weight):
    count, width = rows.shape
    return pl.pallas_call(
        temporal_kernel,
        grid=(8,),
        out_shape=jax.ShapeDtypeStruct((count, width), BF),
        in_specs=[
            smem(),
            pl.BlockSpec((count, width), lambda i: (0, 0)),
            pl.BlockSpec((8, 1, 256, 256), lambda i: (0, i, 0, 0)),
        ],
        out_specs=pl.BlockSpec((count, width), lambda i: (0, 0)),
        scratch_shapes=[
            pltpu.VMEM((6, count, E), F32),
            pltpu.VMEM((2, count, E), F32),
            pltpu.VMEM((count, width), F32),
        ],
        compiler_params=params(),
        cost_estimate=pl.CostEstimate(
            flops=2 * 512 * 2048 * 2048, bytes_accessed=14 << 20, transcendentals=131072
        ),
    )(start, rows, weight)


def shifted(value, axis, step):
    count = lax.axis_size(axis)
    return lax.ppermute(value, axis, [(i, (i + step) % count) for i in range(count)])


def gathered_rows(chunks):
    up, down = list(chunks), list(chunks)
    pieces = {0: list(chunks)}
    for step in (1, 2, 3):
        up = [shifted(value, "z", 1) for value in up]
        down = [shifted(value, "z", -1) for value in down]
        pieces[-step], pieces[step] = up, down
    pieces[4] = [shifted(up[0], "z", 1), shifted(down[1], "z", -1)]
    return [value for offset in OFFSETS for value in pieces[offset]]


def local(stream, spatial_gain, spatial_qkv, spatial_out, temporal_gain, temporal_qkv, temporal_out, starts):
    patches, frames, width = stream.shape
    w, xl, y, c, z = (lax.axis_index(name) for name in ("w", "xl", "y", "c", "z"))

    rows = jnp.transpose(stream, (1, 0, 2)).reshape(frames * patches, width)
    chunks = norm_rows(rows, spatial_gain.reshape(1, width))
    pieces = gathered_rows(chunks)

    column = (w * 2 + xl) * 4 + y
    share = lax.dynamic_slice(spatial_out, (0, column * E), (256, E))
    parts = []
    for k in range(4):
        pairs = [
            (a * 8 + b, (b // 4) * 8 + (b + 4 * a + k) % 8) for a in range(2) for b in range(8)
        ]
        parts.append(lax.ppermute(share, ("c", "z"), pairs))
    ring = jnp.stack([parts[0], parts[3], parts[2], parts[1]] * 2)
    share = lax.dynamic_slice(ring, (lax.rem(8 - z, 4), 0, 0), (4, 256, E)).reshape(1024, E)
    whole_out = lax.all_gather(share, ("w", "xl", "y", "c"), axis=0, tiled=True)
    whole_out = whole_out.reshape(16, 2048, E)

    eighth = (w * 2 + xl) * 2 + c
    qkv_rows = lax.dynamic_slice(temporal_qkv, (eighth * 256, 0, 0), (256, 3, 256))
    out_cols = lax.dynamic_slice(temporal_out, (0, eighth * 256), (256, 256))
    share = jnp.concatenate([jnp.transpose(qkv_rows, (1, 0, 2)), out_cols[None]], axis=0)
    got = []
    for k in range(8):
        pairs = []
        for a in range(4):
            for b in range(8):
                order = a * 2 + b % 2
                pairs.append((a * 8 + b, (b // 2) * 8 + (order + k) % 8))
        low = 64 * (k // 2)
        got.append(lax.ppermute(share[:, low : low + 64], ("y", "z"), pairs))
    even = jnp.concatenate(got[0::2], axis=1)
    odd = jnp.concatenate(got[1::2], axis=1)
    swap = lax.rem(z, 2) == 1
    share = jnp.concatenate([jnp.where(swap, odd, even), jnp.where(swap, even, odd)], axis=0)
    quarter = lax.all_gather(share[None], ("w", "xl", "c"), axis=0, tiled=True)

    mix = spatial_attend(z.reshape(1), spatial_qkv.reshape(width, -1), pieces)
    mix = lax.all_to_all(mix, "z", 0, 0, tiled=True)
    middle, send = middle_rows(mix, whole_out, rows, temporal_gain.reshape(1, width))

    window = lax.all_to_all(send, ("xl", "y", "c"), 0, 0, tiled=True)
    start = lax.dynamic_slice(starts, (w,), (1,))
    partial = temporal_attend(start, window.reshape(512, width), quarter)
    back = lax.all_to_all(partial.reshape(16, 32, width), ("xl", "y", "c"), 0, 0, tiled=True)
    summed = jnp.sum(back.reshape(2, 4, 2, 4, 8, width).astype(F32), axis=1)
    out = middle.reshape(4, 2, 2, 8, width).astype(F32) + jnp.transpose(summed, (2, 0, 1, 3, 4))
    out = out.astype(BF).reshape(frames, patches, width)
    return jnp.transpose(out, (1, 0, 2))


def solution(mesh):
    names = ("w", "xl", "y", "c", "z")
    fine = Mesh(mesh.devices.reshape(2, 2, 4, 2, NZ), names)
    tm = ("w", "xl", "y", "c")
    placed = (
        P("z", tm, None),
        P(),
        P(None, None, "z"),
        P("z", None),
        P(),
        P(None, None, "z"),
        P("z", None),
        P(),
    )
    return jax.shard_map(
        local, mesh=fine, in_specs=placed, out_specs=P("z", tm, None), check_vma=False
    )
```

```python
import functools
import math

import jax
import jax.numpy as jnp
from jax import lax
from jax.experimental import pallas as pl
from jax.experimental.pallas import tpu as pltpu
from jax.sharding import Mesh
from jax.sharding import PartitionSpec as P

E = 128
SEQ = 64
SCALE = 1.0 / math.sqrt(E)
BF = jnp.bfloat16
F32 = jnp.float32
NZ = 8
VMEM_LIMIT = 56 * 1024 * 1024
OFFSETS = (0, -1, 1, -2, 2, -3, 3, 4)


def params():
    return pltpu.CompilerParams(vmem_limit_bytes=VMEM_LIMIT)


def vmem():
    return pl.BlockSpec(memory_space=pltpu.VMEM)


def smem():
    return pl.BlockSpec(memory_space=pltpu.SMEM)


def normed(values, gain):
    scaled = values * lax.rsqrt(jnp.mean(values * values, axis=-1, keepdims=True) + 1e-05)
    return (scaled * gain).astype(BF)


def softmax(scores):
    shifted = jnp.exp(scores - jnp.max(scores, axis=-1, keepdims=True))
    return (shifted / jnp.sum(shifted, axis=-1, keepdims=True)).astype(BF)


def dot(a, b):
    return jnp.dot(a, b, preferred_element_type=F32)


def dot_t(a, b):
    return lax.dot_general(a, b, (((1,), (1,)), ((), ())), preferred_element_type=F32)


def norm_kernel(x_ref, gain_ref, a_ref, b_ref):
    gain = gain_ref[...]
    half = a_ref.shape[0]
    a_ref[...] = normed(x_ref[:half].astype(F32), gain)
    b_ref[...] = normed(x_ref[half:].astype(F32), gain)


def norm_rows(rows, gain):
    count, width = rows.shape
    half = jax.ShapeDtypeStruct((count // 2, width), BF)
    return pl.pallas_call(
        norm_kernel,
        out_shape=(half, half),
        in_specs=[vmem(), vmem()],
        out_specs=(vmem(), vmem()),
        compiler_params=params(),
        cost_estimate=pl.CostEstimate(
            flops=4 * count * width, bytes_accessed=4 * count * width, transcendentals=0
        ),
    )(rows, gain)


def spatial_kernel(place_ref, weight_ref, *refs):
    out_ref = refs[-1]
    pieces = refs[:-1]
    place = place_ref[0]
    for frame in range(4):
        part, inner = frame // 2, frame % 2
        rows = jnp.concatenate(
            [pieces[2 * k + part][32 * inner : 32 * inner + 32, :] for k in range(NZ)], axis=0
        )
        qkv = dot(rows, weight_ref[...]).astype(BF)
        for head in range(2):
            low = head * E
            query = qkv[:, low : low + E]
            key = qkv[:, 256 + low : 256 + low + E]
            value = qkv[:, 512 + low : 512 + low + E]
            weights = softmax(dot_t(query, key) * SCALE)
            mixed = dot(weights, value).astype(BF)
            for k in range(NZ):
                target = lax.rem(place + (OFFSETS[k] + NZ), NZ)
                out_ref[target, 32 * frame : 32 * frame + 32, low : low + E] = mixed[
                    32 * k : 32 * k + 32
                ]


def spatial_attend(place, weight, pieces):
    return pl.pallas_call(
        spatial_kernel,
        out_shape=jax.ShapeDtypeStruct((NZ, 128, 256), BF),
        in_specs=[smem(), vmem()] + [vmem()] * len(pieces),
        out_specs=vmem(),
        compiler_params=params(),
        cost_estimate=pl.CostEstimate(
            flops=2 * 1024 * 2048 * 768 * 2, bytes_accessed=8 << 20, transcendentals=8 * 65536
        ),
    )(place, weight, *pieces)


def middle_kernel(mix_ref, weight_ref, rows_ref, gain_ref, middle_ref, send_ref, total):
    step = pl.program_id(0)
    mix = jnp.concatenate(
        [mix_ref[k, :, head * E : head * E + E] for head in range(2) for k in range(NZ)], axis=1
    )
    blocks = weight_ref.shape[0]
    weight = jnp.concatenate([weight_ref[k] for k in range(blocks)], axis=1)
    width = blocks * E
    total[:, pl.ds(pl.multiple_of(step * width, width), width)] = dot(mix, weight)

    @pl.when(step == pl.num_programs(0) - 1)
    def _():
        middle = (total[...] + rows_ref[...].astype(F32)).astype(BF)
        middle_ref[...] = middle
        values = middle.astype(F32)
        scaled = values * lax.rsqrt(jnp.mean(values * values, axis=-1, keepdims=True) + 1e-05)
        scaled = scaled * gain_ref[...]
        for group in range(4):
            chunk = jnp.concatenate(
                [scaled[32 * f + 8 * group : 32 * f + 8 * group + 8] for f in range(4)], axis=0
            ).astype(BF)
            for y in range(4):
                send_ref[(group // 2) * 8 + y * 2 + group % 2] = chunk


def middle_rows(mix, weight, rows, gain):
    steps = 4
    width = rows.shape[1]
    return pl.pallas_call(
        middle_kernel,
        grid=(steps,),
        out_shape=(
            jax.ShapeDtypeStruct((128, width), BF),
            jax.ShapeDtypeStruct((16, 32, width), BF),
        ),
        in_specs=[
            pl.BlockSpec((NZ, 128, 256), lambda i: (0, 0, 0)),
            pl.BlockSpec((16 // steps, 2048, E), lambda i: (i, 0, 0)),
            pl.BlockSpec((128, width), lambda i: (0, 0)),
            pl.BlockSpec((1, width), lambda i: (0, 0)),
        ],
        out_specs=(
            pl.BlockSpec((128, width), lambda i: (0, 0)),
            pl.BlockSpec((16, 32, width), lambda i: (0, 0, 0)),
        ),
        scratch_shapes=[pltpu.VMEM((128, width), F32)],
        compiler_params=params(),
        cost_estimate=pl.CostEstimate(
            flops=2 * 128 * 2048 * 2048, bytes_accessed=12 << 20, transcendentals=0
        ),
    )(mix, weight, rows, gain)


def temporal_kernel(start_ref, rows_ref, weight_ref, last_ref, out_ref, qkv, mix, bias):
    step = pl.program_id(0)
    kind = lax.rem(step, 3)
    rows_count = rows_ref.shape[0]

    @pl.when(step < 6)
    def _():
        weight = weight_ref[:, 0].reshape(2048, 256)
        qkv[kind] = dot(rows_ref[...], weight).astype(BF)

    @pl.when(step == 0)
    def _():
        start = start_ref[0]
        late = lax.broadcasted_iota(jnp.int32, (rows_count, rows_count), 0)
        early = lax.broadcasted_iota(jnp.int32, (rows_count, rows_count), 1)
        same = (late & 7) == (early & 7)
        allowed = same & (early <= late) & ((early >= 8 * start) == (late >= 8 * start))
        bias[...] = jnp.where(allowed, 0.0, -1e30)

    def attend(pair):
        block = 128
        for low in range(0, rows_count, block):
            for head in range(2):
                cols = slice(head * E, head * E + E)
                query = qkv[0, low : low + block, cols]
                key = qkv[1, : low + block, cols]
                value = qkv[2, : low + block, cols]
                scores = dot_t(query, key) * SCALE
                hidden = bias[low : low + block, : low + block]
                scores = jnp.where(hidden < 0.0, hidden, scores)
                at = 256 * pair + head * E
                mix[low : low + block, at : at + E] = dot(softmax(scores), value).astype(BF)

    @pl.when(step == 2)
    def _():
        attend(0)

    @pl.when(step == 5)
    def _():
        attend(1)

    @pl.when(step >= 6)
    def _():
        for block in range(4):
            weight = last_ref[block].reshape(512, 256)
            out_ref[:, 256 * block : 256 * block + 256] = dot(mix[...], weight).astype(BF)


def temporal_attend(start, rows, weight):
    count, width = rows.shape
    return pl.pallas_call(
        temporal_kernel,
        grid=(8,),
        out_shape=jax.ShapeDtypeStruct((count, width), BF),
        in_specs=[
            smem(),
            pl.BlockSpec((count, width), lambda i: (0, 0)),
            pl.BlockSpec((8, 1, 256, 256), lambda i: (0, jnp.minimum(i, 5), 0, 0)),
            pl.BlockSpec((4, 2, 256, 256), lambda i: (jnp.maximum(i - 6, 0), 3, 0, 0)),
        ],
        out_specs=pl.BlockSpec((count, width // 2), lambda i: (0, jnp.maximum(i - 6, 0))),
        scratch_shapes=[
            pltpu.VMEM((3, count, 256), BF),
            pltpu.VMEM((count, 512), BF),
            pltpu.VMEM((count, count), F32),
        ],
        compiler_params=params(),
        cost_estimate=pl.CostEstimate(
            flops=2 * 512 * 2048 * 2048, bytes_accessed=14 << 20, transcendentals=131072
        ),
    )(start, rows, weight, weight)


def shifted(value, axis, step):
    count = lax.axis_size(axis)
    return lax.ppermute(value, axis, [(i, (i + step) % count) for i in range(count)])


def gathered_rows(chunks):
    up, down = list(chunks), list(chunks)
    pieces = {0: list(chunks)}
    for step in (1, 2, 3):
        up = [shifted(value, "z", 1) for value in up]
        down = [shifted(value, "z", -1) for value in down]
        pieces[-step], pieces[step] = up, down
    pieces[4] = [shifted(up[0], "z", 1), shifted(down[1], "z", -1)]
    return [value for offset in OFFSETS for value in pieces[offset]]


def local(stream, spatial_gain, spatial_qkv, spatial_out, temporal_gain, temporal_qkv, temporal_out, starts):
    patches, frames, width = stream.shape
    w, xl, y, c, z = (lax.axis_index(name) for name in ("w", "xl", "y", "c", "z"))

    rows = jnp.transpose(stream, (1, 0, 2)).reshape(frames * patches, width)
    chunks = norm_rows(rows, spatial_gain.reshape(1, width))
    pieces = gathered_rows(chunks)

    column = (w * 2 + xl) * 4 + y
    eighth = (w * 2 + xl) * 2 + c
    out_share = lax.dynamic_slice(spatial_out, (c * E, column * E), (E, E))
    qkv_share = lax.dynamic_slice(temporal_qkv, (eighth * 256 + y * 64, 0, 0), (64, 3, 256))
    qkv_share = jnp.transpose(qkv_share.reshape(64, 6, E), (1, 0, 2)).reshape(384, E)
    last_share = lax.dynamic_slice(temporal_out, (y * 64, eighth * 256), (64, 256))
    last_share = jnp.transpose(last_share.reshape(64, 2, E), (1, 0, 2)).reshape(E, E)
    share = jnp.concatenate([out_share, qkv_share, last_share], axis=0)
    shares = lax.all_gather(share, "z", axis=0, tiled=False)

    whole_out = lax.all_gather(
        shares[:, :E].reshape(1024, E), ("w", "xl", "y", "c"), axis=0, tiled=True
    ).reshape(16, 2048, E)

    mine = shares[:, E:].reshape(4, 2, 8, 64, E)
    got = []
    for k in range(4):
        part = lax.dynamic_index_in_dim(mine, lax.rem(y + k, 4), 0, keepdims=False)
        got.append(shifted(part, "y", k) if k else part)
    ring = jnp.stack([got[0], got[3], got[2], got[1]] * 2)
    got = lax.dynamic_slice(ring, (lax.rem(4 - y, 4), 0, 0, 0, 0), (4, 2, 8, 64, E))
    got = jnp.transpose(got.reshape(4, 2, 4, 2, 64, E), (1, 2, 0, 4, 3, 5)).reshape(2, 4, 256, 256)
    quarter = jnp.concatenate([got[:, :3].reshape(6, 256, 256), got[:, 3]], axis=0)
    quarter = lax.all_gather(quarter[None], ("w", "xl", "c"), axis=0, tiled=True)

    mix = spatial_attend(z.reshape(1), spatial_qkv.reshape(width, -1), pieces)
    mix = lax.all_to_all(mix, "z", 0, 0, tiled=True)
    middle, send = middle_rows(mix, whole_out, rows, temporal_gain.reshape(1, width))

    window = lax.all_to_all(send, ("xl", "y", "c"), 0, 0, tiled=True)
    start = lax.dynamic_slice(starts, (w,), (1,))
    partial = temporal_attend(start, window.reshape(512, width), quarter)
    back = lax.all_to_all(partial.reshape(16, 32, width), ("xl", "y", "c"), 0, 0, tiled=True)
    summed = jnp.sum(back.reshape(2, 4, 2, 4, 8, width).astype(F32), axis=1)
    out = middle.reshape(4, 2, 2, 8, width).astype(F32) + jnp.transpose(summed, (2, 0, 1, 3, 4))
    out = out.astype(BF).reshape(frames, patches, width)
    return jnp.transpose(out, (1, 0, 2))


def solution(mesh):
    names = ("w", "xl", "y", "c", "z")
    fine = Mesh(mesh.devices.reshape(2, 2, 4, 2, NZ), names)
    tm = ("w", "xl", "y", "c")
    placed = (
        P("z", tm, None),
        P(),
        P(None, None, "z"),
        P("z", None),
        P(),
        P(None, None, "z"),
        P("z", None),
        P(),
    )
    return jax.shard_map(
        local, mesh=fine, in_specs=placed, out_specs=P("z", tm, None), check_vma=False
    )
```

```python
import functools
import math

import jax
import jax.numpy as jnp
from jax import lax
from jax.experimental import pallas as pl
from jax.experimental.pallas import tpu as pltpu
from jax.sharding import Mesh
from jax.sharding import PartitionSpec as P

E = 128
SEQ = 64
SCALE = 1.0 / math.sqrt(E)
BF = jnp.bfloat16
F32 = jnp.float32
NZ = 8
VMEM_LIMIT = 56 * 1024 * 1024
OFFSETS = (0, -1, 1, -2, 2, -3, 3, 4)


def params():
    return pltpu.CompilerParams(vmem_limit_bytes=VMEM_LIMIT)


def vmem():
    return pl.BlockSpec(memory_space=pltpu.VMEM)


def smem():
    return pl.BlockSpec(memory_space=pltpu.SMEM)


def normed(values, gain):
    scaled = values * lax.rsqrt(jnp.mean(values * values, axis=-1, keepdims=True) + 1e-05)
    return (scaled * gain).astype(BF)


def softmax(scores):
    shifted = jnp.exp(scores - jnp.max(scores, axis=-1, keepdims=True))
    return (shifted / jnp.sum(shifted, axis=-1, keepdims=True)).astype(BF)


def dot(a, b):
    return jnp.dot(a, b, preferred_element_type=F32)


def dot_t(a, b):
    return lax.dot_general(a, b, (((1,), (1,)), ((), ())), preferred_element_type=F32)


def norm_kernel(x_ref, gain_ref, a_ref, b_ref, rows_ref):
    gain = gain_ref[...]
    values = jnp.transpose(x_ref[...].astype(F32), (1, 0, 2)).reshape(rows_ref.shape)
    half = a_ref.shape[0]
    rows_ref[...] = values.astype(BF)
    a_ref[...] = normed(values[:half], gain)
    b_ref[...] = normed(values[half:], gain)


def norm_rows(stream, gain):
    patches, frames, width = stream.shape
    count = patches * frames
    half = jax.ShapeDtypeStruct((count // 2, width), BF)
    return pl.pallas_call(
        norm_kernel,
        out_shape=(half, half, jax.ShapeDtypeStruct((count, width), BF)),
        in_specs=[vmem(), vmem()],
        out_specs=(vmem(), vmem(), vmem()),
        compiler_params=params(),
        cost_estimate=pl.CostEstimate(
            flops=4 * count * width, bytes_accessed=6 * count * width, transcendentals=0
        ),
    )(stream, gain)


def cut_kernel(place_ref, out_ref, qkv_ref, last_ref, share_ref):
    share_ref[0] = out_ref[...]
    for kind in range(3):
        share_ref[1 + kind] = qkv_ref[kind]
    share_ref[4] = last_ref[...]


def cut_share(place, spatial_out, temporal_qkv, temporal_out):
    return pl.pallas_call(
        cut_kernel,
        grid_spec=pltpu.PrefetchScalarGridSpec(
            num_scalar_prefetch=1,
            grid=(1,),
            in_specs=[
                pl.BlockSpec((64, 256), lambda i, at: (at[0], at[1])),
                pl.BlockSpec((3, 64, 256), lambda i, at: (0, at[2], 0)),
                pl.BlockSpec((64, 256), lambda i, at: (at[3], at[4])),
            ],
            out_specs=pl.BlockSpec((5, 64, 256), lambda i, at: (0, 0, 0)),
        ),
        out_shape=jax.ShapeDtypeStruct((5, 64, 256), BF),
        compiler_params=params(),
        cost_estimate=pl.CostEstimate(flops=0, bytes_accessed=320 << 10, transcendentals=0),
    )(place, spatial_out, temporal_qkv, temporal_out)


def split_kernel(y_ref, shares_ref, out_ref, *sends):
    for k in range(NZ):
        out_ref[k] = shares_ref[k, 0]
    for step in range(4):
        pair = lax.rem(y_ref[0] + step, 4)
        for k in range(2):
            sends[step][k] = shares_ref[2 * pair + k, 1:]


def split_shares(y, shares):
    send = jax.ShapeDtypeStruct((2, 4, 64, 256), BF)
    return pl.pallas_call(
        split_kernel,
        out_shape=(jax.ShapeDtypeStruct((NZ, 64, 256), BF),) + (send,) * 4,
        in_specs=[smem(), vmem()],
        out_specs=(vmem(),) * 5,
        compiler_params=params(),
        cost_estimate=pl.CostEstimate(flops=0, bytes_accessed=3 << 20, transcendentals=0),
    )(y, shares)


def join_kernel(y_ref, *refs):
    out_ref = refs[-1]
    for step in range(4):
        low = pl.multiple_of(64 * lax.rem(y_ref[0] + (4 - step), 4), 64)
        for pair in range(2):
            for kind in range(4):
                block = 3 * pair + kind if kind < 3 else 6 + pair
                out_ref[block, pl.ds(low, 64), :] = refs[step][pair, kind]


def join_shares(y, got):
    return pl.pallas_call(
        join_kernel,
        out_shape=jax.ShapeDtypeStruct((8, 256, 256), BF),
        in_specs=[smem()] + [vmem()] * 4,
        out_specs=vmem(),
        compiler_params=params(),
        cost_estimate=pl.CostEstimate(flops=0, bytes_accessed=2 << 20, transcendentals=0),
    )(y, *got)


def spatial_kernel(place_ref, weight_ref, *refs):
    out_ref = refs[-1]
    pieces = refs[:-1]
    place = place_ref[0]
    for frame in range(4):
        part, inner = frame // 2, frame % 2
        rows = jnp.concatenate(
            [pieces[2 * k + part][32 * inner : 32 * inner + 32, :] for k in range(NZ)], axis=0
        )
        qkv = [dot(rows, weight_ref[kind]).astype(BF) for kind in range(3)]
        for head in range(2):
            low = head * E
            query = qkv[0][:, low : low + E]
            key = qkv[1][:, low : low + E]
            value = qkv[2][:, low : low + E]
            weights = softmax(dot_t(query, key) * SCALE)
            mixed = dot(weights, value).astype(BF)
            for k in range(NZ):
                target = lax.rem(place + (OFFSETS[k] + NZ), NZ)
                out_ref[target, 32 * frame : 32 * frame + 32, low : low + E] = mixed[
                    32 * k : 32 * k + 32
                ]


def spatial_attend(place, weight, pieces):
    return pl.pallas_call(
        spatial_kernel,
        out_shape=jax.ShapeDtypeStruct((NZ, 128, 256), BF),
        in_specs=[smem(), vmem()] + [vmem()] * len(pieces),
        out_specs=vmem(),
        compiler_params=params(),
        cost_estimate=pl.CostEstimate(
            flops=2 * 1024 * 2048 * 768 * 2, bytes_accessed=8 << 20, transcendentals=8 * 65536
        ),
    )(place, weight, *pieces)


def middle_kernel(mix_ref, weight_ref, rows_ref, gain_ref, middle_ref, send_ref, total):
    step = pl.program_id(0)
    mix = jnp.concatenate([mix_ref[k] for k in range(NZ)], axis=1)
    for block in range(weight_ref.shape[0]):
        weight = jnp.concatenate(
            [weight_ref[block, quarter, k] for k in range(NZ) for quarter in range(4)], axis=0
        )
        low = pl.multiple_of((step * weight_ref.shape[0] + block) * 256, 256)
        total[:, pl.ds(low, 256)] = dot(mix, weight)

    @pl.when(step == pl.num_programs(0) - 1)
    def _():
        middle = (total[...] + rows_ref[...].astype(F32)).astype(BF)
        middle_ref[...] = middle
        values = middle.astype(F32)
        scaled = values * lax.rsqrt(jnp.mean(values * values, axis=-1, keepdims=True) + 1e-05)
        scaled = scaled * gain_ref[...]
        for group in range(4):
            chunk = jnp.concatenate(
                [scaled[32 * f + 8 * group : 32 * f + 8 * group + 8] for f in range(4)], axis=0
            ).astype(BF)
            for y in range(4):
                send_ref[(group // 2) * 8 + y * 2 + group % 2] = chunk


def middle_rows(mix, weight, rows, gain):
    steps = 4
    width = rows.shape[1]
    return pl.pallas_call(
        middle_kernel,
        grid=(steps,),
        out_shape=(
            jax.ShapeDtypeStruct((128, width), BF),
            jax.ShapeDtypeStruct((16, 32, width), BF),
        ),
        in_specs=[
            pl.BlockSpec((NZ, 128, 256), lambda i: (0, 0, 0)),
            pl.BlockSpec((8 // steps, 4, NZ, 64, 256), lambda i: (i, 0, 0, 0, 0)),
            pl.BlockSpec((128, width), lambda i: (0, 0)),
            pl.BlockSpec((1, width), lambda i: (0, 0)),
        ],
        out_specs=(
            pl.BlockSpec((128, width), lambda i: (0, 0)),
            pl.BlockSpec((16, 32, width), lambda i: (0, 0, 0)),
        ),
        scratch_shapes=[pltpu.VMEM((128, width), F32)],
        compiler_params=params(),
        cost_estimate=pl.CostEstimate(
            flops=2 * 128 * 2048 * 2048, bytes_accessed=12 << 20, transcendentals=0
        ),
    )(mix, weight, rows, gain)


def temporal_kernel(start_ref, rows_ref, weight_ref, last_ref, out_ref, qkv, mix, bias):
    step = pl.program_id(0)
    kind = lax.rem(step, 3)
    rows_count = rows_ref.shape[0]

    @pl.when(step < 6)
    def _():
        weight = weight_ref[:, 0].reshape(2048, 256)
        qkv[kind] = dot(rows_ref[...], weight).astype(BF)

    @pl.when(step == 0)
    def _():
        start = start_ref[0]
        late = lax.broadcasted_iota(jnp.int32, (rows_count, rows_count), 0)
        early = lax.broadcasted_iota(jnp.int32, (rows_count, rows_count), 1)
        same = (late & 7) == (early & 7)
        allowed = same & (early <= late) & ((early >= 8 * start) == (late >= 8 * start))
        bias[...] = jnp.where(allowed, 0.0, -1e30)

    def attend(pair):
        block = 128
        for low in range(0, rows_count, block):
            for head in range(2):
                cols = slice(head * E, head * E + E)
                query = qkv[0, low : low + block, cols]
                key = qkv[1, : low + block, cols]
                value = qkv[2, : low + block, cols]
                scores = dot_t(query, key) * SCALE
                hidden = bias[low : low + block, : low + block]
                scores = jnp.where(hidden < 0.0, hidden, scores)
                at = 256 * pair + head * E
                mix[low : low + block, at : at + E] = dot(softmax(scores), value).astype(BF)

    @pl.when(step == 2)
    def _():
        attend(0)

    @pl.when(step == 5)
    def _():
        attend(1)

    @pl.when(step >= 6)
    def _():
        for block in range(4):
            weight = last_ref[block].reshape(512, 256)
            out_ref[:, 256 * block : 256 * block + 256] = dot(mix[...], weight).astype(BF)


def temporal_attend(start, rows, weight):
    count, width = rows.shape
    return pl.pallas_call(
        temporal_kernel,
        grid=(8,),
        out_shape=jax.ShapeDtypeStruct((count, width), BF),
        in_specs=[
            smem(),
            pl.BlockSpec((count, width), lambda i: (0, 0)),
            pl.BlockSpec((8, 1, 256, 256), lambda i: (0, jnp.minimum(i, 5), 0, 0)),
            pl.BlockSpec((4, 2, 256, 256), lambda i: (jnp.maximum(i - 6, 0), 3, 0, 0)),
        ],
        out_specs=pl.BlockSpec((count, width // 2), lambda i: (0, jnp.maximum(i - 6, 0))),
        scratch_shapes=[
            pltpu.VMEM((3, count, 256), BF),
            pltpu.VMEM((count, 512), BF),
            pltpu.VMEM((count, count), F32),
        ],
        compiler_params=params(),
        cost_estimate=pl.CostEstimate(
            flops=2 * 512 * 2048 * 2048, bytes_accessed=14 << 20, transcendentals=131072
        ),
    )(start, rows, weight, weight)


def shifted(value, axis, step):
    count = lax.axis_size(axis)
    return lax.ppermute(value, axis, [(i, (i + step) % count) for i in range(count)])


def gathered_rows(chunks):
    up, down = list(chunks), list(chunks)
    pieces = {0: list(chunks)}
    for step in (1, 2, 3):
        up = [shifted(value, "z", 1) for value in up]
        down = [shifted(value, "z", -1) for value in down]
        pieces[-step], pieces[step] = up, down
    pieces[4] = [shifted(up[0], "z", 1), shifted(down[1], "z", -1)]
    return [value for offset in OFFSETS for value in pieces[offset]]


def local(stream, spatial_gain, spatial_qkv, spatial_out, temporal_gain, temporal_qkv, temporal_out, starts):
    patches, frames, width = stream.shape
    w, xl, y, c, z = (lax.axis_index(name) for name in ("w", "xl", "y", "c", "z"))

    place = jnp.stack(
        [
            lax.rem(y, 2) * 2 + c,
            (w * 2 + xl) * 2 + y // 2,
            ((w * 2 + xl) * 2 + c) * 4 + y,
            y,
            (w * 2 + xl) * 2 + c,
        ]
    ).astype(jnp.int32)
    share = cut_share(place, spatial_out, jnp.transpose(temporal_qkv, (1, 0, 2)), temporal_out)
    shares = lax.all_gather(share, "z", axis=0, tiled=False)

    first, second, rows = norm_rows(stream, spatial_gain.reshape(1, width))
    pieces = gathered_rows((first, second))
    *pieces, shares = lax.optimization_barrier((*pieces, shares))

    out_share, *sends = split_shares(y.reshape(1), shares)
    whole_out = lax.all_gather(out_share, ("w", "xl", "y", "c"), axis=0, tiled=False)
    whole_out = whole_out.reshape(8, 4, NZ, 64, 256)

    got = [sends[0]] + [shifted(sends[k], "y", k) for k in range(1, 4)]

    weight = jnp.transpose(spatial_qkv, (1, 0, 2))
    mix = spatial_attend(z.reshape(1), weight, pieces)
    mix, *got = lax.optimization_barrier((mix, *got))
    mix = lax.all_to_all(mix, "z", 0, 0, tiled=True)
    quarter = join_shares(y.reshape(1), got)
    quarter = lax.all_gather(quarter[None], ("w", "xl", "c"), axis=0, tiled=True)

    middle, send = middle_rows(mix, whole_out, rows, temporal_gain.reshape(1, width))

    window = lax.all_to_all(send, ("xl", "y", "c"), 0, 0, tiled=True)
    start = lax.dynamic_slice(starts, (w,), (1,))
    partial = temporal_attend(start, window.reshape(512, width), quarter)
    back = lax.all_to_all(partial.reshape(16, 32, width), ("xl", "y", "c"), 0, 0, tiled=True)
    summed = jnp.sum(back.reshape(2, 4, 2, 4, 8, width).astype(F32), axis=1)
    out = middle.reshape(4, 2, 2, 8, width).astype(F32) + jnp.transpose(summed, (2, 0, 1, 3, 4))
    out = out.astype(BF).reshape(frames, patches, width)
    return jnp.transpose(out, (1, 0, 2))


def solution(mesh):
    names = ("w", "xl", "y", "c", "z")
    fine = Mesh(mesh.devices.reshape(2, 2, 4, 2, NZ), names)
    tm = ("w", "xl", "y", "c")
    placed = (
        P("z", tm, None),
        P(),
        P(None, None, "z"),
        P("z", None),
        P(),
        P(None, None, "z"),
        P("z", None),
        P(),
    )
    return jax.shard_map(
        local, mesh=fine, in_specs=placed, out_specs=P("z", tm, None), check_vma=False
    )
```

```python
import functools
import math

import jax
import jax.numpy as jnp
from jax import lax
from jax.experimental import pallas as pl
from jax.experimental.pallas import tpu as pltpu
from jax.sharding import Mesh
from jax.sharding import PartitionSpec as P

E = 128
SEQ = 64
SCALE = 1.0 / math.sqrt(E)
BF = jnp.bfloat16
F32 = jnp.float32
NZ = 8
VMEM_LIMIT = 56 * 1024 * 1024
OFFSETS = (0, -1, 1, -2, 2, -3, 3, 4)


def params():
    return pltpu.CompilerParams(vmem_limit_bytes=VMEM_LIMIT)


def vmem():
    return pl.BlockSpec(memory_space=pltpu.VMEM)


def smem():
    return pl.BlockSpec(memory_space=pltpu.SMEM)


def normed(values, gain):
    scaled = values * lax.rsqrt(jnp.mean(values * values, axis=-1, keepdims=True) + 1e-05)
    return (scaled * gain).astype(BF)


def softmax(scores):
    shifted = jnp.exp(scores - jnp.max(scores, axis=-1, keepdims=True))
    return (shifted / jnp.sum(shifted, axis=-1, keepdims=True)).astype(BF)


def dot(a, b):
    return jnp.dot(a, b, preferred_element_type=F32)


def dot_t(a, b):
    return lax.dot_general(a, b, (((1,), (1,)), ((), ())), preferred_element_type=F32)


def norm_kernel(place_ref, x_ref, gain_ref, qkv_ref, last_ref, a_ref, b_ref, rows_ref):
    gain = gain_ref[...]
    values = jnp.transpose(x_ref[...].astype(F32), (1, 0, 2)).reshape(rows_ref.shape)
    half = rows_ref.shape[0] // 2
    rows_ref[...] = values.astype(BF)
    a_ref[:half] = normed(values[:half], gain)
    b_ref[:half] = normed(values[half:], gain)
    shares = (qkv_ref[0], qkv_ref[1], qkv_ref[2], last_ref[...])
    for chunk, ref in enumerate((a_ref, b_ref)):
        for group in range(8):
            share = shares[2 * chunk + group // 4]
            low = 16 * (group % 4)
            ref[half:, 256 * group : 256 * group + 256] = share[low : low + 16]


def norm_rows(place, stream, gain, temporal_qkv, temporal_out):
    patches, frames, width = stream.shape
    count = patches * frames
    half = jax.ShapeDtypeStruct((count // 2 + 16, width), BF)
    whole = lambda *shape: pl.BlockSpec(shape, lambda i, at: (0,) * len(shape))
    return pl.pallas_call(
        norm_kernel,
        grid_spec=pltpu.PrefetchScalarGridSpec(
            num_scalar_prefetch=1,
            grid=(1,),
            in_specs=[
                whole(patches, frames, width),
                whole(1, width),
                pl.BlockSpec((3, 64, 256), lambda i, at: (0, at[2], 0)),
                pl.BlockSpec((64, 256), lambda i, at: (at[0], at[1])),
            ],
            out_specs=(
                whole(count // 2 + 16, width),
                whole(count // 2 + 16, width),
                whole(count, width),
            ),
        ),
        out_shape=(half, half, jax.ShapeDtypeStruct((count, width), BF)),
        compiler_params=params(),
        cost_estimate=pl.CostEstimate(
            flops=4 * count * width, bytes_accessed=6 * count * width, transcendentals=0
        ),
    )(place, stream, gain, temporal_qkv, temporal_out)


def split_kernel(place_ref, *refs):
    pieces = refs[: 2 * NZ]
    out_ref, sends = refs[2 * NZ], refs[2 * NZ + 1 :]
    z, y = place_ref[0], place_ref[1]
    for k in range(NZ):
        source = lax.rem(z + (OFFSETS[k] + NZ), NZ)
        step = lax.rem(source // 2 + 4 - y, 4)
        pair = lax.rem(source, 2)
        for block in range(4):
            ref = pieces[2 * k + block // 2]
            for group in range(4):
                low = 256 * (4 * (block % 2) + group)
                value = ref[:, low : low + 256]
                rows = slice(16 * group, 16 * group + 16)
                if block == 3:
                    out_ref[source, rows] = value
                else:
                    sends[0][step, pair, block, rows] = value


def split_shares(place, pieces):
    return pl.pallas_call(
        split_kernel,
        grid=(1,),
        out_shape=(
            jax.ShapeDtypeStruct((NZ, 64, 256), BF),
            jax.ShapeDtypeStruct((4, 2, 3, 64, 256), BF),
        ),
        in_specs=[smem()] + [pl.BlockSpec((16, 2048), lambda i: (4, 0))] * len(pieces),
        out_specs=(
            pl.BlockSpec((NZ, 64, 256), lambda i: (0, 0, 0)),
            pl.BlockSpec((4, 2, 3, 64, 256), lambda i: (0, 0, 0, 0, 0)),
        ),
        compiler_params=params(),
        cost_estimate=pl.CostEstimate(flops=0, bytes_accessed=2 << 20, transcendentals=0),
    )(place, *pieces)


def join_kernel(y_ref, *refs):
    out_ref = refs[-1]
    for step in range(4):
        low = pl.multiple_of(64 * lax.rem(y_ref[0] + (4 - step), 4), 64)
        for pair in range(2):
            for kind in range(3):
                out_ref[3 * pair + kind, pl.ds(low, 64), :] = refs[step][pair, kind]


def join_shares(y, got):
    return pl.pallas_call(
        join_kernel,
        out_shape=jax.ShapeDtypeStruct((6, 256, 256), BF),
        in_specs=[smem()] + [vmem()] * 4,
        out_specs=vmem(),
        compiler_params=params(),
        cost_estimate=pl.CostEstimate(flops=0, bytes_accessed=2 << 20, transcendentals=0),
    )(y, *got)


def spatial_kernel(place_ref, weight_ref, *refs):
    out_ref = refs[-1]
    pieces = refs[:-1]
    place = place_ref[0]
    for frame in range(4):
        part, inner = frame // 2, frame % 2
        rows = jnp.concatenate(
            [pieces[2 * k + part][32 * inner : 32 * inner + 32, :] for k in range(NZ)], axis=0
        )
        qkv = [dot(rows, weight_ref[kind]).astype(BF) for kind in range(3)]
        for head in range(2):
            low = head * E
            query = qkv[0][:, low : low + E]
            key = qkv[1][:, low : low + E]
            value = qkv[2][:, low : low + E]
            weights = softmax(dot_t(query, key) * SCALE)
            mixed = dot(weights, value).astype(BF)
            for k in range(NZ):
                target = lax.rem(place + (OFFSETS[k] + NZ), NZ)
                out_ref[target, 32 * frame : 32 * frame + 32, low : low + E] = mixed[
                    32 * k : 32 * k + 32
                ]


def spatial_attend(place, weight, pieces):
    return pl.pallas_call(
        spatial_kernel,
        out_shape=jax.ShapeDtypeStruct((NZ, 128, 256), BF),
        in_specs=[smem(), vmem()] + [vmem()] * len(pieces),
        out_specs=vmem(),
        compiler_params=params(),
        cost_estimate=pl.CostEstimate(
            flops=2 * 1024 * 2048 * 768 * 2, bytes_accessed=8 << 20, transcendentals=8 * 65536
        ),
    )(place, weight, *pieces)


def column_block(weight_ref, block):
    return jnp.concatenate(
        [weight_ref[block, quarter, k] for k in range(NZ) for quarter in range(4)], axis=0
    )


def join_blocks_kernel(z_ref, *refs):
    out_ref = refs[-1]
    for step in range(4):
        out_ref[lax.rem(z_ref[0] + (4 - step), 4)] = refs[step][...]


def join_blocks(z, parts):
    return pl.pallas_call(
        join_blocks_kernel,
        out_shape=jax.ShapeDtypeStruct((4, 128, 256), BF),
        in_specs=[smem()] + [vmem()] * 4,
        out_specs=vmem(),
        compiler_params=params(),
        cost_estimate=pl.CostEstimate(flops=0, bytes_accessed=512 << 10, transcendentals=0),
    )(z, *parts)


def middle_kernel(mix_ref, weight_ref, rows_ref, gain_ref, middle_ref, send_ref, total):
    step = pl.program_id(0)
    mix = jnp.concatenate([mix_ref[k] for k in range(NZ)], axis=1)
    for block in range(weight_ref.shape[0]):
        weight = jnp.concatenate(
            [weight_ref[block, head, k // 4, k % 4] for k in range(NZ) for head in range(2)], axis=0
        )
        low = pl.multiple_of((step * weight_ref.shape[0] + block) * 256, 256)
        total[:, pl.ds(low, 256)] = dot(mix, weight)

    @pl.when(step == pl.num_programs(0) - 1)
    def _():
        middle = (total[...] + rows_ref[...].astype(F32)).astype(BF)
        middle_ref[...] = middle
        values = middle.astype(F32)
        scaled = values * lax.rsqrt(jnp.mean(values * values, axis=-1, keepdims=True) + 1e-05)
        scaled = scaled * gain_ref[...]
        for group in range(4):
            chunk = jnp.concatenate(
                [scaled[32 * f + 8 * group : 32 * f + 8 * group + 8] for f in range(4)], axis=0
            ).astype(BF)
            for y in range(4):
                send_ref[(group // 2) * 8 + y * 2 + group % 2] = chunk


def middle_rows(mix, weight, rows, gain):
    steps = 4
    width = rows.shape[1]
    return pl.pallas_call(
        middle_kernel,
        grid=(steps,),
        out_shape=(
            jax.ShapeDtypeStruct((128, width), BF),
            jax.ShapeDtypeStruct((16, 32, width), BF),
        ),
        in_specs=[
            pl.BlockSpec((NZ, 128, 256), lambda i: (0, 0, 0)),
            pl.BlockSpec((8 // steps, 2, 2, 4, 128, 256), lambda i: (i, 0, 0, 0, 0, 0)),
            pl.BlockSpec((128, width), lambda i: (0, 0)),
            pl.BlockSpec((1, width), lambda i: (0, 0)),
        ],
        out_specs=(
            pl.BlockSpec((128, width), lambda i: (0, 0)),
            pl.BlockSpec((16, 32, width), lambda i: (0, 0, 0)),
        ),
        scratch_shapes=[pltpu.VMEM((128, width), F32)],
        compiler_params=params(),
        cost_estimate=pl.CostEstimate(
            flops=2 * 128 * 2048 * 2048, bytes_accessed=12 << 20, transcendentals=0
        ),
    )(mix, weight, rows, gain)


def temporal_kernel(start_ref, rows_ref, weight_ref, out_ref, qkv, bias):
    step = pl.program_id(0)
    kind = lax.rem(step, 3)
    rows_count = rows_ref.shape[0]
    weight = weight_ref[:, 0].reshape(2048, 256)
    qkv[kind] = dot(rows_ref[...], weight).astype(BF)

    @pl.when(step == 0)
    def _():
        start = start_ref[0]
        late = lax.broadcasted_iota(jnp.int32, (rows_count, rows_count), 0)
        early = lax.broadcasted_iota(jnp.int32, (rows_count, rows_count), 1)
        same = (late & 7) == (early & 7)
        allowed = same & (early <= late) & ((early >= 8 * start) == (late >= 8 * start))
        bias[...] = jnp.where(allowed, 0.0, -1e30)

    def attend(pair):
        block = 128
        for low in range(0, rows_count, block):
            for head in range(2):
                cols = slice(head * E, head * E + E)
                query = qkv[0, low : low + block, cols]
                key = qkv[1, : low + block, cols]
                value = qkv[2, : low + block, cols]
                scores = dot_t(query, key) * SCALE
                hidden = bias[low : low + block, : low + block]
                scores = jnp.where(hidden < 0.0, hidden, scores)
                at = 256 * pair + head * E
                mixed = dot(softmax(scores), value).astype(BF)
                out_ref[low // 32 : low // 32 + 4, :, at : at + E] = mixed.reshape(4, 32, E)

    @pl.when(step == 2)
    def _():
        attend(0)

    @pl.when(step == 5)
    def _():
        attend(1)


def temporal_attend(start, rows, weight):
    count, width = rows.shape
    return pl.pallas_call(
        temporal_kernel,
        grid=(6,),
        out_shape=jax.ShapeDtypeStruct((16, 32, 512), BF),
        in_specs=[
            smem(),
            pl.BlockSpec((count, width), lambda i: (0, 0)),
            pl.BlockSpec((8, 1, 256, 256), lambda i: (0, i, 0, 0)),
        ],
        out_specs=pl.BlockSpec((16, 32, 512), lambda i: (0, 0, 0)),
        scratch_shapes=[
            pltpu.VMEM((3, count, 256), BF),
            pltpu.VMEM((count, count), F32),
        ],
        compiler_params=params(),
        cost_estimate=pl.CostEstimate(
            flops=2 * 512 * 2048 * 1536, bytes_accessed=9 << 20, transcendentals=131072
        ),
    )(start, rows, weight)


def last_kernel(mix_ref, weight_ref, middle_ref, out_ref, total):
    step = pl.program_id(0)
    mix = jnp.concatenate(
        [
            jnp.concatenate([mix_ref[xl * 8 + y * 2 + c] for xl in range(2) for c in range(2)], axis=0)
            for y in range(4)
        ],
        axis=1,
    )
    for block in range(weight_ref.shape[0]):
        low = pl.multiple_of((step * weight_ref.shape[0] + block) * 256, 256)
        total[:, pl.ds(low, 256)] = dot(mix, column_block(weight_ref, block))

    @pl.when(step == pl.num_programs(0) - 1)
    def _():
        for group in range(4):
            rows = total[32 * group : 32 * group + 32].reshape(4, 8, -1)
            middle = jnp.stack(
                [
                    middle_ref[32 * f : 32 * f + 32].astype(F32)[8 * group : 8 * group + 8]
                    for f in range(4)
                ],
                axis=0,
            )
            out = jnp.transpose(rows + middle, (1, 0, 2)).astype(BF)
            out_ref[8 * group : 8 * group + 8] = out


def last_rows(mix, weight, middle):
    steps = 4
    width = middle.shape[1]
    return pl.pallas_call(
        last_kernel,
        grid=(steps,),
        out_shape=jax.ShapeDtypeStruct((32, 4, width), BF),
        in_specs=[
            pl.BlockSpec((16, 32, 512), lambda i: (0, 0, 0)),
            pl.BlockSpec((8 // steps, 4, NZ, 64, 256), lambda i: (i, 0, 0, 0, 0)),
            pl.BlockSpec((128, width), lambda i: (0, 0)),
        ],
        out_specs=pl.BlockSpec((32, 4, width), lambda i: (0, 0, 0)),
        scratch_shapes=[pltpu.VMEM((128, width), F32)],
        compiler_params=params(),
        cost_estimate=pl.CostEstimate(
            flops=2 * 128 * 2048 * 2048, bytes_accessed=12 << 20, transcendentals=0
        ),
    )(mix, weight, middle)


def shifted(value, axis, step):
    count = lax.axis_size(axis)
    return lax.ppermute(value, axis, [(i, (i + step) % count) for i in range(count)])


def gathered_rows(chunks):
    up, down = list(chunks), list(chunks)
    pieces = {0: list(chunks)}
    for step in (1, 2, 3):
        up = [shifted(value, "z", 1) for value in up]
        down = [shifted(value, "z", -1) for value in down]
        pieces[-step], pieces[step] = up, down
    pieces[4] = [shifted(up[0], "z", 1), shifted(down[1], "z", -1)]
    return [value for offset in OFFSETS for value in pieces[offset]]


def local(stream, spatial_gain, spatial_qkv, spatial_out, temporal_gain, temporal_qkv, temporal_out, starts):
    patches, frames, width = stream.shape
    w, xl, y, c, z = (lax.axis_index(name) for name in ("w", "xl", "y", "c", "z"))

    place = jnp.stack(
        [
            lax.rem(y, 2) * 2 + c,
            (w * 2 + xl) * 2 + y // 2,
            ((w * 2 + xl) * 2 + c) * 4 + y,
        ]
    ).astype(jnp.int32)

    block = lax.dynamic_slice(
        spatial_out, (lax.rem(y, 2) * 128, place[1] * 256), (128, 256)
    )
    parts = []
    for k in range(4):
        pairs = [
            (a * 8 + b, (b // 4) * 8 + (b + 4 * a + k) % 8) for a in range(2) for b in range(8)
        ]
        parts.append(lax.ppermute(block, ("c", "z"), pairs))
    gathered = join_blocks(z.reshape(1), parts)
    whole_out = lax.all_gather(gathered, ("w", "xl", "y", "c"), axis=0, tiled=False)
    whole_out = whole_out.reshape(8, 2, 2, 4, 128, 256)

    stream, parts = lax.optimization_barrier((stream, parts))
    first, second, rows = norm_rows(
        place, stream, spatial_gain.reshape(1, width), jnp.transpose(temporal_qkv, (1, 0, 2)), temporal_out
    )
    pieces = gathered_rows((first, second))

    last_share, sends = split_shares(jnp.stack([z, y]).astype(jnp.int32), pieces)
    got = [sends[0]] + [shifted(sends[k], "y", k) for k in range(1, 4)]

    weight = jnp.transpose(spatial_qkv, (1, 0, 2))
    mix = spatial_attend(z.reshape(1), weight, pieces)
    mix, *got = lax.optimization_barrier((mix, *got))
    quarter = join_shares(y.reshape(1), got)
    mix, quarter = lax.optimization_barrier((mix, quarter))
    quarter = lax.all_gather(quarter[None], ("w", "xl", "c"), axis=0, tiled=True)
    mix = lax.all_to_all(mix, "z", 0, 0, tiled=True)

    middle, send = middle_rows(mix, whole_out, rows, temporal_gain.reshape(1, width))
    last_share, middle = lax.optimization_barrier((last_share, middle))
    whole_last = lax.all_gather(last_share, ("w", "xl", "y", "c"), axis=0, tiled=False)
    whole_last = whole_last.reshape(8, 4, NZ, 64, 256)

    window = lax.all_to_all(send, ("xl", "y", "c"), 0, 0, tiled=True)
    start = lax.dynamic_slice(starts, (w,), (1,))
    mix = temporal_attend(start, window.reshape(512, width), quarter)
    mix = lax.all_to_all(mix, ("xl", "y", "c"), 0, 0, tiled=True)
    return last_rows(mix, whole_last, middle)


def solution(mesh):
    names = ("w", "xl", "y", "c", "z")
    fine = Mesh(mesh.devices.reshape(2, 2, 4, 2, NZ), names)
    tm = ("w", "xl", "y", "c")
    placed = (
        P("z", tm, None),
        P(),
        P(None, None, "z"),
        P("z", None),
        P(),
        P(None, None, "z"),
        P("z", None),
        P(),
    )
    return jax.shard_map(
        local, mesh=fine, in_specs=placed, out_specs=P("z", tm, None), check_vma=False
    )
```

```python
import functools
import math

import jax
import jax.numpy as jnp
from jax import lax
from jax.experimental import pallas as pl
from jax.experimental.pallas import tpu as pltpu
from jax.sharding import Mesh
from jax.sharding import PartitionSpec as P

E = 128
SEQ = 64
SCALE = 1.0 / math.sqrt(E)
BF = jnp.bfloat16
F32 = jnp.float32
NZ = 8
VMEM_LIMIT = 56 * 1024 * 1024
OFFSETS = (0, -1, 1, -2, 2, -3, 3, 4)


def params():
    return pltpu.CompilerParams(vmem_limit_bytes=VMEM_LIMIT)


def vmem():
    return pl.BlockSpec(memory_space=pltpu.VMEM)


def smem():
    return pl.BlockSpec(memory_space=pltpu.SMEM)


def normed(values, gain):
    scaled = values * lax.rsqrt(jnp.mean(values * values, axis=-1, keepdims=True) + 1e-05)
    return (scaled * gain).astype(BF)


def softmax(scores):
    shifted = jnp.exp(scores - jnp.max(scores, axis=-1, keepdims=True))
    return (shifted / jnp.sum(shifted, axis=-1, keepdims=True)).astype(BF)


def dot(a, b):
    return jnp.dot(a, b, preferred_element_type=F32)


def dot_t(a, b):
    return lax.dot_general(a, b, (((1,), (1,)), ((), ())), preferred_element_type=F32)


def norm_kernel(place_ref, x_ref, gain_ref, qkv_ref, a_ref, b_ref, rows_ref):
    gain = gain_ref[...]
    values = jnp.transpose(x_ref[...].astype(F32), (1, 0, 2)).reshape(rows_ref.shape)
    half = rows_ref.shape[0] // 2
    rows_ref[...] = values.astype(BF)
    a_ref[:half] = normed(values[:half], gain)
    b_ref[:half] = normed(values[half:], gain)
    b_ref[half:, 1024:] = jnp.zeros((16, 1024), BF)
    for kind in range(3):
        share = qkv_ref[kind]
        ref = (a_ref, b_ref)[kind // 2]
        for group in range(4):
            low = 256 * (4 * (kind % 2) + group)
            ref[half:, low : low + 256] = share[16 * group : 16 * group + 16]


def norm_rows(place, stream, gain, temporal_qkv):
    patches, frames, width = stream.shape
    count = patches * frames
    half = jax.ShapeDtypeStruct((count // 2 + 16, width), BF)
    whole = lambda *shape: pl.BlockSpec(shape, lambda i, at: (0,) * len(shape))
    return pl.pallas_call(
        norm_kernel,
        grid_spec=pltpu.PrefetchScalarGridSpec(
            num_scalar_prefetch=1,
            grid=(1,),
            in_specs=[
                whole(patches, frames, width),
                whole(1, width),
                pl.BlockSpec((3, 64, 256), lambda i, at: (0, at[0], 0)),
            ],
            out_specs=(
                whole(count // 2 + 16, width),
                whole(count // 2 + 16, width),
                whole(count, width),
            ),
        ),
        out_shape=(half, half, jax.ShapeDtypeStruct((count, width), BF)),
        compiler_params=params(),
        cost_estimate=pl.CostEstimate(
            flops=4 * count * width, bytes_accessed=6 * count * width, transcendentals=0
        ),
    )(place, stream, gain, temporal_qkv)


def split_kernel(place_ref, *refs):
    pieces, send_ref = refs[:-1], refs[-1]
    z, y = place_ref[0], place_ref[1]
    for k in range(NZ):
        source = lax.rem(z + (OFFSETS[k] + NZ), NZ)
        step = lax.rem(source // 2 + 4 - y, 4)
        pair = lax.rem(source, 2)
        for kind in range(3):
            for group in range(4):
                low = 256 * (4 * (kind % 2) + group)
                rows = slice(16 * group, 16 * group + 16)
                send_ref[step, pair, kind, rows] = pieces[2 * k + kind // 2][:, low : low + 256]


def split_shares(place, pieces):
    return pl.pallas_call(
        split_kernel,
        grid=(1,),
        out_shape=jax.ShapeDtypeStruct((4, 2, 3, 64, 256), BF),
        in_specs=[smem()] + [pl.BlockSpec((16, 2048), lambda i: (4, 0))] * len(pieces),
        out_specs=pl.BlockSpec((4, 2, 3, 64, 256), lambda i: (0, 0, 0, 0, 0)),
        compiler_params=params(),
        cost_estimate=pl.CostEstimate(flops=0, bytes_accessed=2 << 20, transcendentals=0),
    )(place, *pieces)


def join_kernel(y_ref, *refs):
    out_ref = refs[-1]
    for step in range(4):
        low = pl.multiple_of(64 * lax.rem(y_ref[0] + (4 - step), 4), 64)
        for pair in range(2):
            for kind in range(3):
                out_ref[3 * pair + kind, pl.ds(low, 64), :] = refs[step][pair, kind]


def join_shares(y, got):
    return pl.pallas_call(
        join_kernel,
        out_shape=jax.ShapeDtypeStruct((6, 256, 256), BF),
        in_specs=[smem()] + [vmem()] * 4,
        out_specs=vmem(),
        compiler_params=params(),
        cost_estimate=pl.CostEstimate(flops=0, bytes_accessed=2 << 20, transcendentals=0),
    )(y, *got)


def spatial_kernel(place_ref, weight_ref, *refs):
    out_ref = refs[-1]
    pieces = refs[:-1]
    place = place_ref[0]
    for frame in range(4):
        part, inner = frame // 2, frame % 2
        rows = jnp.concatenate(
            [pieces[2 * k + part][32 * inner : 32 * inner + 32, :] for k in range(NZ)], axis=0
        )
        qkv = [dot(rows, weight_ref[kind]).astype(BF) for kind in range(3)]
        for head in range(2):
            low = head * E
            query = qkv[0][:, low : low + E]
            key = qkv[1][:, low : low + E]
            value = qkv[2][:, low : low + E]
            weights = softmax(dot_t(query, key) * SCALE)
            mixed = dot(weights, value).astype(BF)
            for k in range(NZ):
                target = lax.rem(place + (OFFSETS[k] + NZ), NZ)
                out_ref[target, 32 * frame : 32 * frame + 32, low : low + E] = mixed[
                    32 * k : 32 * k + 32
                ]


def spatial_attend(place, weight, pieces):
    return pl.pallas_call(
        spatial_kernel,
        out_shape=jax.ShapeDtypeStruct((NZ, 128, 256), BF),
        in_specs=[smem(), vmem()] + [vmem()] * len(pieces),
        out_specs=vmem(),
        compiler_params=params(),
        cost_estimate=pl.CostEstimate(
            flops=2 * 1024 * 2048 * 768 * 2, bytes_accessed=8 << 20, transcendentals=8 * 65536
        ),
    )(place, weight, *pieces)


def column_block(weight_ref, block):
    return jnp.concatenate(
        [weight_ref[block, head, k // 4, k % 4, 0] for k in range(NZ) for head in range(2)], axis=0
    )


def weight_spec(blocks, which):
    return pl.BlockSpec((blocks, 2, 2, 4, 1, E, 256), lambda i: (i, 0, 0, 0, which, 0, 0))


def join_blocks_kernel(z_ref, *refs):
    out_ref = refs[-1]
    for step in range(4):
        out_ref[lax.rem(z_ref[0] + (4 - step), 4)] = refs[step][...]


def join_blocks(z, parts):
    return pl.pallas_call(
        join_blocks_kernel,
        out_shape=jax.ShapeDtypeStruct((4, 2, 128, 256), BF),
        in_specs=[smem()] + [vmem()] * 4,
        out_specs=vmem(),
        compiler_params=params(),
        cost_estimate=pl.CostEstimate(flops=0, bytes_accessed=512 << 10, transcendentals=0),
    )(z, *parts)


def middle_kernel(mix_ref, weight_ref, rows_ref, gain_ref, middle_ref, send_ref, total):
    step = pl.program_id(0)
    mix = jnp.concatenate([mix_ref[k] for k in range(NZ)], axis=1)
    for block in range(weight_ref.shape[0]):
        weight = column_block(weight_ref, block)
        low = pl.multiple_of((step * weight_ref.shape[0] + block) * 256, 256)
        total[:, pl.ds(low, 256)] = dot(mix, weight)

    @pl.when(step == pl.num_programs(0) - 1)
    def _():
        middle = (total[...] + rows_ref[...].astype(F32)).astype(BF)
        middle_ref[...] = middle
        values = middle.astype(F32)
        scaled = values * lax.rsqrt(jnp.mean(values * values, axis=-1, keepdims=True) + 1e-05)
        scaled = scaled * gain_ref[...]
        for group in range(4):
            chunk = jnp.concatenate(
                [scaled[32 * f + 8 * group : 32 * f + 8 * group + 8] for f in range(4)], axis=0
            ).astype(BF)
            for y in range(4):
                send_ref[(group // 2) * 8 + y * 2 + group % 2] = chunk


def middle_rows(mix, weight, rows, gain):
    steps = 4
    width = rows.shape[1]
    return pl.pallas_call(
        middle_kernel,
        grid=(steps,),
        out_shape=(
            jax.ShapeDtypeStruct((128, width), BF),
            jax.ShapeDtypeStruct((16, 32, width), BF),
        ),
        in_specs=[
            pl.BlockSpec((NZ, 128, 256), lambda i: (0, 0, 0)),
            weight_spec(8 // steps, 0),
            pl.BlockSpec((128, width), lambda i: (0, 0)),
            pl.BlockSpec((1, width), lambda i: (0, 0)),
        ],
        out_specs=(
            pl.BlockSpec((128, width), lambda i: (0, 0)),
            pl.BlockSpec((16, 32, width), lambda i: (0, 0, 0)),
        ),
        scratch_shapes=[pltpu.VMEM((128, width), F32)],
        compiler_params=params(),
        cost_estimate=pl.CostEstimate(
            flops=2 * 128 * 2048 * 2048, bytes_accessed=12 << 20, transcendentals=0
        ),
    )(mix, weight, rows, gain)


def temporal_kernel(start_ref, rows_ref, weight_ref, out_ref, qkv, bias):
    step = pl.program_id(0)
    kind = lax.rem(step, 3)
    rows_count = rows_ref.shape[0]
    weight = weight_ref[:, 0].reshape(2048, 256)
    qkv[kind] = dot(rows_ref[...], weight).astype(BF)

    @pl.when(step == 0)
    def _():
        start = start_ref[0]
        late = lax.broadcasted_iota(jnp.int32, (rows_count, rows_count), 0)
        early = lax.broadcasted_iota(jnp.int32, (rows_count, rows_count), 1)
        same = (late & 7) == (early & 7)
        allowed = same & (early <= late) & ((early >= 8 * start) == (late >= 8 * start))
        bias[...] = jnp.where(allowed, 0.0, -1e30)

    def attend(pair):
        block = 128
        for low in range(0, rows_count, block):
            for head in range(2):
                cols = slice(head * E, head * E + E)
                query = qkv[0, low : low + block, cols]
                key = qkv[1, : low + block, cols]
                value = qkv[2, : low + block, cols]
                scores = dot_t(query, key) * SCALE
                hidden = bias[low : low + block, : low + block]
                scores = jnp.where(hidden < 0.0, hidden, scores)
                at = 256 * pair + head * E
                mixed = dot(softmax(scores), value).astype(BF)
                out_ref[low // 32 : low // 32 + 4, :, at : at + E] = mixed.reshape(4, 32, E)

    @pl.when(step == 2)
    def _():
        attend(0)

    @pl.when(step == 5)
    def _():
        attend(1)


def temporal_attend(start, rows, weight):
    count, width = rows.shape
    return pl.pallas_call(
        temporal_kernel,
        grid=(6,),
        out_shape=jax.ShapeDtypeStruct((16, 32, 512), BF),
        in_specs=[
            smem(),
            pl.BlockSpec((count, width), lambda i: (0, 0)),
            pl.BlockSpec((8, 1, 256, 256), lambda i: (0, i, 0, 0)),
        ],
        out_specs=pl.BlockSpec((16, 32, 512), lambda i: (0, 0, 0)),
        scratch_shapes=[
            pltpu.VMEM((3, count, 256), BF),
            pltpu.VMEM((count, count), F32),
        ],
        compiler_params=params(),
        cost_estimate=pl.CostEstimate(
            flops=2 * 512 * 2048 * 1536, bytes_accessed=9 << 20, transcendentals=131072
        ),
    )(start, rows, weight)


def last_kernel(mix_ref, weight_ref, middle_ref, out_ref, total):
    step = pl.program_id(0)
    mix = jnp.concatenate(
        [
            jnp.concatenate([mix_ref[xl * 8 + y * 2 + c] for xl in range(2) for c in range(2)], axis=0)
            for y in range(4)
        ],
        axis=1,
    )
    for block in range(weight_ref.shape[0]):
        low = pl.multiple_of((step * weight_ref.shape[0] + block) * 256, 256)
        total[:, pl.ds(low, 256)] = dot(mix, column_block(weight_ref, block))

    @pl.when(step == pl.num_programs(0) - 1)
    def _():
        for group in range(4):
            rows = total[32 * group : 32 * group + 32].reshape(4, 8, -1)
            middle = jnp.stack(
                [
                    middle_ref[32 * f : 32 * f + 32].astype(F32)[8 * group : 8 * group + 8]
                    for f in range(4)
                ],
                axis=0,
            )
            out = jnp.transpose(rows + middle, (1, 0, 2)).astype(BF)
            out_ref[8 * group : 8 * group + 8] = out


def last_rows(mix, weight, middle):
    steps = 4
    width = middle.shape[1]
    return pl.pallas_call(
        last_kernel,
        grid=(steps,),
        out_shape=jax.ShapeDtypeStruct((32, 4, width), BF),
        in_specs=[
            pl.BlockSpec((16, 32, 512), lambda i: (0, 0, 0)),
            weight_spec(8 // steps, 1),
            pl.BlockSpec((128, width), lambda i: (0, 0)),
        ],
        out_specs=pl.BlockSpec((32, 4, width), lambda i: (0, 0, 0)),
        scratch_shapes=[pltpu.VMEM((128, width), F32)],
        compiler_params=params(),
        cost_estimate=pl.CostEstimate(
            flops=2 * 128 * 2048 * 2048, bytes_accessed=12 << 20, transcendentals=0
        ),
    )(mix, weight, middle)


def shifted(value, axis, step):
    count = lax.axis_size(axis)
    return lax.ppermute(value, axis, [(i, (i + step) % count) for i in range(count)])


def gathered_rows(chunks, beside):
    up, down = list(chunks), list(chunks)
    pieces = {0: list(chunks)}
    for step in (1, 2, 3):
        up = [shifted(value, "z", 1) for value in up]
        down = [shifted(value, "z", -1) for value in down]
        if step == 1:
            up, down, beside = lax.optimization_barrier((up, down, beside))
        pieces[-step], pieces[step] = up, down
    pieces[4] = [shifted(up[0], "z", 1), shifted(down[1], "z", -1)]
    return [value for offset in OFFSETS for value in pieces[offset]], beside


def local(stream, spatial_gain, spatial_qkv, spatial_out, temporal_gain, temporal_qkv, temporal_out, starts):
    patches, frames, width = stream.shape
    w, xl, y, c, z = (lax.axis_index(name) for name in ("w", "xl", "y", "c", "z"))

    place = (((w * 2 + xl) * 2 + c) * 4 + y).reshape(1)
    first, second, rows = norm_rows(
        place, stream, spatial_gain.reshape(1, width), jnp.transpose(temporal_qkv, (1, 0, 2))
    )

    first, spatial_out, temporal_out = lax.optimization_barrier((first, spatial_out, temporal_out))
    low = (lax.rem(y, 2) * E, ((w * 2 + xl) * 2 + y // 2) * 256)
    block = jnp.stack(
        [lax.dynamic_slice(weight, low, (E, 256)) for weight in (spatial_out, temporal_out)]
    )
    parts = []
    for k in range(4):
        pairs = [
            (a * 8 + b, (b // 4) * 8 + (b + 4 * a + k) % 8) for a in range(2) for b in range(8)
        ]
        parts.append(lax.ppermute(block, ("c", "z"), pairs))
    pieces, parts = gathered_rows((first, second), parts)
    outs = join_blocks(z.reshape(1), parts)
    outs = lax.all_gather(outs, ("w", "xl", "y", "c"), axis=0, tiled=False)
    outs = outs.reshape(8, 2, 2, 4, 2, E, 256)

    weight = jnp.transpose(spatial_qkv, (1, 0, 2))
    mix = spatial_attend(z.reshape(1), weight, pieces)
    mix, *pieces = lax.optimization_barrier((mix, *pieces))
    mix = lax.all_to_all(mix, "z", 0, 0, tiled=True)

    sends = split_shares(jnp.stack([z, y]).astype(jnp.int32), pieces)
    got = [sends[0]] + [shifted(sends[k], "y", k) for k in range(1, 4)]
    quarter = join_shares(y.reshape(1), got)
    quarter = lax.all_gather(quarter[None], ("w", "xl", "c"), axis=0, tiled=True)

    middle, send = middle_rows(mix, outs, rows, temporal_gain.reshape(1, width))
    window = lax.all_to_all(send, ("xl", "y", "c"), 0, 0, tiled=True)
    start = lax.dynamic_slice(starts, (w,), (1,))
    mix = temporal_attend(start, window.reshape(512, width), quarter)
    mix = lax.all_to_all(mix, ("xl", "y", "c"), 0, 0, tiled=True)
    return last_rows(mix, outs, middle)


def solution(mesh):
    names = ("w", "xl", "y", "c", "z")
    fine = Mesh(mesh.devices.reshape(2, 2, 4, 2, NZ), names)
    tm = ("w", "xl", "y", "c")
    placed = (
        P("z", tm, None),
        P(),
        P(None, None, "z"),
        P("z", None),
        P(),
        P(None, None, "z"),
        P("z", None),
        P(),
    )
    return jax.shard_map(
        local, mesh=fine, in_specs=placed, out_specs=P("z", tm, None), check_vma=False
    )
```

```python
import functools
import math

import jax
import jax.numpy as jnp
from jax import lax
from jax.experimental import pallas as pl
from jax.experimental.pallas import tpu as pltpu
from jax.sharding import Mesh
from jax.sharding import PartitionSpec as P

E = 128
SEQ = 64
SCALE = 1.0 / math.sqrt(E)
BF = jnp.bfloat16
F32 = jnp.float32
NZ = 8
VMEM_LIMIT = 28 * 1024 * 1024
OFFSETS = (0, -1, 1, -2, 2, -3, 3, 4)


def params():
    return pltpu.CompilerParams(vmem_limit_bytes=VMEM_LIMIT)


def vmem():
    return pl.BlockSpec(memory_space=pltpu.VMEM)


def smem():
    return pl.BlockSpec(memory_space=pltpu.SMEM)


def normed(values, gain):
    scaled = values * lax.rsqrt(jnp.mean(values * values, axis=-1, keepdims=True) + 1e-05)
    return (scaled * gain).astype(BF)


def softmax(scores):
    top = jnp.max(scores, axis=-1, keepdims=True)
    shifted = jnp.exp2((scores - top) * (SCALE * math.log2(math.e)))
    return (shifted * (1.0 / jnp.sum(shifted, axis=-1, keepdims=True))).astype(BF)


def dot(a, b):
    return jnp.dot(a, b, preferred_element_type=F32)


def dot_t(a, b):
    return lax.dot_general(a, b, (((1,), (1,)), ((), ())), preferred_element_type=F32)


def norm_kernel(place_ref, x_ref, gain_ref, qkv_ref, a_ref, b_ref, rows_ref):
    gain = gain_ref[...]
    values = jnp.transpose(x_ref[...].astype(F32), (1, 0, 2)).reshape(rows_ref.shape)
    half = rows_ref.shape[0] // 2
    rows_ref[...] = values.astype(BF)
    a_ref[:half] = normed(values[:half], gain)
    b_ref[:half] = normed(values[half:], gain)
    b_ref[half:, 1024:] = jnp.zeros((16, 1024), BF)
    for kind in range(3):
        share = qkv_ref[kind]
        ref = (a_ref, b_ref)[kind // 2]
        for group in range(4):
            low = 256 * (4 * (kind % 2) + group)
            ref[half:, low : low + 256] = share[16 * group : 16 * group + 16]


def norm_rows(place, stream, gain, temporal_qkv):
    patches, frames, width = stream.shape
    count = patches * frames
    half = jax.ShapeDtypeStruct((count // 2 + 16, width), BF)
    whole = lambda *shape: pl.BlockSpec(shape, lambda i, at: (0,) * len(shape))
    return pl.pallas_call(
        norm_kernel,
        grid_spec=pltpu.PrefetchScalarGridSpec(
            num_scalar_prefetch=1,
            grid=(1,),
            in_specs=[
                whole(patches, frames, width),
                whole(1, width),
                pl.BlockSpec((3, 64, 256), lambda i, at: (0, at[0], 0)),
            ],
            out_specs=(
                whole(count // 2 + 16, width),
                whole(count // 2 + 16, width),
                whole(count, width),
            ),
        ),
        out_shape=(half, half, jax.ShapeDtypeStruct((count, width), BF)),
        compiler_params=params(),
        cost_estimate=pl.CostEstimate(
            flops=4 * count * width, bytes_accessed=6 * count * width, transcendentals=0
        ),
    )(place, stream, gain, temporal_qkv)


def split_kernel(place_ref, *refs):
    pieces, sends = refs[:-4], refs[-4:]
    z, y = place_ref[0], place_ref[1]
    for k in range(NZ):
        source = lax.rem(z + (OFFSETS[k] + NZ), NZ)
        step = lax.rem(source // 2 + 4 - y, 4)
        pair = lax.rem(source, 2)
        for index, send_ref in enumerate(sends):

            @pl.when(step == index)
            def _():
                for kind in range(3):
                    for group in range(4):
                        low = 256 * (4 * (kind % 2) + group)
                        rows = slice(16 * group, 16 * group + 16)
                        value = pieces[2 * k + kind // 2][:, low : low + 256]
                        send_ref[pair, kind, rows] = value


def split_shares(place, pieces):
    return pl.pallas_call(
        split_kernel,
        grid=(1,),
        out_shape=(jax.ShapeDtypeStruct((2, 3, 64, 256), BF),) * 4,
        in_specs=[smem()] + [pl.BlockSpec((16, 2048), lambda i: (4, 0))] * len(pieces),
        out_specs=(pl.BlockSpec((2, 3, 64, 256), lambda i: (0, 0, 0, 0)),) * 4,
        compiler_params=params(),
        cost_estimate=pl.CostEstimate(flops=0, bytes_accessed=2 << 20, transcendentals=0),
    )(place, *pieces)


def join_kernel(y_ref, *refs):
    out_ref = refs[-1]
    for step in range(4):
        low = pl.multiple_of(64 * lax.rem(y_ref[0] + (4 - step), 4), 64)
        for pair in range(2):
            for kind in range(3):
                out_ref[3 * pair + kind, pl.ds(low, 64), :] = refs[step][pair, kind]


def join_shares(y, got):
    return pl.pallas_call(
        join_kernel,
        out_shape=jax.ShapeDtypeStruct((6, 256, 256), BF),
        in_specs=[smem()] + [vmem()] * 4,
        out_specs=vmem(),
        compiler_params=params(),
        cost_estimate=pl.CostEstimate(flops=0, bytes_accessed=2 << 20, transcendentals=0),
    )(y, *got)


def attend(chains):
    scores = [dot_t(query, key) for query, key, _, _ in chains]
    scores = [
        one if chain[3] is None else jnp.where(chain[3] < 0.0, chain[3], one)
        for one, chain in zip(scores, chains)
    ]
    weights = [softmax(one) for one in scores]
    return [dot(one, chain[2]).astype(BF) for one, chain in zip(weights, chains)]


def spatial_kernel(place_ref, weight_ref, *refs):
    pieces, out_ref, qkv = refs[: 2 * NZ], refs[2 * NZ], refs[2 * NZ + 1]
    place = place_ref[0]
    for frame in range(4):
        low = 32 * (frame % 2)
        rows = jnp.concatenate(
            [pieces[2 * k + frame // 2][low : low + 32, :] for k in range(NZ)], axis=0
        )
        for kind in range(3):
            qkv[kind, 256 * frame : 256 * frame + 256] = dot(rows, weight_ref[kind]).astype(BF)
    for frames in ((0, 1), (2, 3)):
        spots = [(frame, head * E) for frame in frames for head in range(2)]
        chains = []
        for frame, low in spots:
            at, cols = slice(256 * frame, 256 * frame + 256), slice(low, low + E)
            chains.append((qkv[0, at, cols], qkv[1, at, cols], qkv[2, at, cols], None))
        for (frame, low), mixed in zip(spots, attend(chains)):
            for k in range(NZ):
                target = lax.rem(place + (OFFSETS[k] + NZ), NZ)
                out_ref[target, 32 * frame : 32 * frame + 32, low : low + E] = mixed[
                    32 * k : 32 * k + 32
                ]


def spatial_attend(place, weight, pieces):
    return pl.pallas_call(
        spatial_kernel,
        out_shape=jax.ShapeDtypeStruct((NZ, 128, 256), BF),
        in_specs=[smem(), vmem()] + [vmem()] * len(pieces),
        out_specs=vmem(),
        scratch_shapes=[pltpu.VMEM((3, 1024, 256), BF)],
        compiler_params=params(),
        cost_estimate=pl.CostEstimate(
            flops=2 * 1024 * 2048 * 768 * 2, bytes_accessed=8 << 20, transcendentals=8 * 65536
        ),
    )(place, weight, *pieces)


def column_block(read):
    return jnp.concatenate([read(head, k // 4, k % 4) for k in range(NZ) for head in range(2)], axis=0)


def join_blocks_kernel(z_ref, *refs):
    out_ref = refs[-1]
    for step in range(4):
        out_ref[lax.rem(z_ref[0] + (4 - step), 4)] = refs[step][...]


def join_blocks(z, parts):
    return pl.pallas_call(
        join_blocks_kernel,
        out_shape=jax.ShapeDtypeStruct((4, 2, 128, 256), BF),
        in_specs=[smem()] + [vmem()] * 4,
        out_specs=vmem(),
        compiler_params=params(),
        cost_estimate=pl.CostEstimate(flops=0, bytes_accessed=512 << 10, transcendentals=0),
    )(z, *parts)


def middle_kernel(mix_ref, weight_ref, rows_ref, gain_ref, middle_ref, send_ref, weight, total, sems):
    copies = [
        pltpu.make_async_copy(weight_ref.at[block, :, :, :, 0], weight.at[block], sems.at[block])
        for block in range(8)
    ]
    for copy in copies:
        copy.start()
    mix = jnp.concatenate([mix_ref[k] for k in range(NZ)], axis=1)
    for block in range(8):
        copies[block].wait()
        part = column_block(lambda *at: weight[(block, *at)])
        total[:, 256 * block : 256 * block + 256] = dot(mix, part)
    middle = (total[...] + rows_ref[...].astype(F32)).astype(BF)
    middle_ref[...] = middle
    values = middle.astype(F32)
    scaled = values * lax.rsqrt(jnp.mean(values * values, axis=-1, keepdims=True) + 1e-05)
    scaled = scaled * gain_ref[...]
    for group in range(4):
        chunk = jnp.concatenate(
            [scaled[32 * f + 8 * group : 32 * f + 8 * group + 8] for f in range(4)], axis=0
        ).astype(BF)
        for y in range(4):
            send_ref[(group // 2) * 8 + y * 2 + group % 2] = chunk


def middle_rows(mix, weight, rows, gain):
    width = rows.shape[1]
    return pl.pallas_call(
        middle_kernel,
        out_shape=(
            jax.ShapeDtypeStruct((128, width), BF),
            jax.ShapeDtypeStruct((16, 32, width), BF),
        ),
        in_specs=[vmem(), pl.BlockSpec(memory_space=pl.ANY), vmem(), vmem()],
        out_specs=(vmem(), vmem()),
        scratch_shapes=[
            pltpu.VMEM((8, 2, 2, 4, E, 256), BF),
            pltpu.VMEM((128, width), F32),
            pltpu.SemaphoreType.DMA((8,)),
        ],
        compiler_params=params(),
        cost_estimate=pl.CostEstimate(
            flops=2 * 128 * 2048 * 2048, bytes_accessed=12 << 20, transcendentals=0
        ),
    )(mix, weight, rows, gain)


def temporal_kernel(start_ref, rows_ref, weight_ref, out_ref, qkv, bias):
    count = rows_ref.shape[0]
    start = start_ref[0]
    late = lax.broadcasted_iota(jnp.int32, (count, count), 0)
    early = lax.broadcasted_iota(jnp.int32, (count, count), 1)
    same = (late & 7) == (early & 7)
    allowed = same & (early <= late) & ((early >= 8 * start) == (late >= 8 * start))
    bias[...] = jnp.where(allowed, 0.0, -1e30)
    for block in range(6):
        qkv[block] = dot(rows_ref[...], weight_ref[:, block].reshape(2048, 256)).astype(BF)
    size = 256
    for pair in range(2):
        for low in range(0, count, size):
            chains = []
            high = low + size
            for head in range(2):
                cols = slice(head * E, head * E + E)
                chains.append(
                    (
                        qkv[3 * pair, low:high, cols],
                        qkv[3 * pair + 1, :high, cols],
                        qkv[3 * pair + 2, :high, cols],
                        bias[low:high, :high],
                    )
                )
            for head, mixed in enumerate(attend(chains)):
                at = 256 * pair + head * E
                out_ref[low // 32 : high // 32, :, at : at + E] = mixed.reshape(size // 32, 32, E)


def temporal_attend(start, rows, weight):
    count, width = rows.shape
    return pl.pallas_call(
        temporal_kernel,
        out_shape=jax.ShapeDtypeStruct((16, 32, 512), BF),
        in_specs=[smem(), vmem(), vmem()],
        out_specs=vmem(),
        scratch_shapes=[
            pltpu.VMEM((6, count, 256), BF),
            pltpu.VMEM((count, count), F32),
        ],
        compiler_params=params(),
        cost_estimate=pl.CostEstimate(
            flops=2 * 512 * 2048 * 1536, bytes_accessed=9 << 20, transcendentals=131072
        ),
    )(start, rows, weight)


def last_kernel(mix_ref, weight_ref, middle_ref, out_ref, total):
    mix = jnp.concatenate(
        [
            jnp.concatenate([mix_ref[xl * 8 + y * 2 + c] for xl in range(2) for c in range(2)], axis=0)
            for y in range(4)
        ],
        axis=1,
    )
    for block in range(8):
        part = column_block(lambda *at: weight_ref[(block, *at, 1)])
        total[:, 256 * block : 256 * block + 256] = dot(mix, part)
    for group in range(4):
        rows = total[32 * group : 32 * group + 32].reshape(4, 8, -1)
        middle = jnp.stack(
            [
                middle_ref[32 * f : 32 * f + 32].astype(F32)[8 * group : 8 * group + 8]
                for f in range(4)
            ],
            axis=0,
        )
        out = jnp.transpose(rows + middle, (1, 0, 2)).astype(BF)
        out_ref[8 * group : 8 * group + 8] = out


def last_rows(mix, weight, middle):
    width = middle.shape[1]
    return pl.pallas_call(
        last_kernel,
        out_shape=jax.ShapeDtypeStruct((32, 4, width), BF),
        in_specs=[vmem()] * 3,
        out_specs=vmem(),
        scratch_shapes=[pltpu.VMEM((128, width), F32)],
        compiler_params=params(),
        cost_estimate=pl.CostEstimate(
            flops=2 * 128 * 2048 * 2048, bytes_accessed=12 << 20, transcendentals=0
        ),
    )(mix, weight, middle)


def shifted(value, axis, step):
    count = lax.axis_size(axis)
    return lax.ppermute(value, axis, [(i, (i + step) % count) for i in range(count)])


def gathered_rows(chunks):
    up, down = list(chunks), list(chunks)
    pieces = {0: list(chunks)}
    for step in (1, 2, 3):
        up = [shifted(value, "z", 1) for value in up]
        down = [shifted(value, "z", -1) for value in down]
        pieces[-step], pieces[step] = up, down
    pieces[4] = [shifted(up[0], "z", 1), shifted(down[1], "z", -1)]
    return [value for offset in OFFSETS for value in pieces[offset]]


def local(stream, spatial_gain, spatial_qkv, spatial_out, temporal_gain, temporal_qkv, temporal_out, starts):
    patches, frames, width = stream.shape
    w, xl, y, c, z = (lax.axis_index(name) for name in ("w", "xl", "y", "c", "z"))

    place = (((w * 2 + xl) * 2 + c) * 4 + y).reshape(1)
    first, second, rows = norm_rows(
        place, stream, spatial_gain.reshape(1, width), jnp.transpose(temporal_qkv, (1, 0, 2))
    )

    low = (lax.rem(y, 2) * E, ((w * 2 + xl) * 2 + y // 2) * 256)
    block = jnp.stack(
        [lax.dynamic_slice(weight, low, (E, 256)) for weight in (spatial_out, temporal_out)]
    )
    parts = []
    for k in range(4):
        pairs = [
            (a * 8 + b, (b // 4) * 8 + (b + 4 * a + k) % 8) for a in range(2) for b in range(8)
        ]
        parts.append(lax.ppermute(block, ("c", "z"), pairs))
    first, second, parts = lax.optimization_barrier((first, second, parts))
    outs = join_blocks(z.reshape(1), parts)
    outs = lax.all_gather(outs, ("w", "xl", "y", "c"), axis=0, tiled=False)
    outs = outs.reshape(8, 2, 2, 4, 2, E, 256)

    pieces = gathered_rows((first, second))

    sends = split_shares(jnp.stack([z, y]).astype(jnp.int32), pieces)
    got = [sends[0]] + [shifted(sends[k], "y", k) for k in range(1, 4)]

    weight = jnp.transpose(spatial_qkv, (1, 0, 2))
    mix = spatial_attend(z.reshape(1), weight, pieces)
    mix, *got = lax.optimization_barrier((mix, *got))
    quarter = join_shares(y.reshape(1), got)
    mix, quarter = lax.optimization_barrier((mix, quarter))
    quarter = lax.all_gather(quarter[None], ("w", "xl", "c"), axis=0, tiled=True)
    mix = lax.all_to_all(mix, "z", 0, 0, tiled=True)

    middle, send = middle_rows(mix, outs, rows, temporal_gain.reshape(1, width))
    window = lax.all_to_all(send, ("xl", "y", "c"), 0, 0, tiled=True)
    start = lax.dynamic_slice(starts, (w,), (1,))
    mix = temporal_attend(start, window.reshape(512, width), quarter)
    mix = lax.all_to_all(mix, ("xl", "y", "c"), 0, 0, tiled=True)
    return last_rows(mix, outs, middle)


def solution(mesh):
    names = ("w", "xl", "y", "c", "z")
    fine = Mesh(mesh.devices.reshape(2, 2, 4, 2, NZ), names)
    tm = ("w", "xl", "y", "c")
    placed = (
        P("z", tm, None),
        P(),
        P(None, None, "z"),
        P("z", None),
        P(),
        P(None, None, "z"),
        P("z", None),
        P(),
    )
    return jax.shard_map(
        local, mesh=fine, in_specs=placed, out_specs=P("z", tm, None), check_vma=False
    )
```

```python
import functools
import math

import jax
import jax.numpy as jnp
from jax import lax
from jax.experimental import pallas as pl
from jax.experimental.pallas import tpu as pltpu
from jax.sharding import Mesh
from jax.sharding import PartitionSpec as P

E = 128
SEQ = 64
SCALE = 1.0 / math.sqrt(E)
BF = jnp.bfloat16
F32 = jnp.float32
NZ = 8
VMEM_LIMIT = 28 * 1024 * 1024
OFFSETS = (0, -1, 1, -2, 2, -3, 3, 4)


def params():
    return pltpu.CompilerParams(vmem_limit_bytes=VMEM_LIMIT)


def vmem():
    return pl.BlockSpec(memory_space=pltpu.VMEM)


def smem():
    return pl.BlockSpec(memory_space=pltpu.SMEM)


def normed(values, gain):
    scaled = values * lax.rsqrt(jnp.mean(values * values, axis=-1, keepdims=True) + 1e-05)
    return (scaled * gain).astype(BF)


def softmax(scores):
    top = jnp.max(scores, axis=-1, keepdims=True)
    shifted = jnp.exp2((scores - top) * (SCALE * math.log2(math.e)))
    return (shifted * (1.0 / jnp.sum(shifted, axis=-1, keepdims=True))).astype(BF)


def dot(a, b):
    return jnp.dot(a, b, preferred_element_type=F32)


def dot_t(a, b):
    return lax.dot_general(a, b, (((1,), (1,)), ((), ())), preferred_element_type=F32)


def norm_kernel(place_ref, x_ref, gain_ref, qkv_ref, a_ref, b_ref, rows_ref):
    gain = gain_ref[...]
    values = jnp.transpose(x_ref[...].astype(F32), (1, 0, 2)).reshape(rows_ref.shape)
    half = rows_ref.shape[0] // 2
    rows_ref[...] = values.astype(BF)
    a_ref[:half] = normed(values[:half], gain)
    b_ref[:half] = normed(values[half:], gain)
    b_ref[half:, 1024:] = jnp.zeros((16, 1024), BF)
    for kind in range(3):
        share = qkv_ref[kind]
        ref = (a_ref, b_ref)[kind // 2]
        for group in range(4):
            low = 256 * (4 * (kind % 2) + group)
            ref[half:, low : low + 256] = share[16 * group : 16 * group + 16]


def norm_rows(place, stream, gain, temporal_qkv):
    patches, frames, width = stream.shape
    count = patches * frames
    half = jax.ShapeDtypeStruct((count // 2 + 16, width), BF)
    whole = lambda *shape: pl.BlockSpec(shape, lambda i, at: (0,) * len(shape))
    return pl.pallas_call(
        norm_kernel,
        grid_spec=pltpu.PrefetchScalarGridSpec(
            num_scalar_prefetch=1,
            grid=(1,),
            in_specs=[
                whole(patches, frames, width),
                whole(1, width),
                pl.BlockSpec((3, 64, 256), lambda i, at: (0, at[0], 0)),
            ],
            out_specs=(
                whole(count // 2 + 16, width),
                whole(count // 2 + 16, width),
                whole(count, width),
            ),
        ),
        out_shape=(half, half, jax.ShapeDtypeStruct((count, width), BF)),
        compiler_params=params(),
        cost_estimate=pl.CostEstimate(
            flops=4 * count * width, bytes_accessed=6 * count * width, transcendentals=0
        ),
    )(place, stream, gain, temporal_qkv)


def split_kernel(place_ref, *refs):
    pieces, sends = refs[:-4], refs[-4:]
    z, y = place_ref[0], place_ref[1]
    for k in range(NZ):
        source = lax.rem(z + (OFFSETS[k] + NZ), NZ)
        step = lax.rem(source // 2 + 4 - y, 4)
        pair = lax.rem(source, 2)
        for index, send_ref in enumerate(sends):

            @pl.when(step == index)
            def _():
                for kind in range(3):
                    for group in range(4):
                        low = 256 * (4 * (kind % 2) + group)
                        rows = slice(16 * group, 16 * group + 16)
                        value = pieces[2 * k + kind // 2][:, low : low + 256]
                        send_ref[pair, kind, rows] = value


def split_shares(place, pieces):
    return pl.pallas_call(
        split_kernel,
        grid=(1,),
        out_shape=(jax.ShapeDtypeStruct((2, 3, 64, 256), BF),) * 4,
        in_specs=[smem()] + [pl.BlockSpec((16, 2048), lambda i: (4, 0))] * len(pieces),
        out_specs=(pl.BlockSpec((2, 3, 64, 256), lambda i: (0, 0, 0, 0)),) * 4,
        compiler_params=params(),
        cost_estimate=pl.CostEstimate(flops=0, bytes_accessed=2 << 20, transcendentals=0),
    )(place, *pieces)


def join_kernel(y_ref, *refs):
    out_ref = refs[-1]
    for step in range(4):
        low = pl.multiple_of(64 * lax.rem(y_ref[0] + (4 - step), 4), 64)
        for pair in range(2):
            for kind in range(3):
                out_ref[3 * pair + kind, pl.ds(low, 64), :] = refs[step][pair, kind]


def join_shares(y, got):
    return pl.pallas_call(
        join_kernel,
        out_shape=jax.ShapeDtypeStruct((6, 256, 256), BF),
        in_specs=[smem()] + [vmem()] * 4,
        out_specs=vmem(),
        compiler_params=params(),
        cost_estimate=pl.CostEstimate(flops=0, bytes_accessed=2 << 20, transcendentals=0),
    )(y, *got)


def attend(chains):
    scores = [dot_t(query, key) for query, key, _, _ in chains]
    scores = [
        one if chain[3] is None else jnp.where(chain[3] < 0.0, chain[3], one)
        for one, chain in zip(scores, chains)
    ]
    weights = [softmax(one) for one in scores]
    return [dot(one, chain[2]).astype(BF) for one, chain in zip(weights, chains)]


def spatial_kernel(place_ref, weight_ref, *refs):
    pieces, out_ref, qkv = refs[: 2 * NZ], refs[2 * NZ], refs[2 * NZ + 1]
    place = place_ref[0]
    for frame in range(4):
        low = 32 * (frame % 2)
        rows = jnp.concatenate(
            [pieces[2 * k + frame // 2][low : low + 32, :] for k in range(NZ)], axis=0
        )
        for kind in range(3):
            qkv[kind, 256 * frame : 256 * frame + 256] = dot(rows, weight_ref[kind]).astype(BF)
    for frames in ((0, 1), (2, 3)):
        spots = [(frame, head * E) for frame in frames for head in range(2)]
        chains = []
        for frame, low in spots:
            at, cols = slice(256 * frame, 256 * frame + 256), slice(low, low + E)
            chains.append((qkv[0, at, cols], qkv[1, at, cols], qkv[2, at, cols], None))
        for (frame, low), mixed in zip(spots, attend(chains)):
            for k in range(NZ):
                target = lax.rem(place + (OFFSETS[k] + NZ), NZ)
                out_ref[target, 32 * frame : 32 * frame + 32, low : low + E] = mixed[
                    32 * k : 32 * k + 32
                ]


def spatial_attend(place, weight, pieces):
    return pl.pallas_call(
        spatial_kernel,
        out_shape=jax.ShapeDtypeStruct((NZ, 128, 256), BF),
        in_specs=[smem(), vmem()] + [vmem()] * len(pieces),
        out_specs=vmem(),
        scratch_shapes=[pltpu.VMEM((3, 1024, 256), BF)],
        compiler_params=params(),
        cost_estimate=pl.CostEstimate(
            flops=2 * 1024 * 2048 * 768 * 2, bytes_accessed=8 << 20, transcendentals=8 * 65536
        ),
    )(place, weight, *pieces)


def column_block(read):
    return jnp.concatenate([read(head, k // 4, k % 4) for k in range(NZ) for head in range(2)], axis=0)


def join_blocks_kernel(z_ref, *refs):
    out_ref = refs[-1]
    for step in range(4):
        out_ref[lax.rem(z_ref[0] + (4 - step), 4)] = refs[step][...]


def join_blocks(z, parts):
    return pl.pallas_call(
        join_blocks_kernel,
        out_shape=jax.ShapeDtypeStruct((4, 128, 256), BF),
        in_specs=[smem()] + [vmem()] * 4,
        out_specs=vmem(),
        compiler_params=params(),
        cost_estimate=pl.CostEstimate(flops=0, bytes_accessed=512 << 10, transcendentals=0),
    )(z, *parts)


def middle_kernel(mix_ref, weight_ref, rows_ref, gain_ref, middle_ref, send_ref, total):
    mix = jnp.concatenate([mix_ref[k] for k in range(NZ)], axis=1)
    for block in range(8):
        part = column_block(lambda *at: weight_ref[(block, *at)])
        total[:, 256 * block : 256 * block + 256] = dot(mix, part)
    middle = (total[...] + rows_ref[...].astype(F32)).astype(BF)
    middle_ref[...] = middle
    values = middle.astype(F32)
    scaled = values * lax.rsqrt(jnp.mean(values * values, axis=-1, keepdims=True) + 1e-05)
    scaled = scaled * gain_ref[...]
    for group in range(4):
        chunk = jnp.concatenate(
            [scaled[32 * f + 8 * group : 32 * f + 8 * group + 8] for f in range(4)], axis=0
        ).astype(BF)
        for y in range(4):
            send_ref[(group // 2) * 8 + y * 2 + group % 2] = chunk


def middle_rows(mix, weight, rows, gain):
    width = rows.shape[1]
    return pl.pallas_call(
        middle_kernel,
        out_shape=(
            jax.ShapeDtypeStruct((128, width), BF),
            jax.ShapeDtypeStruct((16, 32, width), BF),
        ),
        in_specs=[vmem()] * 4,
        out_specs=(vmem(), vmem()),
        scratch_shapes=[pltpu.VMEM((128, width), F32)],
        compiler_params=params(),
        cost_estimate=pl.CostEstimate(
            flops=2 * 128 * 2048 * 2048, bytes_accessed=12 << 20, transcendentals=0
        ),
    )(mix, weight, rows, gain)


def temporal_kernel(start_ref, rows_ref, weight_ref, out_ref, qkv, bias):
    count = rows_ref.shape[0]
    start = start_ref[0]
    late = lax.broadcasted_iota(jnp.int32, (count, count), 0)
    early = lax.broadcasted_iota(jnp.int32, (count, count), 1)
    same = (late & 7) == (early & 7)
    allowed = same & (early <= late) & ((early >= 8 * start) == (late >= 8 * start))
    bias[...] = jnp.where(allowed, 0.0, -1e30)
    for block in range(6):
        qkv[block] = dot(rows_ref[...], weight_ref[:, block].reshape(2048, 256)).astype(BF)
    size = 256
    for pair in range(2):
        for low in range(0, count, size):
            chains = []
            high = low + size
            for head in range(2):
                cols = slice(head * E, head * E + E)
                chains.append(
                    (
                        qkv[3 * pair, low:high, cols],
                        qkv[3 * pair + 1, :high, cols],
                        qkv[3 * pair + 2, :high, cols],
                        bias[low:high, :high],
                    )
                )
            for head, mixed in enumerate(attend(chains)):
                for spot in range(low // 32, high // 32):
                    rows = mixed[32 * spot - low : 32 * spot - low + 32]
                    at = (spot // 2 * 2 + head, spot % 2, slice(None), slice(E * pair, E * pair + E))
                    out_ref[at] = rows


def temporal_attend(start, rows, weight):
    count, width = rows.shape
    return pl.pallas_call(
        temporal_kernel,
        out_shape=jax.ShapeDtypeStruct((16, 2, 32, 256), BF),
        in_specs=[smem(), vmem(), vmem()],
        out_specs=vmem(),
        scratch_shapes=[
            pltpu.VMEM((6, count, 256), BF),
            pltpu.VMEM((count, count), F32),
        ],
        compiler_params=params(),
        cost_estimate=pl.CostEstimate(
            flops=2 * 512 * 2048 * 1536, bytes_accessed=9 << 20, transcendentals=131072
        ),
    )(start, rows, weight)


def last_kernel(place_ref, mix_ref, *refs):
    pieces, (keep_ref, give_ref, total) = refs[: NZ + 1], refs[NZ + 1 :]
    z, c = place_ref[0], place_ref[1]
    blocks = []
    for k in range(NZ):
        source = lax.rem(z + (OFFSETS[k] + NZ), NZ)
        cols = pl.ds(pl.multiple_of(lax.rem(source, 2) * E, E), E)
        blocks.append(
            jnp.concatenate(
                [
                    mix_ref[xl * 8 + source // 2 * 2 + core, frames, :, cols]
                    for frames in range(2)
                    for xl in range(2)
                    for core in range(2)
                ],
                axis=0,
            )
        )
    mix = jnp.concatenate(blocks, axis=1)
    for low in range(0, 2048, 512):
        part = jnp.concatenate([piece[:, low : low + 512] for piece in pieces], axis=0)
        total[:, :, low : low + 512] = dot(mix, part).reshape(2, 128, 512)
    keep_ref[...] = total[c]
    give_ref[...] = total[1 - c].astype(BF)


def last_sums(place, mix, pieces):
    width = pieces[0].shape[1]
    return pl.pallas_call(
        last_kernel,
        out_shape=(
            jax.ShapeDtypeStruct((128, width), F32),
            jax.ShapeDtypeStruct((128, width), BF),
        ),
        in_specs=[smem()] + [vmem()] * (NZ + 2),
        out_specs=(vmem(), vmem()),
        scratch_shapes=[pltpu.VMEM((2, 128, width), F32)],
        compiler_params=params(),
        cost_estimate=pl.CostEstimate(
            flops=2 * 128 * 2048 * 2048, bytes_accessed=8 << 20, transcendentals=0
        ),
    )(place, mix, *pieces)


def end_kernel(keep_ref, got_ref, middle_ref, out_ref):
    for group in range(4):
        at = slice(32 * group, 32 * group + 32)
        rows = (keep_ref[at] + got_ref[at].astype(F32)).reshape(4, 8, -1)
        middle = jnp.stack(
            [
                middle_ref[32 * f : 32 * f + 32].astype(F32)[8 * group : 8 * group + 8]
                for f in range(4)
            ],
            axis=0,
        )
        out = jnp.transpose(rows + middle, (1, 0, 2)).astype(BF)
        out_ref[8 * group : 8 * group + 8] = out


def end_rows(keep, got, middle):
    return pl.pallas_call(
        end_kernel,
        out_shape=jax.ShapeDtypeStruct((32, 4, middle.shape[1]), BF),
        in_specs=[vmem()] * 3,
        out_specs=vmem(),
        compiler_params=params(),
        cost_estimate=pl.CostEstimate(flops=1 << 20, bytes_accessed=3 << 20, transcendentals=0),
    )(keep, got, middle)


def shifted(value, axis, step):
    count = lax.axis_size(axis)
    return lax.ppermute(value, axis, [(i, (i + step) % count) for i in range(count)])


def gathered_rows(chunks):
    up, down = list(chunks), list(chunks)
    pieces = {0: list(chunks)}
    for step in (1, 2, 3):
        up = [shifted(value, "z", 1) for value in up]
        down = [shifted(value, "z", -1) for value in down]
        pieces[-step], pieces[step] = up, down
    pieces[4] = [shifted(up[0], "z", 1), shifted(down[1], "z", -1)]
    return [value for offset in OFFSETS for value in pieces[offset]]


def local(stream, spatial_gain, spatial_qkv, spatial_out, temporal_gain, temporal_qkv, temporal_out, starts):
    patches, frames, width = stream.shape
    w, xl, y, c, z = (lax.axis_index(name) for name in ("w", "xl", "y", "c", "z"))

    place = (((w * 2 + xl) * 2 + c) * 4 + y).reshape(1)
    first, second, rows = norm_rows(
        place, stream, spatial_gain.reshape(1, width), jnp.transpose(temporal_qkv, (1, 0, 2))
    )

    low = (lax.rem(y, 2) * E, ((w * 2 + xl) * 2 + y // 2) * 256)
    block = lax.dynamic_slice(spatial_out, low, (E, 256))
    parts = []
    for k in range(4):
        pairs = [
            (a * 8 + b, (b // 4) * 8 + (b + 4 * a + k) % 8) for a in range(2) for b in range(8)
        ]
        parts.append(lax.ppermute(block, ("c", "z"), pairs))
    first, second, parts = lax.optimization_barrier((first, second, parts))
    whole_out = join_blocks(z.reshape(1), parts)
    whole_out = lax.all_gather(whole_out, ("w", "xl", "y", "c"), axis=0, tiled=False)
    whole_out = whole_out.reshape(8, 2, 2, 4, E, 256)

    pieces = gathered_rows((first, second))

    sends = split_shares(jnp.stack([z, y]).astype(jnp.int32), pieces)
    got = [sends[0]] + [shifted(sends[k], "y", k) for k in range(1, 4)]

    weight = jnp.transpose(spatial_qkv, (1, 0, 2))
    mix = spatial_attend(z.reshape(1), weight, pieces)
    mix, *got = lax.optimization_barrier((mix, *got))
    quarter = join_shares(y.reshape(1), got)
    mix, quarter, whole_out = lax.optimization_barrier((mix, quarter, whole_out))
    quarter = lax.all_gather(quarter[None], ("w", "xl", "c"), axis=0, tiled=True)
    mix = lax.all_to_all(mix, "z", 0, 0, tiled=True)

    middle, send = middle_rows(mix, whole_out, rows, temporal_gain.reshape(1, width))

    half = lax.dynamic_slice(temporal_out, (c * E, 0), (E, width))
    send, half = lax.optimization_barrier((send, half))
    up, down = half, half
    halves = [half]
    for step in (1, 2, 3):
        up, down = shifted(up, "z", 1), shifted(down, "z", -1)
        halves += [up, down]
    halves += [shifted(up[:64], "z", 1), shifted(down[64:], "z", -1)]

    window = lax.all_to_all(send, ("xl", "y", "c"), 0, 0, tiled=True)
    window, *halves[1:5] = lax.optimization_barrier((window, *halves[1:5]))
    start = lax.dynamic_slice(starts, (w,), (1,))
    mix = temporal_attend(start, window.reshape(512, width), quarter)
    mix = lax.all_to_all(mix, ("xl", "y", "c"), 0, 0, tiled=True)
    keep, give = last_sums(jnp.stack([z, c]).astype(jnp.int32), mix, halves)
    return end_rows(keep, shifted(give, "c", 1), middle)


def solution(mesh):
    names = ("w", "xl", "y", "c", "z")
    fine = Mesh(mesh.devices.reshape(2, 2, 4, 2, NZ), names)
    tm = ("w", "xl", "y", "c")
    placed = (
        P("z", tm, None),
        P(),
        P(None, None, "z"),
        P("z", None),
        P(),
        P(None, None, "z"),
        P("z", None),
        P(),
    )
    return jax.shard_map(
        local, mesh=fine, in_specs=placed, out_specs=P("z", tm, None), check_vma=False
    )
```

```python
import functools
import math

import jax
import jax.numpy as jnp
from jax import lax
from jax.experimental import pallas as pl
from jax.experimental.pallas import tpu as pltpu
from jax.sharding import Mesh
from jax.sharding import PartitionSpec as P

E = 128
SEQ = 64
SCALE = 1.0 / math.sqrt(E)
BF = jnp.bfloat16
F32 = jnp.float32
NZ = 8
VMEM_LIMIT = 28 * 1024 * 1024
OFFSETS = (0, -1, 1, -2, 2, -3, 3, 4)


def params():
    return pltpu.CompilerParams(vmem_limit_bytes=VMEM_LIMIT)


def vmem():
    return pl.BlockSpec(memory_space=pltpu.VMEM)


def smem():
    return pl.BlockSpec(memory_space=pltpu.SMEM)


def normed(values, gain):
    scaled = values * lax.rsqrt(jnp.mean(values * values, axis=-1, keepdims=True) + 1e-05)
    return (scaled * gain).astype(BF)


def softmax(scores):
    top = jnp.max(scores, axis=-1, keepdims=True)
    shifted = jnp.exp2((scores - top) * (SCALE * math.log2(math.e)))
    return (shifted * (1.0 / jnp.sum(shifted, axis=-1, keepdims=True))).astype(BF)


def dot(a, b):
    return jnp.dot(a, b, preferred_element_type=F32)


def dot_t(a, b):
    return lax.dot_general(a, b, (((1,), (1,)), ((), ())), preferred_element_type=F32)


def norm_kernel(place_ref, x_ref, gain_ref, qkv_ref, a_ref, b_ref, rows_a_ref, rows_b_ref):
    gain = gain_ref[...]
    half = rows_a_ref.shape[0]
    values = jnp.transpose(x_ref[...].astype(F32), (1, 0, 2)).reshape(2 * half, -1)
    rows_a_ref[...] = values[:half].astype(BF)
    rows_b_ref[...] = values[half:].astype(BF)
    a_ref[:half] = normed(values[:half], gain)
    b_ref[:half] = normed(values[half:], gain)
    b_ref[half:, 1024:] = jnp.zeros((16, 1024), BF)
    for kind in range(3):
        share = qkv_ref[kind]
        ref = (a_ref, b_ref)[kind // 2]
        for group in range(4):
            low = 256 * (4 * (kind % 2) + group)
            ref[half:, low : low + 256] = share[16 * group : 16 * group + 16]


def norm_rows(place, stream, gain, temporal_qkv):
    patches, frames, width = stream.shape
    count = patches * frames
    half = jax.ShapeDtypeStruct((count // 2 + 16, width), BF)
    whole = lambda *shape: pl.BlockSpec(shape, lambda i, at: (0,) * len(shape))
    return pl.pallas_call(
        norm_kernel,
        grid_spec=pltpu.PrefetchScalarGridSpec(
            num_scalar_prefetch=1,
            grid=(1,),
            in_specs=[
                whole(patches, frames, width),
                whole(1, width),
                pl.BlockSpec((3, 64, 256), lambda i, at: (0, at[0], 0)),
            ],
            out_specs=(
                whole(count // 2 + 16, width),
                whole(count // 2 + 16, width),
                whole(count // 2, width),
                whole(count // 2, width),
            ),
        ),
        out_shape=(half, half) + (jax.ShapeDtypeStruct((count // 2, width), BF),) * 2,
        compiler_params=params(),
        cost_estimate=pl.CostEstimate(
            flops=4 * count * width, bytes_accessed=6 * count * width, transcendentals=0
        ),
    )(place, stream, gain, temporal_qkv)


def split_kernel(place_ref, *refs):
    pieces, sends = refs[:-4], refs[-4:]
    z, y = place_ref[0], place_ref[1]
    for k in range(NZ):
        source = lax.rem(z + (OFFSETS[k] + NZ), NZ)
        step = lax.rem(source // 2 + 4 - y, 4)
        pair = lax.rem(source, 2)
        for index, send_ref in enumerate(sends):

            @pl.when(step == index)
            def _():
                for kind in range(3):
                    for group in range(4):
                        low = 256 * (4 * (kind % 2) + group)
                        rows = slice(16 * group, 16 * group + 16)
                        value = pieces[2 * k + kind // 2][:, low : low + 256]
                        send_ref[pair, kind, rows] = value


def split_shares(place, pieces):
    return pl.pallas_call(
        split_kernel,
        grid=(1,),
        out_shape=(jax.ShapeDtypeStruct((2, 3, 64, 256), BF),) * 4,
        in_specs=[smem()] + [pl.BlockSpec((16, 2048), lambda i: (4, 0))] * len(pieces),
        out_specs=(pl.BlockSpec((2, 3, 64, 256), lambda i: (0, 0, 0, 0)),) * 4,
        compiler_params=params(),
        cost_estimate=pl.CostEstimate(flops=0, bytes_accessed=2 << 20, transcendentals=0),
    )(place, *pieces)


def join_kernel(y_ref, *refs):
    out_ref = refs[-1]
    for step in range(4):
        low = pl.multiple_of(64 * lax.rem(y_ref[0] + (4 - step), 4), 64)
        for pair in range(2):
            for kind in range(3):
                out_ref[3 * pair + kind, pl.ds(low, 64), :] = refs[step][pair, kind]


def join_shares(y, got):
    return pl.pallas_call(
        join_kernel,
        out_shape=jax.ShapeDtypeStruct((6, 256, 256), BF),
        in_specs=[smem()] + [vmem()] * 4,
        out_specs=vmem(),
        compiler_params=params(),
        cost_estimate=pl.CostEstimate(flops=0, bytes_accessed=2 << 20, transcendentals=0),
    )(y, *got)


def attend(chains):
    scores = [dot_t(query, key) for query, key, _, _ in chains]
    scores = [
        one if chain[3] is None else jnp.where(chain[3] < 0.0, chain[3], one)
        for one, chain in zip(scores, chains)
    ]
    weights = [softmax(one) for one in scores]
    return [dot(one, chain[2]).astype(BF) for one, chain in zip(weights, chains)]


def spatial_kernel(place_ref, weight_ref, *refs):
    pieces, out_ref, qkv = refs[:NZ], refs[NZ], refs[NZ + 1]
    place = place_ref[0]
    for frame in range(2):
        low = 32 * frame
        rows = jnp.concatenate([piece[low : low + 32, :] for piece in pieces], axis=0)
        for kind in range(3):
            qkv[kind, 256 * frame : 256 * frame + 256] = dot(rows, weight_ref[kind]).astype(BF)
    spots = [(frame, head * E) for frame in range(2) for head in range(2)]
    chains = []
    for frame, low in spots:
        at, cols = slice(256 * frame, 256 * frame + 256), slice(low, low + E)
        chains.append((qkv[0, at, cols], qkv[1, at, cols], qkv[2, at, cols], None))
    for (frame, low), mixed in zip(spots, attend(chains)):
        for k in range(NZ):
            target = lax.rem(place + (OFFSETS[k] + NZ), NZ)
            out_ref[target, 32 * frame : 32 * frame + 32, low : low + E] = mixed[
                32 * k : 32 * k + 32
            ]


def spatial_attend(place, weight, pieces):
    return pl.pallas_call(
        spatial_kernel,
        out_shape=jax.ShapeDtypeStruct((NZ, 64, 256), BF),
        in_specs=[smem(), vmem()] + [vmem()] * len(pieces),
        out_specs=vmem(),
        scratch_shapes=[pltpu.VMEM((3, 512, 256), BF)],
        compiler_params=params(),
        cost_estimate=pl.CostEstimate(
            flops=2 * 1024 * 2048 * 768, bytes_accessed=6 << 20, transcendentals=4 * 65536
        ),
    )(place, weight, *pieces)


def column_block(read):
    return jnp.concatenate([read(head, k // 4, k % 4) for k in range(NZ) for head in range(2)], axis=0)


def join_blocks_kernel(z_ref, *refs):
    out_ref = refs[-1]
    for step in range(4):
        out_ref[lax.rem(z_ref[0] + (4 - step), 4)] = refs[step][...]


def join_blocks(z, parts):
    return pl.pallas_call(
        join_blocks_kernel,
        out_shape=jax.ShapeDtypeStruct((4, 128, 256), BF),
        in_specs=[smem()] + [vmem()] * 4,
        out_specs=vmem(),
        compiler_params=params(),
        cost_estimate=pl.CostEstimate(flops=0, bytes_accessed=512 << 10, transcendentals=0),
    )(z, *parts)


def middle_kernel(mix_ref, weight_ref, rows_ref, gain_ref, middle_ref, send_ref, total):
    mix = jnp.concatenate([mix_ref[k] for k in range(NZ)], axis=1)
    for block in range(8):
        part = column_block(lambda *at: weight_ref[(block, *at)])
        total[:, 256 * block : 256 * block + 256] = dot(mix, part)
    middle = (total[...] + rows_ref[...].astype(F32)).astype(BF)
    middle_ref[...] = middle
    values = middle.astype(F32)
    scaled = values * lax.rsqrt(jnp.mean(values * values, axis=-1, keepdims=True) + 1e-05)
    scaled = scaled * gain_ref[...]
    for group in range(4):
        chunk = jnp.concatenate(
            [scaled[32 * f + 8 * group : 32 * f + 8 * group + 8] for f in range(2)], axis=0
        ).astype(BF)
        for y in range(4):
            send_ref[(group // 2) * 8 + y * 2 + group % 2] = chunk


def middle_rows(mix, weight, rows, gain):
    count, width = rows.shape
    return pl.pallas_call(
        middle_kernel,
        out_shape=(
            jax.ShapeDtypeStruct((count, width), BF),
            jax.ShapeDtypeStruct((16, count // 4, width), BF),
        ),
        in_specs=[vmem()] * 4,
        out_specs=(vmem(), vmem()),
        scratch_shapes=[pltpu.VMEM((count, width), F32)],
        compiler_params=params(),
        cost_estimate=pl.CostEstimate(
            flops=2 * 64 * 2048 * 2048, bytes_accessed=10 << 20, transcendentals=0
        ),
    )(mix, weight, rows, gain)


def temporal_kernel(start_ref, first_ref, second_ref, weight_ref, out_ref, rows, qkv, bias):
    count = rows.shape[0]
    for spot in range(16):
        rows[32 * spot : 32 * spot + 16] = first_ref[spot]
        rows[32 * spot + 16 : 32 * spot + 32] = second_ref[spot]
    start = start_ref[0]
    late = lax.broadcasted_iota(jnp.int32, (count, count), 0)
    early = lax.broadcasted_iota(jnp.int32, (count, count), 1)
    same = (late & 7) == (early & 7)
    allowed = same & (early <= late) & ((early >= 8 * start) == (late >= 8 * start))
    bias[...] = jnp.where(allowed, 0.0, -1e30)
    for block in range(6):
        qkv[block] = dot(rows[...], weight_ref[:, block].reshape(2048, 256)).astype(BF)
    size = 256
    for pair in range(2):
        for low in range(0, count, size):
            chains = []
            high = low + size
            for head in range(2):
                cols = slice(head * E, head * E + E)
                chains.append(
                    (
                        qkv[3 * pair, low:high, cols],
                        qkv[3 * pair + 1, :high, cols],
                        qkv[3 * pair + 2, :high, cols],
                        bias[low:high, :high],
                    )
                )
            for head, mixed in enumerate(attend(chains)):
                for spot in range(low // 32, high // 32):
                    rows = mixed[32 * spot - low : 32 * spot - low + 32]
                    at = (spot // 2 * 2 + head, spot % 2, slice(None), slice(E * pair, E * pair + E))
                    out_ref[at] = rows


def temporal_attend(start, first, second, weight):
    count, width = 2 * 16 * first.shape[1], first.shape[2]
    return pl.pallas_call(
        temporal_kernel,
        out_shape=jax.ShapeDtypeStruct((16, 2, 32, 256), BF),
        in_specs=[smem(), vmem(), vmem(), vmem()],
        out_specs=vmem(),
        scratch_shapes=[
            pltpu.VMEM((count, width), BF),
            pltpu.VMEM((6, count, 256), BF),
            pltpu.VMEM((count, count), F32),
        ],
        compiler_params=params(),
        cost_estimate=pl.CostEstimate(
            flops=2 * 512 * 2048 * 1536, bytes_accessed=9 << 20, transcendentals=131072
        ),
    )(start, first, second, weight)


def last_kernel(place_ref, mix_ref, *refs):
    pieces, (keep_ref, give_ref, total) = refs[: NZ + 1], refs[NZ + 1 :]
    z, c = place_ref[0], place_ref[1]
    blocks = []
    for k in range(NZ):
        source = lax.rem(z + (OFFSETS[k] + NZ), NZ)
        cols = pl.ds(pl.multiple_of(lax.rem(source, 2) * E, E), E)
        blocks.append(
            jnp.concatenate(
                [
                    mix_ref[xl * 8 + source // 2 * 2 + core, frames, :, cols]
                    for frames in range(2)
                    for xl in range(2)
                    for core in range(2)
                ],
                axis=0,
            )
        )
    mix = jnp.concatenate(blocks, axis=1)
    for low in range(0, 2048, 512):
        part = jnp.concatenate([piece[:, low : low + 512] for piece in pieces], axis=0)
        total[:, :, low : low + 512] = dot(mix, part).reshape(2, 128, 512)
    keep_ref[...] = total[c]
    give_ref[...] = total[1 - c].astype(BF)


def last_sums(place, mix, pieces):
    width = pieces[0].shape[1]
    return pl.pallas_call(
        last_kernel,
        out_shape=(
            jax.ShapeDtypeStruct((128, width), F32),
            jax.ShapeDtypeStruct((128, width), BF),
        ),
        in_specs=[smem()] + [vmem()] * (NZ + 2),
        out_specs=(vmem(), vmem()),
        scratch_shapes=[pltpu.VMEM((2, 128, width), F32)],
        compiler_params=params(),
        cost_estimate=pl.CostEstimate(
            flops=2 * 128 * 2048 * 2048, bytes_accessed=8 << 20, transcendentals=0
        ),
    )(place, mix, *pieces)


def end_kernel(keep_ref, got_ref, first_ref, second_ref, out_ref):
    for group in range(4):
        at = slice(32 * group, 32 * group + 32)
        rows = (keep_ref[at] + got_ref[at].astype(F32)).reshape(4, 8, -1)
        middle = jnp.stack(
            [
                ref[32 * f : 32 * f + 32].astype(F32)[8 * group : 8 * group + 8]
                for ref in (first_ref, second_ref)
                for f in range(2)
            ],
            axis=0,
        )
        out = jnp.transpose(rows + middle, (1, 0, 2)).astype(BF)
        out_ref[8 * group : 8 * group + 8] = out


def end_rows(keep, got, first, second):
    return pl.pallas_call(
        end_kernel,
        out_shape=jax.ShapeDtypeStruct((32, 4, first.shape[1]), BF),
        in_specs=[vmem()] * 4,
        out_specs=vmem(),
        compiler_params=params(),
        cost_estimate=pl.CostEstimate(flops=1 << 20, bytes_accessed=3 << 20, transcendentals=0),
    )(keep, got, first, second)


def shifted(value, axis, step):
    count = lax.axis_size(axis)
    return lax.ppermute(value, axis, [(i, (i + step) % count) for i in range(count)])


def gathered_rows(chunks):
    up, down = list(chunks), list(chunks)
    pieces = {0: list(chunks)}
    for step in (1, 2, 3):
        up = [shifted(value, "z", 1) for value in up]
        down = [shifted(value, "z", -1) for value in down]
        pieces[-step], pieces[step] = up, down
    pieces[4] = [shifted(up[0], "z", 1), shifted(down[1], "z", -1)]
    return [value for offset in OFFSETS for value in pieces[offset]]


def local(stream, spatial_gain, spatial_qkv, spatial_out, temporal_gain, temporal_qkv, temporal_out, starts):
    patches, frames, width = stream.shape
    w, xl, y, c, z = (lax.axis_index(name) for name in ("w", "xl", "y", "c", "z"))

    place = (((w * 2 + xl) * 2 + c) * 4 + y).reshape(1)
    first, second, *rows = norm_rows(
        place, stream, spatial_gain.reshape(1, width), jnp.transpose(temporal_qkv, (1, 0, 2))
    )

    low = (lax.rem(y, 2) * E, ((w * 2 + xl) * 2 + y // 2) * 256)
    block = lax.dynamic_slice(spatial_out, low, (E, 256))
    parts = []
    for k in range(4):
        pairs = [
            (a * 8 + b, (b // 4) * 8 + (b + 4 * a + k) % 8) for a in range(2) for b in range(8)
        ]
        parts.append(lax.ppermute(block, ("c", "z"), pairs))
    first, second, parts = lax.optimization_barrier((first, second, parts))
    whole_out = join_blocks(z.reshape(1), parts)
    whole_out = lax.all_gather(whole_out, ("w", "xl", "y", "c"), axis=0, tiled=False)
    whole_out = whole_out.reshape(8, 2, 2, 4, E, 256)

    pieces = gathered_rows((first, second))

    sends = split_shares(jnp.stack([z, y]).astype(jnp.int32), pieces)
    got = [sends[0]] + [shifted(sends[k], "y", k) for k in range(1, 4)]

    weight = jnp.transpose(spatial_qkv, (1, 0, 2))
    mixes = [spatial_attend(z.reshape(1), weight, pieces[0::2])]
    mixes[0], later = lax.optimization_barrier((mixes[0], pieces[1::2]))
    mixes.append(spatial_attend(z.reshape(1), weight, later))
    mixes[1], got = lax.optimization_barrier((mixes[1], got))
    quarter = join_shares(y.reshape(1), got)
    mixes[1], quarter = lax.optimization_barrier((mixes[1], quarter))
    quarter = lax.all_gather(quarter[None], ("w", "xl", "c"), axis=0, tiled=True)

    gain = temporal_gain.reshape(1, width)
    half = lax.dynamic_slice(temporal_out, (c * E, 0), (E, width))
    middles, sends, windows = [], [], []
    for part in range(2):
        mix = lax.all_to_all(mixes[part], "z", 0, 0, tiled=True)
        if part == 1:
            mix, half, _ = lax.optimization_barrier((mix, half, sends[0]))
        middle, send = middle_rows(mix, whole_out, rows[part], gain)
        middles.append(middle)
        sends.append(send)
        windows.append(lax.all_to_all(send, ("xl", "y", "c"), 0, 0, tiled=True))

    up, down = half, half
    halves = [half]
    for step in (1, 2, 3):
        up, down = shifted(up, "z", 1), shifted(down, "z", -1)
        if step == 1:
            up, down, _ = lax.optimization_barrier((up, down, sends[1]))
        if step == 2:
            up, down, quarter = lax.optimization_barrier((up, down, quarter))
        halves += [up, down]
    halves += [shifted(up[:64], "z", 1), shifted(down[64:], "z", -1)]

    windows, halves[1:3] = lax.optimization_barrier((windows, halves[1:3]))
    start = lax.dynamic_slice(starts, (w,), (1,))
    mix = temporal_attend(start, *windows, quarter)
    mix = lax.all_to_all(mix, ("xl", "y", "c"), 0, 0, tiled=True)
    keep, give = last_sums(jnp.stack([z, c]).astype(jnp.int32), mix, halves)
    return end_rows(keep, shifted(give, "c", 1), *middles)


def solution(mesh):
    names = ("w", "xl", "y", "c", "z")
    fine = Mesh(mesh.devices.reshape(2, 2, 4, 2, NZ), names)
    tm = ("w", "xl", "y", "c")
    placed = (
        P("z", tm, None),
        P(),
        P(None, None, "z"),
        P("z", None),
        P(),
        P(None, None, "z"),
        P("z", None),
        P(),
    )
    return jax.shard_map(
        local, mesh=fine, in_specs=placed, out_specs=P("z", tm, None), check_vma=False
    )
```

```python
import functools
import math

import jax
import jax.numpy as jnp
from jax import lax
from jax.experimental import pallas as pl
from jax.experimental.pallas import tpu as pltpu
from jax.sharding import Mesh
from jax.sharding import PartitionSpec as P

E = 128
SEQ = 64
SCALE = 1.0 / math.sqrt(E)
BF = jnp.bfloat16
F32 = jnp.float32
NZ = 8
VMEM_LIMIT = 28 * 1024 * 1024
OFFSETS = (0, -1, 1, -2, 2, -3, 3, 4)


def params():
    return pltpu.CompilerParams(vmem_limit_bytes=VMEM_LIMIT)


def vmem():
    return pl.BlockSpec(memory_space=pltpu.VMEM)


def smem():
    return pl.BlockSpec(memory_space=pltpu.SMEM)


def normed(values, gain):
    scaled = values * lax.rsqrt(jnp.mean(values * values, axis=-1, keepdims=True) + 1e-05)
    return (scaled * gain).astype(BF)


def softmax(scores):
    top = jnp.max(scores, axis=-1, keepdims=True)
    shifted = jnp.exp2((scores - top) * (SCALE * math.log2(math.e)))
    return (shifted * (1.0 / jnp.sum(shifted, axis=-1, keepdims=True))).astype(BF)


def dot(a, b):
    return jnp.dot(a, b, preferred_element_type=F32)


def dot_t(a, b):
    return lax.dot_general(a, b, (((1,), (1,)), ((), ())), preferred_element_type=F32)


def norm_kernel(place_ref, x_ref, gain_ref, qkv_ref, a_ref, b_ref, rows_ref):
    gain = gain_ref[...]
    values = jnp.transpose(x_ref[...].astype(F32), (1, 0, 2)).reshape(rows_ref.shape)
    half = rows_ref.shape[0] // 2
    rows_ref[...] = values.astype(BF)
    a_ref[:half] = normed(values[:half], gain)
    b_ref[:half] = normed(values[half:], gain)
    b_ref[half:, 1024:] = jnp.zeros((16, 1024), BF)
    for kind in range(3):
        share = qkv_ref[kind]
        ref = (a_ref, b_ref)[kind // 2]
        for group in range(4):
            low = 256 * (4 * (kind % 2) + group)
            ref[half:, low : low + 256] = share[16 * group : 16 * group + 16]


def norm_rows(place, stream, gain, temporal_qkv):
    patches, frames, width = stream.shape
    count = patches * frames
    half = jax.ShapeDtypeStruct((count // 2 + 16, width), BF)
    whole = lambda *shape: pl.BlockSpec(shape, lambda i, at: (0,) * len(shape))
    return pl.pallas_call(
        norm_kernel,
        grid_spec=pltpu.PrefetchScalarGridSpec(
            num_scalar_prefetch=1,
            grid=(1,),
            in_specs=[
                whole(patches, frames, width),
                whole(1, width),
                pl.BlockSpec((3, 64, 256), lambda i, at: (0, at[0], 0)),
            ],
            out_specs=(
                whole(count // 2 + 16, width),
                whole(count // 2 + 16, width),
                whole(count, width),
            ),
        ),
        out_shape=(half, half, jax.ShapeDtypeStruct((count, width), BF)),
        compiler_params=params(),
        cost_estimate=pl.CostEstimate(
            flops=4 * count * width, bytes_accessed=6 * count * width, transcendentals=0
        ),
    )(place, stream, gain, temporal_qkv)


def split_kernel(place_ref, *refs):
    pieces, sends = refs[:-4], refs[-4:]
    z, y = place_ref[0], place_ref[1]
    for k in range(NZ):
        source = lax.rem(z + (OFFSETS[k] + NZ), NZ)
        step = lax.rem(source // 2 + 4 - y, 4)
        pair = lax.rem(source, 2)
        for index, send_ref in enumerate(sends):

            @pl.when(step == index)
            def _():
                for kind in range(3):
                    for group in range(4):
                        low = 256 * (4 * (kind % 2) + group)
                        rows = slice(16 * group, 16 * group + 16)
                        value = pieces[2 * k + kind // 2][:, low : low + 256]
                        send_ref[pair, kind, rows] = value


def split_shares(place, pieces):
    return pl.pallas_call(
        split_kernel,
        grid=(1,),
        out_shape=(jax.ShapeDtypeStruct((2, 3, 64, 256), BF),) * 4,
        in_specs=[smem()] + [pl.BlockSpec((16, 2048), lambda i: (4, 0))] * len(pieces),
        out_specs=(pl.BlockSpec((2, 3, 64, 256), lambda i: (0, 0, 0, 0)),) * 4,
        compiler_params=params(),
        cost_estimate=pl.CostEstimate(flops=0, bytes_accessed=2 << 20, transcendentals=0),
    )(place, *pieces)


def join_kernel(y_ref, *refs):
    out_ref = refs[-1]
    for step in range(4):
        low = pl.multiple_of(64 * lax.rem(y_ref[0] + (4 - step), 4), 64)
        for pair in range(2):
            for kind in range(3):
                out_ref[3 * pair + kind, pl.ds(low, 64), :] = refs[step][pair, kind]


def join_shares(y, got):
    return pl.pallas_call(
        join_kernel,
        out_shape=jax.ShapeDtypeStruct((6, 256, 256), BF),
        in_specs=[smem()] + [vmem()] * 4,
        out_specs=vmem(),
        compiler_params=params(),
        cost_estimate=pl.CostEstimate(flops=0, bytes_accessed=2 << 20, transcendentals=0),
    )(y, *got)


def attend(chains):
    scores = [dot_t(query, key) for query, key, _, _ in chains]
    scores = [
        one if chain[3] is None else jnp.where(chain[3] < 0.0, chain[3], one)
        for one, chain in zip(scores, chains)
    ]
    weights = [softmax(one) for one in scores]
    return [dot(one, chain[2]).astype(BF) for one, chain in zip(weights, chains)]


def spatial_kernel(place_ref, weight_ref, *refs):
    pieces, out_ref, qkv = refs[: 2 * NZ], refs[2 * NZ], refs[2 * NZ + 1]
    place = place_ref[0]
    for frame in range(4):
        low = 32 * (frame % 2)
        rows = jnp.concatenate(
            [pieces[2 * k + frame // 2][low : low + 32, :] for k in range(NZ)], axis=0
        )
        for kind in range(3):
            qkv[kind, 256 * frame : 256 * frame + 256] = dot(rows, weight_ref[kind]).astype(BF)
    for frames in ((0, 1), (2, 3)):
        spots = [(frame, head * E) for frame in frames for head in range(2)]
        chains = []
        for frame, low in spots:
            at, cols = slice(256 * frame, 256 * frame + 256), slice(low, low + E)
            chains.append((qkv[0, at, cols], qkv[1, at, cols], qkv[2, at, cols], None))
        for (frame, low), mixed in zip(spots, attend(chains)):
            for k in range(NZ):
                target = lax.rem(place + (OFFSETS[k] + NZ), NZ)
                out_ref[target, 32 * frame : 32 * frame + 32, low : low + E] = mixed[
                    32 * k : 32 * k + 32
                ]


def spatial_attend(place, weight, pieces):
    return pl.pallas_call(
        spatial_kernel,
        out_shape=jax.ShapeDtypeStruct((NZ, 128, 256), BF),
        in_specs=[smem(), vmem()] + [vmem()] * len(pieces),
        out_specs=vmem(),
        scratch_shapes=[pltpu.VMEM((3, 1024, 256), BF)],
        compiler_params=params(),
        cost_estimate=pl.CostEstimate(
            flops=2 * 1024 * 2048 * 768 * 2, bytes_accessed=8 << 20, transcendentals=8 * 65536
        ),
    )(place, weight, *pieces)


def column_block(weight_ref, block):
    return jnp.concatenate(
        [weight_ref[block, quarter, k] for k in range(NZ) for quarter in range(4)], axis=0
    )


def middle_kernel(mix_ref, weight_ref, rows_ref, gain_ref, middle_ref, send_ref, total):
    mix = jnp.concatenate([mix_ref[k] for k in range(NZ)], axis=1)
    for block in range(8):
        total[:, 256 * block : 256 * block + 256] = dot(mix, column_block(weight_ref, block))
    middle = (total[...] + rows_ref[...].astype(F32)).astype(BF)
    middle_ref[...] = middle
    values = middle.astype(F32)
    scaled = values * lax.rsqrt(jnp.mean(values * values, axis=-1, keepdims=True) + 1e-05)
    scaled = scaled * gain_ref[...]
    for group in range(4):
        chunk = jnp.concatenate(
            [scaled[32 * f + 8 * group : 32 * f + 8 * group + 8] for f in range(4)], axis=0
        ).astype(BF)
        for y in range(4):
            send_ref[(group // 2) * 8 + y * 2 + group % 2] = chunk


def middle_rows(mix, weight, rows, gain):
    width = rows.shape[1]
    return pl.pallas_call(
        middle_kernel,
        out_shape=(
            jax.ShapeDtypeStruct((128, width), BF),
            jax.ShapeDtypeStruct((16, 32, width), BF),
        ),
        in_specs=[vmem()] * 4,
        out_specs=(vmem(), vmem()),
        scratch_shapes=[pltpu.VMEM((128, width), F32)],
        compiler_params=params(),
        cost_estimate=pl.CostEstimate(
            flops=2 * 128 * 2048 * 2048, bytes_accessed=12 << 20, transcendentals=0
        ),
    )(mix, weight, rows, gain)


def temporal_kernel(start_ref, rows_ref, weight_ref, out_ref, qkv, bias):
    count = rows_ref.shape[0]
    start = start_ref[0]
    late = lax.broadcasted_iota(jnp.int32, (count, count), 0)
    early = lax.broadcasted_iota(jnp.int32, (count, count), 1)
    same = (late & 7) == (early & 7)
    allowed = same & (early <= late) & ((early >= 8 * start) == (late >= 8 * start))
    bias[...] = jnp.where(allowed, 0.0, -1e30)
    for block in range(6):
        qkv[block] = dot(rows_ref[...], weight_ref[:, block].reshape(2048, 256)).astype(BF)
    size = 256
    for pair in range(2):
        for low in range(0, count, size):
            chains = []
            high = low + size
            for head in range(2):
                cols = slice(head * E, head * E + E)
                chains.append(
                    (
                        qkv[3 * pair, low:high, cols],
                        qkv[3 * pair + 1, :high, cols],
                        qkv[3 * pair + 2, :high, cols],
                        bias[low:high, :high],
                    )
                )
            for head, mixed in enumerate(attend(chains)):
                for spot in range(low // 32, high // 32):
                    rows = mixed[32 * spot - low : 32 * spot - low + 32]
                    at = (spot // 2 * 2 + head, spot % 2, slice(None), slice(E * pair, E * pair + E))
                    out_ref[at] = rows


def temporal_attend(start, rows, weight):
    count, width = rows.shape
    return pl.pallas_call(
        temporal_kernel,
        out_shape=jax.ShapeDtypeStruct((16, 2, 32, 256), BF),
        in_specs=[smem(), vmem(), vmem()],
        out_specs=vmem(),
        scratch_shapes=[
            pltpu.VMEM((6, count, 256), BF),
            pltpu.VMEM((count, count), F32),
        ],
        compiler_params=params(),
        cost_estimate=pl.CostEstimate(
            flops=2 * 512 * 2048 * 1536, bytes_accessed=9 << 20, transcendentals=131072
        ),
    )(start, rows, weight)


def last_kernel(place_ref, mix_ref, *refs):
    pieces, (keep_ref, give_ref, total) = refs[: 2 * NZ], refs[2 * NZ :]
    z, c = place_ref[0], place_ref[1]
    blocks = []
    for k in range(NZ):
        source = lax.rem(z + (OFFSETS[k] + NZ), NZ)
        cols = pl.ds(pl.multiple_of(lax.rem(source, 2) * E, E), E)
        blocks.append(
            jnp.concatenate(
                [
                    mix_ref[xl * 8 + source // 2 * 2 + core, frames, :, cols]
                    for frames in range(2)
                    for xl in range(2)
                    for core in range(2)
                ],
                axis=0,
            )
        )
    mix = jnp.concatenate(blocks, axis=1)
    for low in range(0, 2048, 512):
        part = jnp.concatenate([piece[:, low : low + 512] for piece in pieces], axis=0)
        total[:, :, low : low + 512] = dot(mix, part).reshape(2, 128, 512)
    keep_ref[...] = total[c]
    give_ref[...] = total[1 - c].astype(BF)


def last_sums(place, mix, pieces):
    width = pieces[0].shape[1]
    return pl.pallas_call(
        last_kernel,
        out_shape=(
            jax.ShapeDtypeStruct((128, width), F32),
            jax.ShapeDtypeStruct((128, width), BF),
        ),
        in_specs=[smem()] + [vmem()] * (2 * NZ + 1),
        out_specs=(vmem(), vmem()),
        scratch_shapes=[pltpu.VMEM((2, 128, width), F32)],
        compiler_params=params(),
        cost_estimate=pl.CostEstimate(
            flops=2 * 128 * 2048 * 2048, bytes_accessed=8 << 20, transcendentals=0
        ),
    )(place, mix, *pieces)


def end_kernel(keep_ref, got_ref, middle_ref, out_ref):
    for group in range(4):
        at = slice(32 * group, 32 * group + 32)
        rows = (keep_ref[at] + got_ref[at].astype(F32)).reshape(4, 8, -1)
        middle = jnp.stack(
            [
                middle_ref[32 * f : 32 * f + 32].astype(F32)[8 * group : 8 * group + 8]
                for f in range(4)
            ],
            axis=0,
        )
        out = jnp.transpose(rows + middle, (1, 0, 2)).astype(BF)
        out_ref[8 * group : 8 * group + 8] = out


def end_rows(keep, got, middle):
    return pl.pallas_call(
        end_kernel,
        out_shape=jax.ShapeDtypeStruct((32, 4, middle.shape[1]), BF),
        in_specs=[vmem()] * 3,
        out_specs=vmem(),
        compiler_params=params(),
        cost_estimate=pl.CostEstimate(flops=1 << 20, bytes_accessed=3 << 20, transcendentals=0),
    )(keep, got, middle)


def shifted(value, axis, step):
    count = lax.axis_size(axis)
    return lax.ppermute(value, axis, [(i, (i + step) % count) for i in range(count)])


def gathered_rows(chunks):
    up, down = list(chunks), list(chunks)
    pieces = {0: list(chunks)}
    for step in (1, 2, 3):
        up = [shifted(value, "z", 1) for value in up]
        down = [shifted(value, "z", -1) for value in down]
        pieces[-step], pieces[step] = up, down
    pieces[4] = [shifted(up[0], "z", 1), shifted(down[1], "z", -1)]
    return [value for offset in OFFSETS for value in pieces[offset]]


def local(stream, spatial_gain, spatial_qkv, spatial_out, temporal_gain, temporal_qkv, temporal_out, starts):
    patches, frames, width = stream.shape
    w, xl, y, c, z = (lax.axis_index(name) for name in ("w", "xl", "y", "c", "z"))

    place = (((w * 2 + xl) * 2 + c) * 4 + y).reshape(1)
    first, second, rows = norm_rows(
        place, stream, spatial_gain.reshape(1, width), jnp.transpose(temporal_qkv, (1, 0, 2))
    )

    low = ((lax.rem(y, 2) * 2 + c) * 64, ((w * 2 + xl) * 2 + y // 2) * 256)
    block = lax.dynamic_slice(spatial_out, low, (64, 256))
    whole_out = lax.all_to_all(jnp.broadcast_to(block, (NZ, 64, 256)), "z", 0, 0, tiled=True)
    first, second, whole_out = lax.optimization_barrier((first, second, whole_out))
    whole_out = lax.all_gather(whole_out, ("w", "xl", "y", "c"), axis=0, tiled=False)
    whole_out = whole_out.reshape(8, 4, NZ, 64, 256)

    pieces = gathered_rows((first, second))

    sends = split_shares(jnp.stack([z, y]).astype(jnp.int32), pieces)
    got = [sends[0]] + [shifted(sends[k], "y", k) for k in range(1, 4)]

    weight = jnp.transpose(spatial_qkv, (1, 0, 2))
    mix = spatial_attend(z.reshape(1), weight, pieces)
    mix, *got = lax.optimization_barrier((mix, *got))
    quarter = join_shares(y.reshape(1), got)
    mix, quarter = lax.optimization_barrier((mix, quarter))
    quarter = lax.all_gather(quarter[None], ("w", "xl", "c"), axis=0, tiled=True)
    mix = lax.all_to_all(mix, "z", 0, 0, tiled=True)
    middle, send = middle_rows(mix, whole_out, rows, temporal_gain.reshape(1, width))

    half = lax.dynamic_slice(temporal_out, (c * E, 0), (E, width))
    send, half = lax.optimization_barrier((send, half))
    halves = gathered_rows((half[:64], half[64:]))

    window = lax.all_to_all(send, ("xl", "y", "c"), 0, 0, tiled=True)
    window, *halves[2:6] = lax.optimization_barrier((window, *halves[2:6]))
    start = lax.dynamic_slice(starts, (w,), (1,))
    mix = temporal_attend(start, window.reshape(512, width), quarter)
    mix = lax.all_to_all(mix, ("xl", "y", "c"), 0, 0, tiled=True)
    keep, give = last_sums(jnp.stack([z, c]).astype(jnp.int32), mix, halves)
    return end_rows(keep, shifted(give, "c", 1), middle)


def solution(mesh):
    names = ("w", "xl", "y", "c", "z")
    fine = Mesh(mesh.devices.reshape(2, 2, 4, 2, NZ), names)
    tm = ("w", "xl", "y", "c")
    placed = (
        P("z", tm, None),
        P(),
        P(None, None, "z"),
        P("z", None),
        P(),
        P(None, None, "z"),
        P("z", None),
        P(),
    )
    return jax.shard_map(
        local, mesh=fine, in_specs=placed, out_specs=P("z", tm, None), check_vma=False
    )
```

```python
import functools
import math

import jax
import jax.numpy as jnp
from jax import lax
from jax.experimental import pallas as pl
from jax.experimental.pallas import tpu as pltpu
from jax.sharding import Mesh
from jax.sharding import PartitionSpec as P

E = 128
SEQ = 64
SCALE = 1.0 / math.sqrt(E)
BF = jnp.bfloat16
F32 = jnp.float32
NZ = 8
VMEM_LIMIT = 28 * 1024 * 1024
OFFSETS = (0, -1, 1, -2, 2, -3, 3, 4)


def params():
    return pltpu.CompilerParams(vmem_limit_bytes=VMEM_LIMIT)


def vmem():
    return pl.BlockSpec(memory_space=pltpu.VMEM)


def smem():
    return pl.BlockSpec(memory_space=pltpu.SMEM)


def normed(values, gain):
    scaled = values * lax.rsqrt(jnp.mean(values * values, axis=-1, keepdims=True) + 1e-05)
    return (scaled * gain).astype(BF)


def softmax(scores):
    top = jnp.max(scores, axis=-1, keepdims=True)
    shifted = jnp.exp2((scores - top) * (SCALE * math.log2(math.e)))
    return (shifted * (1.0 / jnp.sum(shifted, axis=-1, keepdims=True))).astype(BF)


def dot(a, b):
    return jnp.dot(a, b, preferred_element_type=F32)


def dot_t(a, b):
    return lax.dot_general(a, b, (((1,), (1,)), ((), ())), preferred_element_type=F32)


def norm_kernel(place_ref, x_ref, gain_ref, qkv_ref, a_ref, b_ref, rows_ref):
    gain = gain_ref[...]
    values = jnp.transpose(x_ref[...].astype(F32), (1, 0, 2)).reshape(rows_ref.shape)
    half = rows_ref.shape[0] // 2
    rows_ref[...] = values.astype(BF)
    a_ref[:half] = normed(values[:half], gain)
    b_ref[:half] = normed(values[half:], gain)
    b_ref[half:, 1024:] = jnp.zeros((16, 1024), BF)
    for kind in range(3):
        share = qkv_ref[kind]
        ref = (a_ref, b_ref)[kind // 2]
        for group in range(4):
            low = 256 * (4 * (kind % 2) + group)
            ref[half:, low : low + 256] = share[16 * group : 16 * group + 16]


def norm_rows(place, stream, gain, temporal_qkv):
    patches, frames, width = stream.shape
    count = patches * frames
    half = jax.ShapeDtypeStruct((count // 2 + 16, width), BF)
    whole = lambda *shape: pl.BlockSpec(shape, lambda i, at: (0,) * len(shape))
    return pl.pallas_call(
        norm_kernel,
        grid_spec=pltpu.PrefetchScalarGridSpec(
            num_scalar_prefetch=1,
            grid=(1,),
            in_specs=[
                whole(patches, frames, width),
                whole(1, width),
                pl.BlockSpec((3, 64, 256), lambda i, at: (0, at[0], 0)),
            ],
            out_specs=(
                whole(count // 2 + 16, width),
                whole(count // 2 + 16, width),
                whole(count, width),
            ),
        ),
        out_shape=(half, half, jax.ShapeDtypeStruct((count, width), BF)),
        compiler_params=params(),
        cost_estimate=pl.CostEstimate(
            flops=4 * count * width, bytes_accessed=6 * count * width, transcendentals=0
        ),
    )(place, stream, gain, temporal_qkv)


def split_kernel(place_ref, *refs):
    pieces, sends = refs[:-4], refs[-4:]
    z, y = place_ref[0], place_ref[1]
    for k in range(NZ):
        source = lax.rem(z + (OFFSETS[k] + NZ), NZ)
        step = lax.rem(source // 2 + 4 - y, 4)
        pair = lax.rem(source, 2)
        for index, send_ref in enumerate(sends):

            @pl.when(step == index)
            def _():
                for kind in range(3):
                    for group in range(4):
                        low = 256 * (4 * (kind % 2) + group)
                        rows = slice(16 * group, 16 * group + 16)
                        value = pieces[2 * k + kind // 2][:, low : low + 256]
                        send_ref[pair, kind, rows] = value


def split_shares(place, pieces):
    return pl.pallas_call(
        split_kernel,
        grid=(1,),
        out_shape=(jax.ShapeDtypeStruct((2, 3, 64, 256), BF),) * 4,
        in_specs=[smem()] + [pl.BlockSpec((16, 2048), lambda i: (4, 0))] * len(pieces),
        out_specs=(pl.BlockSpec((2, 3, 64, 256), lambda i: (0, 0, 0, 0)),) * 4,
        compiler_params=params(),
        cost_estimate=pl.CostEstimate(flops=0, bytes_accessed=2 << 20, transcendentals=0),
    )(place, *pieces)


def join_kernel(y_ref, *refs):
    out_ref = refs[-1]
    for step in range(4):
        low = pl.multiple_of(64 * lax.rem(y_ref[0] + (4 - step), 4), 64)
        for pair in range(2):
            for kind in range(3):
                out_ref[3 * pair + kind, pl.ds(low, 64), :] = refs[step][pair, kind]


def join_shares(y, got):
    return pl.pallas_call(
        join_kernel,
        out_shape=jax.ShapeDtypeStruct((6, 256, 256), BF),
        in_specs=[smem()] + [vmem()] * 4,
        out_specs=vmem(),
        compiler_params=params(),
        cost_estimate=pl.CostEstimate(flops=0, bytes_accessed=2 << 20, transcendentals=0),
    )(y, *got)


def attend(chains):
    scores = [dot_t(query, key) for query, key, _, _ in chains]
    scores = [
        one if chain[3] is None else jnp.where(chain[3] < 0.0, chain[3], one)
        for one, chain in zip(scores, chains)
    ]
    weights = [softmax(one) for one in scores]
    return [dot(one, chain[2]).astype(BF) for one, chain in zip(weights, chains)]


def spatial_kernel(place_ref, weight_ref, *refs):
    pieces, out_ref, qkv = refs[: 2 * NZ], refs[2 * NZ], refs[2 * NZ + 1]
    place = place_ref[0]
    for frame in range(4):
        low = 32 * (frame % 2)
        rows = jnp.concatenate(
            [pieces[2 * k + frame // 2][low : low + 32, :] for k in range(NZ)], axis=0
        )
        for kind in range(3):
            qkv[kind, 256 * frame : 256 * frame + 256] = dot(rows, weight_ref[kind]).astype(BF)
    for frames in ((0, 1), (2, 3)):
        spots = [(frame, head * E) for frame in frames for head in range(2)]
        chains = []
        for frame, low in spots:
            at, cols = slice(256 * frame, 256 * frame + 256), slice(low, low + E)
            chains.append((qkv[0, at, cols], qkv[1, at, cols], qkv[2, at, cols], None))
        for (frame, low), mixed in zip(spots, attend(chains)):
            for k in range(NZ):
                target = lax.rem(place + (OFFSETS[k] + NZ), NZ)
                out_ref[target, 32 * frame : 32 * frame + 32, low : low + E] = mixed[
                    32 * k : 32 * k + 32
                ]


def spatial_attend(place, weight, pieces):
    return pl.pallas_call(
        spatial_kernel,
        out_shape=jax.ShapeDtypeStruct((NZ, 128, 256), BF),
        in_specs=[smem(), vmem()] + [vmem()] * len(pieces),
        out_specs=vmem(),
        scratch_shapes=[pltpu.VMEM((3, 1024, 256), BF)],
        compiler_params=params(),
        cost_estimate=pl.CostEstimate(
            flops=2 * 1024 * 2048 * 768 * 2, bytes_accessed=8 << 20, transcendentals=8 * 65536
        ),
    )(place, weight, *pieces)


def column_block(weight_ref, block):
    return jnp.concatenate(
        [weight_ref[block, quarter, k] for k in range(NZ) for quarter in range(4)], axis=0
    )


def middle_kernel(mix_ref, weight_ref, rows_ref, gain_ref, middle_out, send_out, total, middle_ref, send_ref, sems):
    mix = jnp.concatenate([mix_ref[k] for k in range(NZ)], axis=1)
    for block in range(8):
        total[:, 256 * block : 256 * block + 256] = dot(mix, column_block(weight_ref, block))
    middle = (total[...] + rows_ref[...].astype(F32)).astype(BF)
    middle_ref[...] = middle
    copies = [pltpu.make_async_copy(middle_ref, middle_out, sems.at[16])]
    copies[0].start()
    values = middle.astype(F32)
    scaled = values * lax.rsqrt(jnp.mean(values * values, axis=-1, keepdims=True) + 1e-05)
    scaled = scaled * gain_ref[...]
    for group in range(4):
        chunk = jnp.concatenate(
            [scaled[32 * f + 8 * group : 32 * f + 8 * group + 8] for f in range(4)], axis=0
        ).astype(BF)
        send_ref[group] = chunk
        for y in range(4):
            at = (group // 2) * 8 + y * 2 + group % 2
            copies.append(pltpu.make_async_copy(send_ref.at[group], send_out.at[at], sems.at[at]))
            copies[-1].start()
    for copy in copies:
        copy.wait()


def middle_rows(mix, weight, rows, gain):
    width = rows.shape[1]
    return pl.pallas_call(
        middle_kernel,
        out_shape=(
            jax.ShapeDtypeStruct((128, width), BF),
            jax.ShapeDtypeStruct((16, 32, width), BF),
        ),
        in_specs=[vmem()] * 4,
        out_specs=(pl.BlockSpec(memory_space=pltpu.HBM),) * 2,
        scratch_shapes=[
            pltpu.VMEM((128, width), F32),
            pltpu.VMEM((128, width), BF),
            pltpu.VMEM((4, 32, width), BF),
            pltpu.SemaphoreType.DMA((17,)),
        ],
        compiler_params=params(),
        cost_estimate=pl.CostEstimate(
            flops=2 * 128 * 2048 * 2048, bytes_accessed=12 << 20, transcendentals=0
        ),
    )(mix, weight, rows, gain)


def temporal_kernel(start_ref, rows_ref, weight_ref, out_ref, qkv, bias):
    count = rows_ref.shape[0]
    start = start_ref[0]
    late = lax.broadcasted_iota(jnp.int32, (count, count), 0)
    early = lax.broadcasted_iota(jnp.int32, (count, count), 1)
    same = (late & 7) == (early & 7)
    allowed = same & (early <= late) & ((early >= 8 * start) == (late >= 8 * start))
    bias[...] = jnp.where(allowed, 0.0, -1e30)
    for block in range(6):
        qkv[block] = dot(rows_ref[...], weight_ref[:, block].reshape(2048, 256)).astype(BF)
    size = 256
    for pair in range(2):
        for low in range(0, count, size):
            chains = []
            high = low + size
            for head in range(2):
                cols = slice(head * E, head * E + E)
                chains.append(
                    (
                        qkv[3 * pair, low:high, cols],
                        qkv[3 * pair + 1, :high, cols],
                        qkv[3 * pair + 2, :high, cols],
                        bias[low:high, :high],
                    )
                )
            for head, mixed in enumerate(attend(chains)):
                for spot in range(low // 32, high // 32):
                    rows = mixed[32 * spot - low : 32 * spot - low + 32]
                    at = (spot // 2 * 2 + head, spot % 2, slice(None), slice(E * pair, E * pair + E))
                    out_ref[at] = rows


def temporal_attend(start, rows, weight):
    count, width = rows.shape
    return pl.pallas_call(
        temporal_kernel,
        out_shape=jax.ShapeDtypeStruct((16, 2, 32, 256), BF),
        in_specs=[smem(), vmem(), vmem()],
        out_specs=vmem(),
        scratch_shapes=[
            pltpu.VMEM((6, count, 256), BF),
            pltpu.VMEM((count, count), F32),
        ],
        compiler_params=params(),
        cost_estimate=pl.CostEstimate(
            flops=2 * 512 * 2048 * 1536, bytes_accessed=9 << 20, transcendentals=131072
        ),
    )(start, rows, weight)


def last_kernel(place_ref, mix_ref, *refs):
    pieces, (keep_ref, give_ref, total) = refs[: 2 * NZ], refs[2 * NZ :]
    z, c = place_ref[0], place_ref[1]
    blocks = []
    for k in range(NZ):
        source = lax.rem(z + (OFFSETS[k] + NZ), NZ)
        cols = pl.ds(pl.multiple_of(lax.rem(source, 2) * E, E), E)
        blocks.append(
            jnp.concatenate(
                [
                    mix_ref[xl * 8 + source // 2 * 2 + core, frames, :, cols]
                    for frames in range(2)
                    for xl in range(2)
                    for core in range(2)
                ],
                axis=0,
            )
        )
    mix = jnp.concatenate(blocks, axis=1)
    for low in range(0, 2048, 512):
        part = jnp.concatenate([piece[:, low : low + 512] for piece in pieces], axis=0)
        total[:, :, low : low + 512] = dot(mix, part).reshape(2, 128, 512)
    keep_ref[...] = total[c]
    give_ref[...] = total[1 - c].astype(BF)


def last_sums(place, mix, pieces):
    width = pieces[0].shape[1]
    return pl.pallas_call(
        last_kernel,
        out_shape=(
            jax.ShapeDtypeStruct((128, width), F32),
            jax.ShapeDtypeStruct((128, width), BF),
        ),
        in_specs=[smem()] + [vmem()] * (2 * NZ + 1),
        out_specs=(vmem(), vmem()),
        scratch_shapes=[pltpu.VMEM((2, 128, width), F32)],
        compiler_params=params(),
        cost_estimate=pl.CostEstimate(
            flops=2 * 128 * 2048 * 2048, bytes_accessed=8 << 20, transcendentals=0
        ),
    )(place, mix, *pieces)


def end_kernel(keep_ref, got_ref, middle_ref, out_ref):
    for group in range(4):
        at = slice(32 * group, 32 * group + 32)
        rows = (keep_ref[at] + got_ref[at].astype(F32)).reshape(4, 8, -1)
        middle = jnp.stack(
            [
                middle_ref[32 * f : 32 * f + 32].astype(F32)[8 * group : 8 * group + 8]
                for f in range(4)
            ],
            axis=0,
        )
        out = jnp.transpose(rows + middle, (1, 0, 2)).astype(BF)
        out_ref[8 * group : 8 * group + 8] = out


def end_rows(keep, got, middle):
    return pl.pallas_call(
        end_kernel,
        out_shape=jax.ShapeDtypeStruct((32, 4, middle.shape[1]), BF),
        in_specs=[vmem()] * 3,
        out_specs=vmem(),
        compiler_params=params(),
        cost_estimate=pl.CostEstimate(flops=1 << 20, bytes_accessed=3 << 20, transcendentals=0),
    )(keep, got, middle)


def shifted(value, axis, step):
    count = lax.axis_size(axis)
    return lax.ppermute(value, axis, [(i, (i + step) % count) for i in range(count)])


def gathered_rows(chunks):
    up, down = list(chunks), list(chunks)
    pieces = {0: list(chunks)}
    for step in (1, 2, 3):
        up = [shifted(value, "z", 1) for value in up]
        down = [shifted(value, "z", -1) for value in down]
        pieces[-step], pieces[step] = up, down
    pieces[4] = [shifted(up[0], "z", 1), shifted(down[1], "z", -1)]
    return [value for offset in OFFSETS for value in pieces[offset]]


def local(stream, spatial_gain, spatial_qkv, spatial_out, temporal_gain, temporal_qkv, temporal_out, starts):
    patches, frames, width = stream.shape
    w, xl, y, c, z = (lax.axis_index(name) for name in ("w", "xl", "y", "c", "z"))

    place = (((w * 2 + xl) * 2 + c) * 4 + y).reshape(1)
    first, second, rows = norm_rows(
        place, stream, spatial_gain.reshape(1, width), jnp.transpose(temporal_qkv, (1, 0, 2))
    )

    low = ((lax.rem(y, 2) * 2 + c) * 64, ((w * 2 + xl) * 2 + y // 2) * 256)
    block = lax.dynamic_slice(spatial_out, low, (64, 256))
    whole_out = lax.all_to_all(jnp.broadcast_to(block, (NZ, 64, 256)), "z", 0, 0, tiled=True)
    pieces = gathered_rows((first, second))
    whole_out, _ = lax.optimization_barrier((whole_out, (pieces[2], pieces[4])))
    whole_out = lax.all_gather(whole_out, ("w", "xl", "y", "c"), axis=0, tiled=False)
    whole_out = whole_out.reshape(8, 4, NZ, 64, 256)

    sends = split_shares(jnp.stack([z, y]).astype(jnp.int32), pieces)
    got = [sends[0]] + [shifted(sends[k], "y", k) for k in range(1, 4)]

    weight = jnp.transpose(spatial_qkv, (1, 0, 2))
    mix = spatial_attend(z.reshape(1), weight, pieces)
    mix, *got = lax.optimization_barrier((mix, *got))
    quarter = join_shares(y.reshape(1), got)
    mix, quarter = lax.optimization_barrier((mix, quarter))
    quarter = lax.all_gather(quarter[None], ("w", "xl", "c"), axis=0, tiled=True)
    mix = lax.all_to_all(mix, "z", 0, 0, tiled=True)
    middle, send = middle_rows(mix, whole_out, rows, temporal_gain.reshape(1, width))

    half = lax.dynamic_slice(temporal_out, (c * E, 0), (E, width))
    send, half = lax.optimization_barrier((send, half))
    halves = gathered_rows((half[:64], half[64:]))

    window = lax.all_to_all(send, ("xl", "y", "c"), 0, 0, tiled=True)
    window, *halves[2:10] = lax.optimization_barrier((window, *halves[2:10]))
    start = lax.dynamic_slice(starts, (w,), (1,))
    mix = temporal_attend(start, window.reshape(512, width), quarter)
    mix = lax.all_to_all(mix, ("xl", "y", "c"), 0, 0, tiled=True)
    keep, give = last_sums(jnp.stack([z, c]).astype(jnp.int32), mix, halves)
    return end_rows(keep, shifted(give, "c", 1), middle)


def solution(mesh):
    names = ("w", "xl", "y", "c", "z")
    fine = Mesh(mesh.devices.reshape(2, 2, 4, 2, NZ), names)
    tm = ("w", "xl", "y", "c")
    placed = (
        P("z", tm, None),
        P(),
        P(None, None, "z"),
        P("z", None),
        P(),
        P(None, None, "z"),
        P("z", None),
        P(),
    )
    return jax.shard_map(
        local, mesh=fine, in_specs=placed, out_specs=P("z", tm, None), check_vma=False
    )
```

```python
import functools
import math

import jax
import jax.numpy as jnp
from jax import lax
from jax.experimental import pallas as pl
from jax.experimental.pallas import tpu as pltpu
from jax.sharding import Mesh
from jax.sharding import PartitionSpec as P

E = 128
SEQ = 64
SCALE = 1.0 / math.sqrt(E)
BF = jnp.bfloat16
F32 = jnp.float32
NZ = 8
VMEM_LIMIT = 28 * 1024 * 1024
OFFSETS = (0, -1, 1, -2, 2, -3, 3, 4)


def params():
    return pltpu.CompilerParams(vmem_limit_bytes=VMEM_LIMIT)


def vmem():
    return pl.BlockSpec(memory_space=pltpu.VMEM)


def smem():
    return pl.BlockSpec(memory_space=pltpu.SMEM)


def normed(values, gain):
    scaled = values * lax.rsqrt(jnp.mean(values * values, axis=-1, keepdims=True) + 1e-05)
    return (scaled * gain).astype(BF)


def softmax(scores):
    top = jnp.max(scores, axis=-1, keepdims=True)
    shifted = jnp.exp2((scores - top) * (SCALE * math.log2(math.e)))
    return (shifted * (1.0 / jnp.sum(shifted, axis=-1, keepdims=True))).astype(BF)


def dot(a, b):
    return jnp.dot(a, b, preferred_element_type=F32)


def dot_t(a, b):
    return lax.dot_general(a, b, (((1,), (1,)), ((), ())), preferred_element_type=F32)


def norm_kernel(place_ref, x_ref, gain_ref, qkv_ref, a_ref, b_ref, rows_ref):
    gain = gain_ref[...]
    values = jnp.transpose(x_ref[...].astype(F32), (1, 0, 2)).reshape(rows_ref.shape)
    half = rows_ref.shape[0] // 2
    rows_ref[...] = values.astype(BF)
    a_ref[:half] = normed(values[:half], gain)
    b_ref[:half] = normed(values[half:], gain)
    b_ref[half:, 1024:] = jnp.zeros((16, 1024), BF)
    for kind in range(3):
        share = qkv_ref[kind]
        ref = (a_ref, b_ref)[kind // 2]
        for group in range(4):
            low = 256 * (4 * (kind % 2) + group)
            ref[half:, low : low + 256] = share[16 * group : 16 * group + 16]


def norm_rows(place, stream, gain, temporal_qkv):
    patches, frames, width = stream.shape
    count = patches * frames
    half = jax.ShapeDtypeStruct((count // 2 + 16, width), BF)
    whole = lambda *shape: pl.BlockSpec(shape, lambda i, at: (0,) * len(shape))
    return pl.pallas_call(
        norm_kernel,
        grid_spec=pltpu.PrefetchScalarGridSpec(
            num_scalar_prefetch=1,
            grid=(1,),
            in_specs=[
                whole(patches, frames, width),
                whole(1, width),
                pl.BlockSpec((3, 64, 256), lambda i, at: (0, at[0], 0)),
            ],
            out_specs=(
                whole(count // 2 + 16, width),
                whole(count // 2 + 16, width),
                whole(count, width),
            ),
        ),
        out_shape=(half, half, jax.ShapeDtypeStruct((count, width), BF)),
        compiler_params=params(),
        cost_estimate=pl.CostEstimate(
            flops=4 * count * width, bytes_accessed=6 * count * width, transcendentals=0
        ),
    )(place, stream, gain, temporal_qkv)


def split_kernel(place_ref, *refs):
    pieces, sends = refs[:-4], refs[-4:]
    z, y = place_ref[0], place_ref[1]
    for k in range(NZ):
        source = lax.rem(z + (OFFSETS[k] + NZ), NZ)
        step = lax.rem(source // 2 + 4 - y, 4)
        pair = lax.rem(source, 2)
        for index, send_ref in enumerate(sends):

            @pl.when(step == index)
            def _():
                for kind in range(3):
                    for group in range(4):
                        low = 256 * (4 * (kind % 2) + group)
                        rows = slice(16 * group, 16 * group + 16)
                        value = pieces[2 * k + kind // 2][:, low : low + 256]
                        send_ref[pair, kind, rows] = value


def split_shares(place, pieces):
    return pl.pallas_call(
        split_kernel,
        grid=(1,),
        out_shape=(jax.ShapeDtypeStruct((2, 3, 64, 256), BF),) * 4,
        in_specs=[smem()] + [pl.BlockSpec((16, 2048), lambda i: (4, 0))] * len(pieces),
        out_specs=(pl.BlockSpec((2, 3, 64, 256), lambda i: (0, 0, 0, 0)),) * 4,
        compiler_params=params(),
        cost_estimate=pl.CostEstimate(flops=0, bytes_accessed=2 << 20, transcendentals=0),
    )(place, *pieces)


def join_kernel(y_ref, *refs):
    out_ref = refs[-1]
    for step in range(4):
        low = pl.multiple_of(64 * lax.rem(y_ref[0] + (4 - step), 4), 64)
        for pair in range(2):
            for kind in range(3):
                out_ref[3 * pair + kind, pl.ds(low, 64), :] = refs[step][pair, kind]


def join_shares(y, got):
    return pl.pallas_call(
        join_kernel,
        out_shape=jax.ShapeDtypeStruct((6, 256, 256), BF),
        in_specs=[smem()] + [vmem()] * 4,
        out_specs=vmem(),
        compiler_params=params(),
        cost_estimate=pl.CostEstimate(flops=0, bytes_accessed=2 << 20, transcendentals=0),
    )(y, *got)


def attend(chains):
    scores = [dot_t(query, key) for query, key, _, _ in chains]
    scores = [
        one if chain[3] is None else jnp.where(chain[3] < 0.0, chain[3], one)
        for one, chain in zip(scores, chains)
    ]
    weights = [softmax(one) for one in scores]
    return [dot(one, chain[2]).astype(BF) for one, chain in zip(weights, chains)]


def spatial_kernel(place_ref, weight_ref, *refs):
    pieces, out_ref, qkv = refs[: 2 * NZ], refs[2 * NZ], refs[2 * NZ + 1]
    place = place_ref[0]
    for frame in range(4):
        low = 32 * (frame % 2)
        rows = jnp.concatenate(
            [pieces[2 * k + frame // 2][low : low + 32, :] for k in range(NZ)], axis=0
        )
        for kind in range(3):
            qkv[kind, 256 * frame : 256 * frame + 256] = dot(rows, weight_ref[kind]).astype(BF)
    for frames in ((0, 1), (2, 3)):
        spots = [(frame, head * E) for frame in frames for head in range(2)]
        chains = []
        for frame, low in spots:
            at, cols = slice(256 * frame, 256 * frame + 256), slice(low, low + E)
            chains.append((qkv[0, at, cols], qkv[1, at, cols], qkv[2, at, cols], None))
        for (frame, low), mixed in zip(spots, attend(chains)):
            for k in range(NZ):
                target = lax.rem(place + (OFFSETS[k] + NZ), NZ)
                at = (low // E, target, slice(32 * frame, 32 * frame + 32))
                out_ref[at] = mixed[32 * k : 32 * k + 32]


def spatial_attend(place, weight, pieces):
    return pl.pallas_call(
        spatial_kernel,
        out_shape=jax.ShapeDtypeStruct((2, NZ, 128, E), BF),
        in_specs=[smem(), vmem()] + [vmem()] * len(pieces),
        out_specs=vmem(),
        scratch_shapes=[pltpu.VMEM((3, 1024, 256), BF)],
        compiler_params=params(),
        cost_estimate=pl.CostEstimate(
            flops=2 * 1024 * 2048 * 768 * 2, bytes_accessed=8 << 20, transcendentals=8 * 65536
        ),
    )(place, weight, *pieces)


def sums(place_ref, read, pieces, keep_ref, give_ref, total):
    z, c = place_ref[0], place_ref[1]
    mix = jnp.concatenate([read(lax.rem(z + (offset + NZ), NZ)) for offset in OFFSETS], axis=1)
    for low in range(0, 2048, 512):
        part = jnp.concatenate([piece[:, low : low + 512] for piece in pieces], axis=0)
        total[:, :, low : low + 512] = dot(mix, part).reshape(2, 128, 512)
    keep_ref[...] = total[c]
    give_ref[...] = total[1 - c].astype(BF)


def first_kernel(place_ref, mix_ref, *refs):
    def read(z):
        return jnp.concatenate([mix_ref[core * NZ + z] for core in range(2)], axis=0)

    sums(place_ref, read, refs[:-3], *refs[-3:])


def last_kernel(place_ref, mix_ref, *refs):
    def read(z):
        cols = pl.ds(pl.multiple_of(lax.rem(z, 2) * E, E), E)
        return jnp.concatenate(
            [
                mix_ref[xl * 8 + z // 2 * 2 + core, frames, :, cols]
                for frames in range(2)
                for xl in range(2)
                for core in range(2)
            ],
            axis=0,
        )

    sums(place_ref, read, refs[:-3], *refs[-3:])


def core_sums(kernel, place, mix, pieces):
    width = pieces[0].shape[1]
    return pl.pallas_call(
        kernel,
        out_shape=(
            jax.ShapeDtypeStruct((128, width), F32),
            jax.ShapeDtypeStruct((128, width), BF),
        ),
        in_specs=[smem()] + [vmem()] * (len(pieces) + 1),
        out_specs=(vmem(), vmem()),
        scratch_shapes=[pltpu.VMEM((2, 128, width), F32)],
        compiler_params=params(),
        cost_estimate=pl.CostEstimate(
            flops=2 * 128 * 2048 * 2048, bytes_accessed=8 << 20, transcendentals=0
        ),
    )(place, mix, *pieces)


def middle_kernel(keep_ref, got_ref, rows_ref, gain_ref, middle_ref, send_ref):
    total = keep_ref[...] + got_ref[...].astype(F32)
    middle = (total + rows_ref[...].astype(F32)).astype(BF)
    middle_ref[...] = middle
    values = middle.astype(F32)
    scaled = values * lax.rsqrt(jnp.mean(values * values, axis=-1, keepdims=True) + 1e-05)
    scaled = scaled * gain_ref[...]
    for group in range(4):
        chunk = jnp.concatenate(
            [scaled[32 * f + 8 * group : 32 * f + 8 * group + 8] for f in range(4)], axis=0
        ).astype(BF)
        for y in range(4):
            send_ref[(group // 2) * 8 + y * 2 + group % 2] = chunk


def middle_rows(keep, got, rows, gain):
    width = rows.shape[1]
    return pl.pallas_call(
        middle_kernel,
        out_shape=(
            jax.ShapeDtypeStruct((128, width), BF),
            jax.ShapeDtypeStruct((16, 32, width), BF),
        ),
        in_specs=[vmem()] * 4,
        out_specs=(vmem(), vmem()),
        compiler_params=params(),
        cost_estimate=pl.CostEstimate(flops=4 << 20, bytes_accessed=5 << 20, transcendentals=0),
    )(keep, got, rows, gain)


def temporal_kernel(place_ref, rows_ref, *refs):
    weights, (out_ref, rows, qkv, bias) = refs[:10], refs[10:]
    count = rows.shape[0]
    x, c = place_ref[1], place_ref[2]
    spots = [(step, core) for step in range(4) for core in range(2)]
    for spot, (step, core) in enumerate(spots):
        owner = lax.rem(x + (4 - step), 4) * 2 + (c if core == 0 else 1 - c)
        cols = pl.ds(pl.multiple_of(owner * 256, 256), 256)
        rows[:, 256 * spot : 256 * spot + 256] = rows_ref[:, cols]

    def block_of(step, core, block):
        own, up, down, up_twice, down_twice = weights[5 * core : 5 * core + 5]
        if step == 2:
            return up_twice[block] if block < 3 else down_twice[block - 3]
        return (own, up, None, down)[step][block]

    start = place_ref[0]
    late = lax.broadcasted_iota(jnp.int32, (count, count), 0)
    early = lax.broadcasted_iota(jnp.int32, (count, count), 1)
    same = (late & 7) == (early & 7)
    allowed = same & (early <= late) & ((early >= 8 * start) == (late >= 8 * start))
    bias[...] = jnp.where(allowed, 0.0, -1e30)
    for block in range(6):
        weight = jnp.concatenate([block_of(*spot, block) for spot in spots], axis=0)
        qkv[block] = dot(rows[...], weight).astype(BF)
    size = 256
    for pair in range(2):
        for low in range(0, count, size):
            chains = []
            high = low + size
            for head in range(2):
                cols = slice(head * E, head * E + E)
                chains.append(
                    (
                        qkv[3 * pair, low:high, cols],
                        qkv[3 * pair + 1, :high, cols],
                        qkv[3 * pair + 2, :high, cols],
                        bias[low:high, :high],
                    )
                )
            for head, mixed in enumerate(attend(chains)):
                for spot in range(low // 32, high // 32):
                    rows = mixed[32 * spot - low : 32 * spot - low + 32]
                    at = (spot // 2 * 2 + head, spot % 2, slice(None), slice(E * pair, E * pair + E))
                    out_ref[at] = rows


def temporal_attend(place, rows, weights):
    count, width = rows.shape
    return pl.pallas_call(
        temporal_kernel,
        out_shape=jax.ShapeDtypeStruct((16, 2, 32, 256), BF),
        in_specs=[smem(), vmem()] + [vmem()] * len(weights),
        out_specs=vmem(),
        scratch_shapes=[
            pltpu.VMEM((count, width), BF),
            pltpu.VMEM((6, count, 256), BF),
            pltpu.VMEM((count, count), F32),
        ],
        compiler_params=params(),
        cost_estimate=pl.CostEstimate(
            flops=2 * 512 * 2048 * 1536, bytes_accessed=9 << 20, transcendentals=131072
        ),
    )(place, rows, *weights)


def end_kernel(keep_ref, got_ref, middle_ref, out_ref):
    for group in range(4):
        at = slice(32 * group, 32 * group + 32)
        rows = (keep_ref[at] + got_ref[at].astype(F32)).reshape(4, 8, -1)
        middle = jnp.stack(
            [
                middle_ref[32 * f : 32 * f + 32].astype(F32)[8 * group : 8 * group + 8]
                for f in range(4)
            ],
            axis=0,
        )
        out = jnp.transpose(rows + middle, (1, 0, 2)).astype(BF)
        out_ref[8 * group : 8 * group + 8] = out


def end_rows(keep, got, middle):
    return pl.pallas_call(
        end_kernel,
        out_shape=jax.ShapeDtypeStruct((32, 4, middle.shape[1]), BF),
        in_specs=[vmem()] * 3,
        out_specs=vmem(),
        compiler_params=params(),
        cost_estimate=pl.CostEstimate(flops=1 << 20, bytes_accessed=3 << 20, transcendentals=0),
    )(keep, got, middle)


def shifted(value, axis, step):
    count = lax.axis_size(axis)
    return lax.ppermute(value, axis, [(i, (i + step) % count) for i in range(count)])


def gathered_rows(chunks):
    up, down = list(chunks), list(chunks)
    pieces = {0: list(chunks)}
    for step in (1, 2, 3):
        up = [shifted(value, "z", 1) for value in up]
        down = [shifted(value, "z", -1) for value in down]
        pieces[-step], pieces[step] = up, down
    pieces[4] = [shifted(up[0], "z", 1), shifted(down[1], "z", -1)]
    return [value for offset in OFFSETS for value in pieces[offset]]


def local(stream, spatial_gain, spatial_qkv, spatial_out, temporal_gain, temporal_qkv, temporal_out, starts):
    patches, frames, width = stream.shape
    w, xl, y, c, z = (lax.axis_index(name) for name in ("w", "xl", "y", "c", "z"))

    place = (((w * 2 + xl) * 2 + c) * 4 + y).reshape(1)
    first, second, rows = norm_rows(
        place, stream, spatial_gain.reshape(1, width), jnp.transpose(temporal_qkv, (1, 0, 2))
    )

    pieces = gathered_rows((first, second))

    spot = jnp.stack([z, c]).astype(jnp.int32)
    half = lax.dynamic_slice(spatial_out, (c * E, 0), (E, width))
    half, _ = lax.optimization_barrier((half, pieces[-2:]))
    halves = gathered_rows((half[:64], half[64:]))

    sends = split_shares(jnp.stack([z, y]).astype(jnp.int32), pieces)
    got = [sends[0]] + [shifted(sends[k], "y", k) for k in range(1, 4)]

    weight = jnp.transpose(spatial_qkv, (1, 0, 2))
    mix = spatial_attend(z.reshape(1), weight, pieces)
    mix, *got = lax.optimization_barrier((mix, *got))
    quarter = join_shares(y.reshape(1), got)
    mix, quarter = lax.optimization_barrier((mix, quarter))
    mix = lax.all_to_all(mix.reshape(16, 128, E), ("c", "z"), 0, 0, tiled=True)
    up, down = shifted(quarter, ("w", "xl"), 1), shifted(quarter, ("w", "xl"), -1)
    weights = [quarter, up, down]
    weights += [shifted(up[:3], ("w", "xl"), 1), shifted(down[3:], ("w", "xl"), -1)]
    weights += [shifted(weight, "c", 1) for weight in weights]

    keep, give = core_sums(first_kernel, spot, mix, halves)
    middle, send = middle_rows(keep, shifted(give, "c", 1), rows, temporal_gain.reshape(1, width))

    half = lax.dynamic_slice(temporal_out, (c * E, 0), (E, width))
    half, _ = lax.optimization_barrier((half, send))
    halves = gathered_rows((half[:64], half[64:]))

    window = lax.all_to_all(send, ("xl", "y", "c"), 0, 0, tiled=True)
    window, *halves[2:10] = lax.optimization_barrier((window, *halves[2:10]))
    start = lax.dynamic_slice(starts, (w,), (1,))[0]
    place = jnp.stack([start, w * 2 + xl, c]).astype(jnp.int32)
    mix = temporal_attend(place, window.reshape(512, width), weights)
    mix = lax.all_to_all(mix, ("xl", "y", "c"), 0, 0, tiled=True)
    keep, give = core_sums(last_kernel, spot, mix, halves)
    return end_rows(keep, shifted(give, "c", 1), middle)


def solution(mesh):
    names = ("w", "xl", "y", "c", "z")
    fine = Mesh(mesh.devices.reshape(2, 2, 4, 2, NZ), names)
    tm = ("w", "xl", "y", "c")
    placed = (
        P("z", tm, None),
        P(),
        P(None, None, "z"),
        P("z", None),
        P(),
        P(None, None, "z"),
        P("z", None),
        P(),
    )
    return jax.shard_map(
        local, mesh=fine, in_specs=placed, out_specs=P("z", tm, None), check_vma=False
    )
```

```python
import functools
import math

import jax
import jax.numpy as jnp
from jax import lax
from jax.experimental import pallas as pl
from jax.experimental.pallas import tpu as pltpu
from jax.sharding import Mesh
from jax.sharding import PartitionSpec as P

E = 128
SEQ = 64
SCALE = 1.0 / math.sqrt(E)
BF = jnp.bfloat16
F32 = jnp.float32
NZ = 8
VMEM_LIMIT = 28 * 1024 * 1024
OFFSETS = (0, -1, 1, -2, 2, -3, 3, 4)


def params():
    return pltpu.CompilerParams(vmem_limit_bytes=VMEM_LIMIT)


def vmem():
    return pl.BlockSpec(memory_space=pltpu.VMEM)


def smem():
    return pl.BlockSpec(memory_space=pltpu.SMEM)


def normed(values, gain):
    scaled = values * lax.rsqrt(jnp.mean(values * values, axis=-1, keepdims=True) + 1e-05)
    return (scaled * gain).astype(BF)


def softmax(scores):
    top = jnp.max(scores, axis=-1, keepdims=True)
    shifted = jnp.exp2((scores - top) * (SCALE * math.log2(math.e)))
    return (shifted * (1.0 / jnp.sum(shifted, axis=-1, keepdims=True))).astype(BF)


def dot(a, b):
    return jnp.dot(a, b, preferred_element_type=F32)


def dot_t(a, b):
    return lax.dot_general(a, b, (((1,), (1,)), ((), ())), preferred_element_type=F32)


def norm_kernel(place_ref, x_ref, gain_ref, qkv_ref, a_ref, b_ref, rows_ref):
    gain = gain_ref[...]
    values = jnp.transpose(x_ref[...].astype(F32), (1, 0, 2)).reshape(rows_ref.shape)
    half = rows_ref.shape[0] // 2
    rows_ref[...] = values.astype(BF)
    a_ref[:half] = normed(values[:half], gain)
    b_ref[:half] = normed(values[half:], gain)
    b_ref[half:, 1024:] = jnp.zeros((16, 1024), BF)
    for kind in range(3):
        share = qkv_ref[kind]
        ref = (a_ref, b_ref)[kind // 2]
        for group in range(4):
            low = 256 * (4 * (kind % 2) + group)
            ref[half:, low : low + 256] = share[16 * group : 16 * group + 16]


def norm_rows(place, stream, gain, temporal_qkv):
    patches, frames, width = stream.shape
    count = patches * frames
    half = jax.ShapeDtypeStruct((count // 2 + 16, width), BF)
    whole = lambda *shape: pl.BlockSpec(shape, lambda i, at: (0,) * len(shape))
    return pl.pallas_call(
        norm_kernel,
        grid_spec=pltpu.PrefetchScalarGridSpec(
            num_scalar_prefetch=1,
            grid=(1,),
            in_specs=[
                whole(patches, frames, width),
                whole(1, width),
                pl.BlockSpec((3, 64, 256), lambda i, at: (0, at[0], 0)),
            ],
            out_specs=(
                whole(count // 2 + 16, width),
                whole(count // 2 + 16, width),
                whole(count, width),
            ),
        ),
        out_shape=(half, half, jax.ShapeDtypeStruct((count, width), BF)),
        compiler_params=params(),
        cost_estimate=pl.CostEstimate(
            flops=4 * count * width, bytes_accessed=6 * count * width, transcendentals=0
        ),
    )(place, stream, gain, temporal_qkv)


def split_kernel(place_ref, *refs):
    pieces, sends = refs[:-4], refs[-4:]
    z, y = place_ref[0], place_ref[1]
    for k in range(NZ):
        source = lax.rem(z + (OFFSETS[k] + NZ), NZ)
        step = lax.rem(source // 2 + 4 - y, 4)
        pair = lax.rem(source, 2)
        for index, send_ref in enumerate(sends):

            @pl.when(step == index)
            def _():
                for kind in range(3):
                    for group in range(4):
                        low = 256 * (4 * (kind % 2) + group)
                        rows = slice(16 * group, 16 * group + 16)
                        value = pieces[2 * k + kind // 2][:, low : low + 256]
                        send_ref[pair, kind, rows] = value


def split_shares(place, pieces):
    return pl.pallas_call(
        split_kernel,
        grid=(1,),
        out_shape=(jax.ShapeDtypeStruct((2, 3, 64, 256), BF),) * 4,
        in_specs=[smem()] + [pl.BlockSpec((16, 2048), lambda i: (4, 0))] * len(pieces),
        out_specs=(pl.BlockSpec((2, 3, 64, 256), lambda i: (0, 0, 0, 0)),) * 4,
        compiler_params=params(),
        cost_estimate=pl.CostEstimate(flops=0, bytes_accessed=2 << 20, transcendentals=0),
    )(place, *pieces)


def join_kernel(y_ref, *refs):
    out_ref = refs[-1]
    for step in range(4):
        low = pl.multiple_of(64 * lax.rem(y_ref[0] + (4 - step), 4), 64)
        for pair in range(2):
            for kind in range(3):
                out_ref[3 * pair + kind, pl.ds(low, 64), :] = refs[step][pair, kind]


def join_shares(y, got):
    return pl.pallas_call(
        join_kernel,
        out_shape=jax.ShapeDtypeStruct((6, 256, 256), BF),
        in_specs=[smem()] + [vmem()] * 4,
        out_specs=vmem(),
        compiler_params=params(),
        cost_estimate=pl.CostEstimate(flops=0, bytes_accessed=2 << 20, transcendentals=0),
    )(y, *got)


def attend(chains):
    scores = [dot_t(query, key) for query, key, _, _ in chains]
    scores = [
        one if chain[3] is None else jnp.where(chain[3] < 0.0, chain[3], one)
        for one, chain in zip(scores, chains)
    ]
    weights = [softmax(one) for one in scores]
    return [dot(one, chain[2]).astype(BF) for one, chain in zip(weights, chains)]


def spatial_kernel(place_ref, weight_ref, *refs):
    pieces, out_ref, qkv = refs[: 2 * NZ], refs[2 * NZ], refs[2 * NZ + 1]
    place = place_ref[0]
    for frame in range(4):
        low = 32 * (frame % 2)
        rows = jnp.concatenate(
            [pieces[2 * k + frame // 2][low : low + 32, :] for k in range(NZ)], axis=0
        )
        for kind in range(3):
            qkv[kind, 256 * frame : 256 * frame + 256] = dot(rows, weight_ref[kind]).astype(BF)
    for frames in ((0, 1), (2, 3)):
        spots = [(frame, head * E) for frame in frames for head in range(2)]
        chains = []
        for frame, low in spots:
            at, cols = slice(256 * frame, 256 * frame + 256), slice(low, low + E)
            chains.append((qkv[0, at, cols], qkv[1, at, cols], qkv[2, at, cols], None))
        for (frame, low), mixed in zip(spots, attend(chains)):
            for k in range(NZ):
                target = lax.rem(place + (OFFSETS[k] + NZ), NZ)
                out_ref[target, 32 * frame : 32 * frame + 32, low : low + E] = mixed[
                    32 * k : 32 * k + 32
                ]


def spatial_attend(place, weight, pieces):
    return pl.pallas_call(
        spatial_kernel,
        out_shape=jax.ShapeDtypeStruct((NZ, 128, 256), BF),
        in_specs=[smem(), vmem()] + [vmem()] * len(pieces),
        out_specs=vmem(),
        scratch_shapes=[pltpu.VMEM((3, 1024, 256), BF)],
        compiler_params=params(),
        cost_estimate=pl.CostEstimate(
            flops=2 * 1024 * 2048 * 768 * 2, bytes_accessed=8 << 20, transcendentals=8 * 65536
        ),
    )(place, weight, *pieces)


def column_block(read):
    return jnp.concatenate([read(head, k // 4, k % 4) for k in range(NZ) for head in range(2)], axis=0)


def join_blocks_kernel(z_ref, *refs):
    out_ref = refs[-1]
    for step in range(4):
        out_ref[lax.rem(z_ref[0] + (4 - step), 4)] = refs[step][...]


def join_blocks(z, parts):
    return pl.pallas_call(
        join_blocks_kernel,
        out_shape=jax.ShapeDtypeStruct((4, 128, 256), BF),
        in_specs=[smem()] + [vmem()] * 4,
        out_specs=vmem(),
        compiler_params=params(),
        cost_estimate=pl.CostEstimate(flops=0, bytes_accessed=512 << 10, transcendentals=0),
    )(z, *parts)


def middle_kernel(mix_ref, weight_ref, rows_ref, gain_ref, middle_ref, send_ref, total):
    mix = jnp.concatenate([mix_ref[k] for k in range(NZ)], axis=1)
    for block in range(8):
        part = column_block(lambda *at: weight_ref[(block, *at)])
        total[:, 256 * block : 256 * block + 256] = dot(mix, part)
    middle = (total[...] + rows_ref[...].astype(F32)).astype(BF)
    middle_ref[...] = middle
    values = middle.astype(F32)
    scaled = values * lax.rsqrt(jnp.mean(values * values, axis=-1, keepdims=True) + 1e-05)
    scaled = scaled * gain_ref[...]
    for group in range(4):
        chunk = jnp.concatenate(
            [scaled[32 * f + 8 * group : 32 * f + 8 * group + 8] for f in range(4)], axis=0
        ).astype(BF)
        for y in range(4):
            send_ref[(group // 2) * 8 + y * 2 + group % 2] = chunk


def middle_rows(mix, weight, rows, gain):
    width = rows.shape[1]
    return pl.pallas_call(
        middle_kernel,
        out_shape=(
            jax.ShapeDtypeStruct((128, width), BF),
            jax.ShapeDtypeStruct((16, 32, width), BF),
        ),
        in_specs=[vmem()] * 4,
        out_specs=(vmem(), vmem()),
        scratch_shapes=[pltpu.VMEM((128, width), F32)],
        compiler_params=params(),
        cost_estimate=pl.CostEstimate(
            flops=2 * 128 * 2048 * 2048, bytes_accessed=12 << 20, transcendentals=0
        ),
    )(mix, weight, rows, gain)


def temporal_kernel(start_ref, rows_ref, weight_ref, out_ref, qkv, bias):
    count = rows_ref.shape[0]
    start = start_ref[0]
    late = lax.broadcasted_iota(jnp.int32, (count, count), 0)
    early = lax.broadcasted_iota(jnp.int32, (count, count), 1)
    same = (late & 7) == (early & 7)
    allowed = same & (early <= late) & ((early >= 8 * start) == (late >= 8 * start))
    bias[...] = jnp.where(allowed, 0.0, -1e30)
    for block in range(6):
        qkv[block] = dot(rows_ref[...], weight_ref[:, block].reshape(2048, 256)).astype(BF)
    size = 256
    for pair in range(2):
        for low in range(0, count, size):
            chains = []
            high = low + size
            for head in range(2):
                cols = slice(head * E, head * E + E)
                chains.append(
                    (
                        qkv[3 * pair, low:high, cols],
                        qkv[3 * pair + 1, :high, cols],
                        qkv[3 * pair + 2, :high, cols],
                        bias[low:high, :high],
                    )
                )
            for head, mixed in enumerate(attend(chains)):
                for spot in range(low // 32, high // 32):
                    rows = mixed[32 * spot - low : 32 * spot - low + 32]
                    at = (spot // 2 * 2 + head, spot % 2, slice(None), slice(E * pair, E * pair + E))
                    out_ref[at] = rows


def temporal_attend(start, rows, weight):
    count, width = rows.shape
    return pl.pallas_call(
        temporal_kernel,
        out_shape=jax.ShapeDtypeStruct((16, 2, 32, 256), BF),
        in_specs=[smem(), vmem(), vmem()],
        out_specs=vmem(),
        scratch_shapes=[
            pltpu.VMEM((6, count, 256), BF),
            pltpu.VMEM((count, count), F32),
        ],
        compiler_params=params(),
        cost_estimate=pl.CostEstimate(
            flops=2 * 512 * 2048 * 1536, bytes_accessed=9 << 20, transcendentals=131072
        ),
    )(start, rows, weight)


def last_kernel(place_ref, mix_ref, *refs):
    pieces, (keep_ref, give_ref, total) = refs[: NZ + 1], refs[NZ + 1 :]
    z, c = place_ref[0], place_ref[1]
    blocks = []
    for k in range(NZ):
        source = lax.rem(z + (OFFSETS[k] + NZ), NZ)
        cols = pl.ds(pl.multiple_of(lax.rem(source, 2) * E, E), E)
        blocks.append(
            jnp.concatenate(
                [
                    mix_ref[xl * 8 + source // 2 * 2 + core, frames, :, cols]
                    for frames in range(2)
                    for xl in range(2)
                    for core in range(2)
                ],
                axis=0,
            )
        )
    mix = jnp.concatenate(blocks, axis=1)
    for low in range(0, 2048, 512):
        part = jnp.concatenate([piece[:, low : low + 512] for piece in pieces], axis=0)
        total[:, :, low : low + 512] = dot(mix, part).reshape(2, 128, 512)
    keep_ref[...] = total[c]
    give_ref[...] = total[1 - c].astype(BF)


def last_sums(place, mix, pieces):
    width = pieces[0].shape[1]
    return pl.pallas_call(
        last_kernel,
        out_shape=(
            jax.ShapeDtypeStruct((128, width), F32),
            jax.ShapeDtypeStruct((128, width), BF),
        ),
        in_specs=[smem()] + [vmem()] * (NZ + 2),
        out_specs=(vmem(), vmem()),
        scratch_shapes=[pltpu.VMEM((2, 128, width), F32)],
        compiler_params=params(),
        cost_estimate=pl.CostEstimate(
            flops=2 * 128 * 2048 * 2048, bytes_accessed=8 << 20, transcendentals=0
        ),
    )(place, mix, *pieces)


def end_kernel(keep_ref, got_ref, middle_ref, out_ref):
    for group in range(4):
        at = slice(32 * group, 32 * group + 32)
        rows = (keep_ref[at] + got_ref[at].astype(F32)).reshape(4, 8, -1)
        middle = jnp.stack(
            [
                middle_ref[32 * f : 32 * f + 32].astype(F32)[8 * group : 8 * group + 8]
                for f in range(4)
            ],
            axis=0,
        )
        out = jnp.transpose(rows + middle, (1, 0, 2)).astype(BF)
        out_ref[8 * group : 8 * group + 8] = out


def end_rows(keep, got, middle):
    return pl.pallas_call(
        end_kernel,
        out_shape=jax.ShapeDtypeStruct((32, 4, middle.shape[1]), BF),
        in_specs=[vmem()] * 3,
        out_specs=vmem(),
        compiler_params=params(),
        cost_estimate=pl.CostEstimate(flops=1 << 20, bytes_accessed=3 << 20, transcendentals=0),
    )(keep, got, middle)


def shifted(value, axis, step):
    count = lax.axis_size(axis)
    return lax.ppermute(value, axis, [(i, (i + step) % count) for i in range(count)])


def gathered_rows(chunks):
    up, down = list(chunks), list(chunks)
    pieces = {0: list(chunks)}
    for step in (1, 2, 3):
        up = [shifted(value, "z", 1) for value in up]
        down = [shifted(value, "z", -1) for value in down]
        pieces[-step], pieces[step] = up, down
    pieces[4] = [shifted(up[0], "z", 1), shifted(down[1], "z", -1)]
    return [value for offset in OFFSETS for value in pieces[offset]]


def local(stream, spatial_gain, spatial_qkv, spatial_out, temporal_gain, temporal_qkv, temporal_out, starts):
    patches, frames, width = stream.shape
    w, xl, y, c, z = (lax.axis_index(name) for name in ("w", "xl", "y", "c", "z"))

    place = (((w * 2 + xl) * 2 + c) * 4 + y).reshape(1)
    first, second, rows = norm_rows(
        place, stream, spatial_gain.reshape(1, width), jnp.transpose(temporal_qkv, (1, 0, 2))
    )

    low = (lax.rem(y, 2) * E, ((w * 2 + xl) * 2 + y // 2) * 256)
    block = lax.dynamic_slice(spatial_out, low, (E, 256))
    parts = []
    for k in range(4):
        pairs = [
            (a * 8 + b, (b // 4) * 8 + (b + 4 * a + k) % 8) for a in range(2) for b in range(8)
        ]
        parts.append(lax.ppermute(block, ("c", "z"), pairs))
    first, second, parts = lax.optimization_barrier((first, second, parts))
    whole_out = join_blocks(z.reshape(1), parts)
    whole_out = lax.all_gather(whole_out, ("w", "xl", "y", "c"), axis=0, tiled=False)
    whole_out = whole_out.reshape(8, 2, 2, 4, E, 256)

    pieces = gathered_rows((first, second))

    sends = split_shares(jnp.stack([z, y]).astype(jnp.int32), pieces)
    got = [sends[0]] + [shifted(sends[k], "y", k) for k in range(1, 4)]

    weight = jnp.transpose(spatial_qkv, (1, 0, 2))
    mix = spatial_attend(z.reshape(1), weight, pieces)
    mix, whole_out = lax.optimization_barrier((mix, whole_out))
    quarter = join_shares(y.reshape(1), got)
    quarter = lax.all_gather(quarter[None], ("w", "xl", "c"), axis=0, tiled=True)
    mix = lax.all_to_all(mix, "z", 0, 0, tiled=True)

    middle, send = middle_rows(mix, whole_out, rows, temporal_gain.reshape(1, width))

    half = lax.dynamic_slice(temporal_out, (c * E, 0), (E, width))
    send, half = lax.optimization_barrier((send, half))
    up, down = half, half
    halves = [half]
    for step in (1, 2, 3):
        up, down = shifted(up, "z", 1), shifted(down, "z", -1)
        halves += [up, down]
    halves += [shifted(up[:64], "z", 1), shifted(down[64:], "z", -1)]

    window = lax.all_to_all(send, ("xl", "y", "c"), 0, 0, tiled=True)
    window, *halves[1:3] = lax.optimization_barrier((window, *halves[1:3]))
    start = lax.dynamic_slice(starts, (w,), (1,))
    mix = temporal_attend(start, window.reshape(512, width), quarter)
    mix = lax.all_to_all(mix, ("xl", "y", "c"), 0, 0, tiled=True)
    keep, give = last_sums(jnp.stack([z, c]).astype(jnp.int32), mix, halves)
    return end_rows(keep, shifted(give, "c", 1), middle)


def solution(mesh):
    names = ("w", "xl", "y", "c", "z")
    fine = Mesh(mesh.devices.reshape(2, 2, 4, 2, NZ), names)
    tm = ("w", "xl", "y", "c")
    placed = (
        P("z", tm, None),
        P(),
        P(None, None, "z"),
        P("z", None),
        P(),
        P(None, None, "z"),
        P("z", None),
        P(),
    )
    return jax.shard_map(
        local, mesh=fine, in_specs=placed, out_specs=P("z", tm, None), check_vma=False
    )
```

```python
import functools
import math

import jax
import jax.numpy as jnp
from jax import lax
from jax.experimental import pallas as pl
from jax.experimental.pallas import tpu as pltpu
from jax.sharding import Mesh
from jax.sharding import PartitionSpec as P

E = 128
SEQ = 64
SCALE = 1.0 / math.sqrt(E)
BF = jnp.bfloat16
F32 = jnp.float32
NZ = 8
VMEM_LIMIT = 20 * 1024 * 1024
OFFSETS = (0, -1, 1, -2, 2, -3, 3, 4)


def params():
    return pltpu.CompilerParams(vmem_limit_bytes=VMEM_LIMIT)


def vmem():
    return pl.BlockSpec(memory_space=pltpu.VMEM)


def smem():
    return pl.BlockSpec(memory_space=pltpu.SMEM)


def normed(values, gain):
    scaled = values * lax.rsqrt(jnp.mean(values * values, axis=-1, keepdims=True) + 1e-05)
    return (scaled * gain).astype(BF)


def softmax(scores):
    top = jnp.max(scores, axis=-1, keepdims=True)
    shifted = jnp.exp2((scores - top) * (SCALE * math.log2(math.e)))
    return (shifted * (1.0 / jnp.sum(shifted, axis=-1, keepdims=True))).astype(BF)


def dot(a, b):
    return jnp.dot(a, b, preferred_element_type=F32)


def dot_t(a, b):
    return lax.dot_general(a, b, (((1,), (1,)), ((), ())), preferred_element_type=F32)


def norm_kernel(place_ref, x_ref, gain_ref, qkv_ref, a_ref, b_ref, rows_ref):
    gain = gain_ref[...]
    values = jnp.transpose(x_ref[...].astype(F32), (1, 0, 2)).reshape(rows_ref.shape)
    half = rows_ref.shape[0] // 2
    rows_ref[...] = values.astype(BF)
    a_ref[:half] = normed(values[:half], gain)
    b_ref[:half] = normed(values[half:], gain)
    b_ref[half:, 1024:] = jnp.zeros((16, 1024), BF)
    for kind in range(3):
        share = qkv_ref[kind]
        ref = (a_ref, b_ref)[kind // 2]
        for group in range(4):
            low = 256 * (4 * (kind % 2) + group)
            ref[half:, low : low + 256] = share[16 * group : 16 * group + 16]


def norm_rows(place, stream, gain, temporal_qkv):
    patches, frames, width = stream.shape
    count = patches * frames
    half = jax.ShapeDtypeStruct((count // 2 + 16, width), BF)
    whole = lambda *shape: pl.BlockSpec(shape, lambda i, at: (0,) * len(shape))
    return pl.pallas_call(
        norm_kernel,
        grid_spec=pltpu.PrefetchScalarGridSpec(
            num_scalar_prefetch=1,
            grid=(1,),
            in_specs=[
                whole(patches, frames, width),
                whole(1, width),
                pl.BlockSpec((3, 64, 256), lambda i, at: (0, at[0], 0)),
            ],
            out_specs=(
                whole(count // 2 + 16, width),
                whole(count // 2 + 16, width),
                whole(count, width),
            ),
        ),
        out_shape=(half, half, jax.ShapeDtypeStruct((count, width), BF)),
        compiler_params=params(),
        cost_estimate=pl.CostEstimate(
            flops=4 * count * width, bytes_accessed=6 * count * width, transcendentals=0
        ),
    )(place, stream, gain, temporal_qkv)


def split_kernel(place_ref, *refs):
    pieces, sends = refs[:-4], refs[-4:]
    z, y = place_ref[0], place_ref[1]
    for k in range(NZ):
        source = lax.rem(z + (OFFSETS[k] + NZ), NZ)
        step = lax.rem(source // 2 + 4 - y, 4)
        pair = lax.rem(source, 2)
        for index, send_ref in enumerate(sends):

            @pl.when(step == index)
            def _():
                for kind in range(3):
                    for group in range(4):
                        low = 256 * (4 * (kind % 2) + group)
                        rows = slice(16 * group, 16 * group + 16)
                        value = pieces[2 * k + kind // 2][:, low : low + 256]
                        send_ref[pair, kind, rows] = value


def split_shares(place, pieces):
    return pl.pallas_call(
        split_kernel,
        grid=(1,),
        out_shape=(jax.ShapeDtypeStruct((2, 3, 64, 256), BF),) * 4,
        in_specs=[smem()] + [pl.BlockSpec((16, 2048), lambda i: (4, 0))] * len(pieces),
        out_specs=(pl.BlockSpec((2, 3, 64, 256), lambda i: (0, 0, 0, 0)),) * 4,
        compiler_params=params(),
        cost_estimate=pl.CostEstimate(flops=0, bytes_accessed=2 << 20, transcendentals=0),
    )(place, *pieces)


def join_kernel(y_ref, *refs):
    out_ref = refs[-1]
    for step in range(4):
        low = pl.multiple_of(64 * lax.rem(y_ref[0] + (4 - step), 4), 64)
        for pair in range(2):
            for kind in range(3):
                out_ref[3 * pair + kind, pl.ds(low, 64), :] = refs[step][pair, kind]


def join_shares(y, got):
    return pl.pallas_call(
        join_kernel,
        out_shape=jax.ShapeDtypeStruct((6, 256, 256), BF),
        in_specs=[smem()] + [vmem()] * 4,
        out_specs=vmem(),
        compiler_params=params(),
        cost_estimate=pl.CostEstimate(flops=0, bytes_accessed=2 << 20, transcendentals=0),
    )(y, *got)


def attend(chains):
    scores = [dot_t(query, key) for query, key, _, _ in chains]
    scores = [
        one if chain[3] is None else jnp.where(chain[3] < 0.0, chain[3], one)
        for one, chain in zip(scores, chains)
    ]
    weights = [softmax(one) for one in scores]
    return [dot(one, chain[2]).astype(BF) for one, chain in zip(weights, chains)]


def spatial_kernel(place_ref, weight_ref, *refs):
    pieces, out_ref, qkv = refs[: 2 * NZ], refs[2 * NZ], refs[2 * NZ + 1]
    place = place_ref[0]
    for frame in range(4):
        low = 32 * (frame % 2)
        rows = jnp.concatenate(
            [pieces[2 * k + frame // 2][low : low + 32, :] for k in range(NZ)], axis=0
        )
        for kind in range(3):
            qkv[kind, 256 * frame : 256 * frame + 256] = dot(rows, weight_ref[kind]).astype(BF)
    for frames in ((0, 1), (2, 3)):
        spots = [(frame, head * E) for frame in frames for head in range(2)]
        chains = []
        for frame, low in spots:
            at, cols = slice(256 * frame, 256 * frame + 256), slice(low, low + E)
            chains.append((qkv[0, at, cols], qkv[1, at, cols], qkv[2, at, cols], None))
        for (frame, low), mixed in zip(spots, attend(chains)):
            for k in range(NZ):
                target = lax.rem(place + (OFFSETS[k] + NZ), NZ)
                out_ref[target, 32 * frame : 32 * frame + 32, low : low + E] = mixed[
                    32 * k : 32 * k + 32
                ]


def spatial_attend(place, weight, pieces):
    return pl.pallas_call(
        spatial_kernel,
        out_shape=jax.ShapeDtypeStruct((NZ, 128, 256), BF),
        in_specs=[smem(), vmem()] + [vmem()] * len(pieces),
        out_specs=vmem(),
        scratch_shapes=[pltpu.VMEM((3, 1024, 256), BF)],
        compiler_params=params(),
        cost_estimate=pl.CostEstimate(
            flops=2 * 1024 * 2048 * 768 * 2, bytes_accessed=8 << 20, transcendentals=8 * 65536
        ),
    )(place, weight, *pieces)


def column_block(read):
    return jnp.concatenate([read(head, k // 4, k % 4) for k in range(NZ) for head in range(2)], axis=0)


def join_blocks_kernel(z_ref, *refs):
    out_ref = refs[-1]
    for step in range(4):
        out_ref[lax.rem(z_ref[0] + (4 - step), 4)] = refs[step][...]


def join_blocks(z, parts):
    return pl.pallas_call(
        join_blocks_kernel,
        out_shape=jax.ShapeDtypeStruct((4, 128, 256), BF),
        in_specs=[smem()] + [vmem()] * 4,
        out_specs=vmem(),
        compiler_params=params(),
        cost_estimate=pl.CostEstimate(flops=0, bytes_accessed=512 << 10, transcendentals=0),
    )(z, *parts)


def middle_kernel(mix_ref, weight_ref, rows_ref, gain_ref, middle_ref, send_ref, total):
    mix = jnp.concatenate([mix_ref[k] for k in range(NZ)], axis=1)
    for block in range(8):
        part = column_block(lambda *at: weight_ref[(block, *at)])
        total[:, 256 * block : 256 * block + 256] = dot(mix, part)
    middle = (total[...] + rows_ref[...].astype(F32)).astype(BF)
    middle_ref[...] = middle
    values = middle.astype(F32)
    scaled = values * lax.rsqrt(jnp.mean(values * values, axis=-1, keepdims=True) + 1e-05)
    scaled = scaled * gain_ref[...]
    for group in range(4):
        chunk = jnp.concatenate(
            [scaled[32 * f + 8 * group : 32 * f + 8 * group + 8] for f in range(4)], axis=0
        ).astype(BF)
        for y in range(4):
            send_ref[(group // 2) * 8 + y * 2 + group % 2] = chunk


def middle_rows(mix, weight, rows, gain):
    width = rows.shape[1]
    return pl.pallas_call(
        middle_kernel,
        out_shape=(
            jax.ShapeDtypeStruct((128, width), BF),
            jax.ShapeDtypeStruct((16, 32, width), BF),
        ),
        in_specs=[vmem()] * 4,
        out_specs=(vmem(), vmem()),
        scratch_shapes=[pltpu.VMEM((128, width), F32)],
        compiler_params=params(),
        cost_estimate=pl.CostEstimate(
            flops=2 * 128 * 2048 * 2048, bytes_accessed=12 << 20, transcendentals=0
        ),
    )(mix, weight, rows, gain)


def temporal_kernel(start_ref, rows_ref, weight_ref, out_ref, qkv, bias):
    count = rows_ref.shape[0]
    start = start_ref[0]
    late = lax.broadcasted_iota(jnp.int32, (count, count), 0)
    early = lax.broadcasted_iota(jnp.int32, (count, count), 1)
    same = (late & 7) == (early & 7)
    allowed = same & (early <= late) & ((early >= 8 * start) == (late >= 8 * start))
    bias[...] = jnp.where(allowed, 0.0, -1e30)
    for block in range(6):
        qkv[block] = dot(rows_ref[...], weight_ref[:, block].reshape(2048, 256)).astype(BF)
    size = 256
    for pair in range(2):
        for low in range(0, count, size):
            chains = []
            high = low + size
            for head in range(2):
                cols = slice(head * E, head * E + E)
                chains.append(
                    (
                        qkv[3 * pair, low:high, cols],
                        qkv[3 * pair + 1, :high, cols],
                        qkv[3 * pair + 2, :high, cols],
                        bias[low:high, :high],
                    )
                )
            for head, mixed in enumerate(attend(chains)):
                for spot in range(low // 32, high // 32):
                    rows = mixed[32 * spot - low : 32 * spot - low + 32]
                    at = (spot // 2 * 2 + head, spot % 2, slice(None), slice(E * pair, E * pair + E))
                    out_ref[at] = rows


def temporal_attend(start, rows, weight):
    count, width = rows.shape
    return pl.pallas_call(
        temporal_kernel,
        out_shape=jax.ShapeDtypeStruct((16, 2, 32, 256), BF),
        in_specs=[smem(), vmem(), vmem()],
        out_specs=vmem(),
        scratch_shapes=[
            pltpu.VMEM((6, count, 256), BF),
            pltpu.VMEM((count, count), F32),
        ],
        compiler_params=params(),
        cost_estimate=pl.CostEstimate(
            flops=2 * 512 * 2048 * 1536, bytes_accessed=9 << 20, transcendentals=131072
        ),
    )(start, rows, weight)


def last_kernel(place_ref, mix_ref, *refs):
    pieces, (keep_ref, give_ref, total) = refs[: NZ + 1], refs[NZ + 1 :]
    z, c = place_ref[0], place_ref[1]
    blocks = []
    for k in range(NZ):
        source = lax.rem(z + (OFFSETS[k] + NZ), NZ)
        cols = pl.ds(pl.multiple_of(lax.rem(source, 2) * E, E), E)
        blocks.append(
            jnp.concatenate(
                [
                    mix_ref[xl * 8 + source // 2 * 2 + core, frames, :, cols]
                    for frames in range(2)
                    for xl in range(2)
                    for core in range(2)
                ],
                axis=0,
            )
        )
    mix = jnp.concatenate(blocks, axis=1)
    for low in range(0, 2048, 512):
        part = jnp.concatenate([piece[:, low : low + 512] for piece in pieces], axis=0)
        total[:, :, low : low + 512] = dot(mix, part).reshape(2, 128, 512)
    keep_ref[...] = total[c]
    give_ref[...] = total[1 - c].astype(BF)


def last_sums(place, mix, pieces):
    width = pieces[0].shape[1]
    return pl.pallas_call(
        last_kernel,
        out_shape=(
            jax.ShapeDtypeStruct((128, width), F32),
            jax.ShapeDtypeStruct((128, width), BF),
        ),
        in_specs=[smem()] + [vmem()] * (NZ + 2),
        out_specs=(vmem(), vmem()),
        scratch_shapes=[pltpu.VMEM((2, 128, width), F32)],
        compiler_params=params(),
        cost_estimate=pl.CostEstimate(
            flops=2 * 128 * 2048 * 2048, bytes_accessed=8 << 20, transcendentals=0
        ),
    )(place, mix, *pieces)


def end_kernel(keep_ref, got_ref, middle_ref, out_ref):
    for group in range(4):
        at = slice(32 * group, 32 * group + 32)
        rows = (keep_ref[at] + got_ref[at].astype(F32)).reshape(4, 8, -1)
        middle = jnp.stack(
            [
                middle_ref[32 * f : 32 * f + 32].astype(F32)[8 * group : 8 * group + 8]
                for f in range(4)
            ],
            axis=0,
        )
        out = jnp.transpose(rows + middle, (1, 0, 2)).astype(BF)
        out_ref[8 * group : 8 * group + 8] = out


def end_rows(keep, got, middle):
    return pl.pallas_call(
        end_kernel,
        out_shape=jax.ShapeDtypeStruct((32, 4, middle.shape[1]), BF),
        in_specs=[vmem()] * 3,
        out_specs=vmem(),
        compiler_params=params(),
        cost_estimate=pl.CostEstimate(flops=1 << 20, bytes_accessed=3 << 20, transcendentals=0),
    )(keep, got, middle)


def shifted(value, axis, step):
    count = lax.axis_size(axis)
    return lax.ppermute(value, axis, [(i, (i + step) % count) for i in range(count)])


def gathered_rows(chunks):
    up, down = list(chunks), list(chunks)
    pieces = {0: list(chunks)}
    for step in (1, 2, 3):
        up = [shifted(value, "z", 1) for value in up]
        down = [shifted(value, "z", -1) for value in down]
        pieces[-step], pieces[step] = up, down
    pieces[4] = [shifted(up[0], "z", 1), shifted(down[1], "z", -1)]
    return [value for offset in OFFSETS for value in pieces[offset]]


def local(stream, spatial_gain, spatial_qkv, spatial_out, temporal_gain, temporal_qkv, temporal_out, starts):
    patches, frames, width = stream.shape
    w, xl, y, c, z = (lax.axis_index(name) for name in ("w", "xl", "y", "c", "z"))

    place = (((w * 2 + xl) * 2 + c) * 4 + y).reshape(1)
    first, second, rows = norm_rows(
        place, stream, spatial_gain.reshape(1, width), jnp.transpose(temporal_qkv, (1, 0, 2))
    )

    low = (lax.rem(y, 2) * E, ((w * 2 + xl) * 2 + y // 2) * 256)
    block = lax.dynamic_slice(spatial_out, low, (E, 256))
    parts = []
    for k in range(4):
        pairs = [
            (a * 8 + b, (b // 4) * 8 + (b + 4 * a + k) % 8) for a in range(2) for b in range(8)
        ]
        parts.append(lax.ppermute(block, ("c", "z"), pairs))
    first, second, parts = lax.optimization_barrier((first, second, parts))
    whole_out = join_blocks(z.reshape(1), parts)
    whole_out = lax.all_gather(whole_out, ("w", "xl", "y", "c"), axis=0, tiled=False)
    whole_out = whole_out.reshape(8, 2, 2, 4, E, 256)

    pieces = gathered_rows((first, second))

    sends = split_shares(jnp.stack([z, y]).astype(jnp.int32), pieces)
    got = [sends[0]] + [shifted(sends[k], "y", k) for k in range(1, 4)]

    weight = jnp.transpose(spatial_qkv, (1, 0, 2))
    pieces, whole_out = lax.optimization_barrier((pieces, whole_out))
    mix = spatial_attend(z.reshape(1), weight, pieces)
    _, *got = lax.optimization_barrier((mix, *got))
    quarter = join_shares(y.reshape(1), got)
    quarter = lax.all_gather(quarter[None], ("w", "xl", "c"), axis=0, tiled=True)
    mix = lax.all_to_all(mix, "z", 0, 0, tiled=True)

    middle, send = middle_rows(mix, whole_out, rows, temporal_gain.reshape(1, width))

    half = lax.dynamic_slice(temporal_out, (c * E, 0), (E, width))
    send, half = lax.optimization_barrier((send, half))
    up, down = half, half
    halves = [half]
    for step in (1, 2, 3):
        up, down = shifted(up, "z", 1), shifted(down, "z", -1)
        halves += [up, down]
    halves += [shifted(up[:64], "z", 1), shifted(down[64:], "z", -1)]

    window = lax.all_to_all(send, ("xl", "y", "c"), 0, 0, tiled=True)
    window, *halves[1:5] = lax.optimization_barrier((window, *halves[1:5]))
    start = lax.dynamic_slice(starts, (w,), (1,))
    mix = temporal_attend(start, window.reshape(512, width), quarter)
    mix = lax.all_to_all(mix, ("xl", "y", "c"), 0, 0, tiled=True)
    keep, give = last_sums(jnp.stack([z, c]).astype(jnp.int32), mix, halves)
    return end_rows(keep, shifted(give, "c", 1), middle)


def solution(mesh):
    names = ("w", "xl", "y", "c", "z")
    fine = Mesh(mesh.devices.reshape(2, 2, 4, 2, NZ), names)
    tm = ("w", "xl", "y", "c")
    placed = (
        P("z", tm, None),
        P(),
        P(None, None, "z"),
        P("z", None),
        P(),
        P(None, None, "z"),
        P("z", None),
        P(),
    )
    return jax.shard_map(
        local, mesh=fine, in_specs=placed, out_specs=P("z", tm, None), check_vma=False
    )
```

```python
import functools
import math

import jax
import jax.numpy as jnp
from jax import lax
from jax.experimental import pallas as pl
from jax.experimental.pallas import tpu as pltpu
from jax.sharding import Mesh
from jax.sharding import PartitionSpec as P

E = 128
SEQ = 64
SCALE = 1.0 / math.sqrt(E)
BF = jnp.bfloat16
F32 = jnp.float32
NZ = 8
VMEM_LIMIT = 28 * 1024 * 1024
OFFSETS = (0, -1, 1, -2, 2, -3, 3, 4)


def params():
    return pltpu.CompilerParams(vmem_limit_bytes=VMEM_LIMIT)


def vmem():
    return pl.BlockSpec(memory_space=pltpu.VMEM)


def smem():
    return pl.BlockSpec(memory_space=pltpu.SMEM)


def normed(values, gain):
    scaled = values * lax.rsqrt(jnp.mean(values * values, axis=-1, keepdims=True) + 1e-05)
    return (scaled * gain).astype(BF)


def softmax(scores):
    top = jnp.max(scores, axis=-1, keepdims=True)
    shifted = jnp.exp2((scores - top) * (SCALE * math.log2(math.e)))
    return (shifted * (1.0 / jnp.sum(shifted, axis=-1, keepdims=True))).astype(BF)


def dot(a, b):
    return jnp.dot(a, b, preferred_element_type=F32)


def dot_t(a, b):
    return lax.dot_general(a, b, (((1,), (1,)), ((), ())), preferred_element_type=F32)


def norm_kernel(place_ref, x_ref, gain_ref, qkv_ref, a_ref, b_ref, rows_ref):
    gain = gain_ref[...]
    values = jnp.transpose(x_ref[...].astype(F32), (1, 0, 2)).reshape(rows_ref.shape)
    half = rows_ref.shape[0] // 2
    rows_ref[...] = values.astype(BF)
    a_ref[:half] = normed(values[:half], gain)
    b_ref[:half] = normed(values[half:], gain)
    b_ref[half:, 1024:] = jnp.zeros((16, 1024), BF)
    for kind in range(3):
        share = qkv_ref[kind]
        ref = (a_ref, b_ref)[kind // 2]
        for group in range(4):
            low = 256 * (4 * (kind % 2) + group)
            ref[half:, low : low + 256] = share[16 * group : 16 * group + 16]


def norm_rows(place, stream, gain, temporal_qkv):
    patches, frames, width = stream.shape
    count = patches * frames
    half = jax.ShapeDtypeStruct((count // 2 + 16, width), BF)
    whole = lambda *shape: pl.BlockSpec(shape, lambda i, at: (0,) * len(shape))
    return pl.pallas_call(
        norm_kernel,
        grid_spec=pltpu.PrefetchScalarGridSpec(
            num_scalar_prefetch=1,
            grid=(1,),
            in_specs=[
                whole(patches, frames, width),
                whole(1, width),
                pl.BlockSpec((3, 64, 256), lambda i, at: (0, at[0], 0)),
            ],
            out_specs=(
                whole(count // 2 + 16, width),
                whole(count // 2 + 16, width),
                whole(count, width),
            ),
        ),
        out_shape=(half, half, jax.ShapeDtypeStruct((count, width), BF)),
        compiler_params=params(),
        cost_estimate=pl.CostEstimate(
            flops=4 * count * width, bytes_accessed=6 * count * width, transcendentals=0
        ),
    )(place, stream, gain, temporal_qkv)


def split_kernel(place_ref, *refs):
    pieces, sends = refs[:-4], refs[-4:]
    z, y = place_ref[0], place_ref[1]
    for k in range(NZ):
        source = lax.rem(z + (OFFSETS[k] + NZ), NZ)
        step = lax.rem(source // 2 + 4 - y, 4)
        pair = lax.rem(source, 2)
        for index, send_ref in enumerate(sends):

            @pl.when(step == index)
            def _():
                for kind in range(3):
                    for group in range(4):
                        low = 256 * (4 * (kind % 2) + group)
                        rows = slice(16 * group, 16 * group + 16)
                        value = pieces[2 * k + kind // 2][:, low : low + 256]
                        send_ref[pair, kind, rows] = value


def split_shares(place, pieces):
    return pl.pallas_call(
        split_kernel,
        grid=(1,),
        out_shape=(jax.ShapeDtypeStruct((2, 3, 64, 256), BF),) * 4,
        in_specs=[smem()] + [pl.BlockSpec((16, 2048), lambda i: (4, 0))] * len(pieces),
        out_specs=(pl.BlockSpec((2, 3, 64, 256), lambda i: (0, 0, 0, 0)),) * 4,
        compiler_params=params(),
        cost_estimate=pl.CostEstimate(flops=0, bytes_accessed=2 << 20, transcendentals=0),
    )(place, *pieces)


def join_kernel(y_ref, *refs):
    out_ref = refs[-1]
    for step in range(4):
        low = pl.multiple_of(64 * lax.rem(y_ref[0] + (4 - step), 4), 64)
        for pair in range(2):
            for kind in range(3):
                out_ref[3 * pair + kind, pl.ds(low, 64), :] = refs[step][pair, kind]


def join_shares(y, got):
    return pl.pallas_call(
        join_kernel,
        out_shape=jax.ShapeDtypeStruct((6, 256, 256), BF),
        in_specs=[smem()] + [vmem()] * 4,
        out_specs=vmem(),
        compiler_params=params(),
        cost_estimate=pl.CostEstimate(flops=0, bytes_accessed=2 << 20, transcendentals=0),
    )(y, *got)


def attend(chains):
    scores = [dot_t(query, key) for query, key, _, _ in chains]
    scores = [
        one if chain[3] is None else jnp.where(chain[3] < 0.0, chain[3], one)
        for one, chain in zip(scores, chains)
    ]
    weights = [softmax(one) for one in scores]
    return [dot(one, chain[2]).astype(BF) for one, chain in zip(weights, chains)]


def spatial_kernel(place_ref, weight_ref, *refs):
    pieces, out_ref, qkv = refs[: 2 * NZ], refs[2 * NZ], refs[2 * NZ + 1]
    place = place_ref[0]
    for frame in range(4):
        low = 32 * (frame % 2)
        rows = jnp.concatenate(
            [pieces[2 * k + frame // 2][low : low + 32, :] for k in range(NZ)], axis=0
        )
        for kind in range(3):
            qkv[kind, 256 * frame : 256 * frame + 256] = dot(rows, weight_ref[kind]).astype(BF)
    for frames in ((0, 1), (2, 3)):
        spots = [(frame, head * E) for frame in frames for head in range(2)]
        chains = []
        for frame, low in spots:
            at, cols = slice(256 * frame, 256 * frame + 256), slice(low, low + E)
            chains.append((qkv[0, at, cols], qkv[1, at, cols], qkv[2, at, cols], None))
        for (frame, low), mixed in zip(spots, attend(chains)):
            for k in range(NZ):
                target = lax.rem(place + (OFFSETS[k] + NZ), NZ)
                out_ref[target, 32 * frame : 32 * frame + 32, low : low + E] = mixed[
                    32 * k : 32 * k + 32
                ]


def spatial_attend(place, weight, pieces):
    return pl.pallas_call(
        spatial_kernel,
        out_shape=jax.ShapeDtypeStruct((NZ, 128, 256), BF),
        in_specs=[smem(), vmem()] + [vmem()] * len(pieces),
        out_specs=vmem(),
        scratch_shapes=[pltpu.VMEM((3, 1024, 256), BF)],
        compiler_params=params(),
        cost_estimate=pl.CostEstimate(
            flops=2 * 1024 * 2048 * 768 * 2, bytes_accessed=8 << 20, transcendentals=8 * 65536
        ),
    )(place, weight, *pieces)


def column_block(read):
    return jnp.concatenate([read(head, k // 4, k % 4) for k in range(NZ) for head in range(2)], axis=0)


def join_blocks_kernel(z_ref, *refs):
    out_ref = refs[-1]
    for step in range(4):
        out_ref[lax.rem(z_ref[0] + (4 - step), 4)] = refs[step][...]


def join_blocks(z, parts):
    return pl.pallas_call(
        join_blocks_kernel,
        out_shape=jax.ShapeDtypeStruct((4, 128, 256), BF),
        in_specs=[smem()] + [vmem()] * 4,
        out_specs=vmem(),
        compiler_params=params(),
        cost_estimate=pl.CostEstimate(flops=0, bytes_accessed=512 << 10, transcendentals=0),
    )(z, *parts)


def middle_kernel(mix_ref, weight_ref, rows_ref, gain_ref, middle_ref, send_ref, total):
    mix = jnp.concatenate([mix_ref[k] for k in range(NZ)], axis=1)
    for block in range(8):
        part = column_block(lambda *at: weight_ref[(block, *at)])
        total[:, 256 * block : 256 * block + 256] = dot(mix, part)
    middle = (total[...] + rows_ref[...].astype(F32)).astype(BF)
    middle_ref[...] = middle
    values = middle.astype(F32)
    scaled = values * lax.rsqrt(jnp.mean(values * values, axis=-1, keepdims=True) + 1e-05)
    scaled = scaled * gain_ref[...]
    for group in range(4):
        chunk = jnp.concatenate(
            [scaled[32 * f + 8 * group : 32 * f + 8 * group + 8] for f in range(4)], axis=0
        ).astype(BF)
        for y in range(4):
            send_ref[(group // 2) * 8 + y * 2 + group % 2] = chunk


def middle_rows(mix, weight, rows, gain):
    width = rows.shape[1]
    return pl.pallas_call(
        middle_kernel,
        out_shape=(
            jax.ShapeDtypeStruct((128, width), BF),
            jax.ShapeDtypeStruct((16, 32, width), BF),
        ),
        in_specs=[vmem()] * 4,
        out_specs=(vmem(), vmem()),
        scratch_shapes=[pltpu.VMEM((128, width), F32)],
        compiler_params=params(),
        cost_estimate=pl.CostEstimate(
            flops=2 * 128 * 2048 * 2048, bytes_accessed=12 << 20, transcendentals=0
        ),
    )(mix, weight, rows, gain)


def temporal_kernel(start_ref, rows_ref, weight_ref, out_ref, qkv, bias):
    count = rows_ref.shape[0]
    start = start_ref[0]
    late = lax.broadcasted_iota(jnp.int32, (count, count), 0)
    early = lax.broadcasted_iota(jnp.int32, (count, count), 1)
    same = (late & 7) == (early & 7)
    allowed = same & (early <= late) & ((early >= 8 * start) == (late >= 8 * start))
    bias[...] = jnp.where(allowed, 0.0, -1e30)
    for block in range(6):
        qkv[block] = dot(rows_ref[...], weight_ref[:, block].reshape(2048, 256)).astype(BF)
    size = 256
    for pair in range(2):
        for low in range(0, count, size):
            chains = []
            high = low + size
            for head in range(2):
                cols = slice(head * E, head * E + E)
                chains.append(
                    (
                        qkv[3 * pair, low:high, cols],
                        qkv[3 * pair + 1, :high, cols],
                        qkv[3 * pair + 2, :high, cols],
                        bias[low:high, :high],
                    )
                )
            for head, mixed in enumerate(attend(chains)):
                for spot in range(low // 32, high // 32):
                    rows = mixed[32 * spot - low : 32 * spot - low + 32]
                    at = (spot // 2 * 2 + head, spot % 2, slice(None), slice(E * pair, E * pair + E))
                    out_ref[at] = rows


def temporal_attend(start, rows, weight):
    count, width = rows.shape
    return pl.pallas_call(
        temporal_kernel,
        out_shape=jax.ShapeDtypeStruct((16, 2, 32, 256), BF),
        in_specs=[smem(), vmem(), vmem()],
        out_specs=vmem(),
        scratch_shapes=[
            pltpu.VMEM((6, count, 256), BF),
            pltpu.VMEM((count, count), F32),
        ],
        compiler_params=params(),
        cost_estimate=pl.CostEstimate(
            flops=2 * 512 * 2048 * 1536, bytes_accessed=9 << 20, transcendentals=131072
        ),
    )(start, rows, weight)


def last_kernel(place_ref, mix_ref, *refs):
    pieces, (keep_ref, give_ref, total, weight, sems) = refs[: NZ + 1], refs[NZ + 1 :]
    z, c = place_ref[0], place_ref[1]
    copies = []
    for index, piece in enumerate(pieces):
        low = E * index if index < NZ else E * NZ - E // 2
        rows = weight.at[pl.ds(low, piece.shape[0])]
        copies.append(pltpu.make_async_copy(piece, rows, sems.at[index]))
        copies[-1].start()
    blocks = []
    for k in range(NZ):
        source = lax.rem(z + (OFFSETS[k] + NZ), NZ)
        cols = pl.ds(pl.multiple_of(lax.rem(source, 2) * E, E), E)
        blocks.append(
            jnp.concatenate(
                [
                    mix_ref[xl * 8 + source // 2 * 2 + core, frames, :, cols]
                    for frames in range(2)
                    for xl in range(2)
                    for core in range(2)
                ],
                axis=0,
            )
        )
    mix = jnp.concatenate(blocks, axis=1)
    for copy in copies:
        copy.wait()
    for low in range(0, 2048, 512):
        total[:, :, low : low + 512] = dot(mix, weight[:, low : low + 512]).reshape(2, 128, 512)
    keep_ref[...] = total[c]
    give_ref[...] = total[1 - c].astype(BF)


def last_sums(place, mix, pieces):
    width = pieces[0].shape[1]
    return pl.pallas_call(
        last_kernel,
        out_shape=(
            jax.ShapeDtypeStruct((128, width), F32),
            jax.ShapeDtypeStruct((128, width), BF),
        ),
        in_specs=[smem(), vmem()] + [pl.BlockSpec(memory_space=pltpu.HBM)] * (NZ + 1),
        out_specs=(vmem(), vmem()),
        scratch_shapes=[
            pltpu.VMEM((2, 128, width), F32),
            pltpu.VMEM((E * NZ, width), BF),
            pltpu.SemaphoreType.DMA((NZ + 1,)),
        ],
        compiler_params=params(),
        cost_estimate=pl.CostEstimate(
            flops=2 * 128 * 2048 * 2048, bytes_accessed=8 << 20, transcendentals=0
        ),
    )(place, mix, *pieces)


def end_kernel(keep_ref, got_ref, middle_ref, out_ref):
    for group in range(4):
        at = slice(32 * group, 32 * group + 32)
        rows = (keep_ref[at] + got_ref[at].astype(F32)).reshape(4, 8, -1)
        middle = jnp.stack(
            [
                middle_ref[32 * f : 32 * f + 32].astype(F32)[8 * group : 8 * group + 8]
                for f in range(4)
            ],
            axis=0,
        )
        out = jnp.transpose(rows + middle, (1, 0, 2)).astype(BF)
        out_ref[8 * group : 8 * group + 8] = out


def end_rows(keep, got, middle):
    return pl.pallas_call(
        end_kernel,
        out_shape=jax.ShapeDtypeStruct((32, 4, middle.shape[1]), BF),
        in_specs=[vmem()] * 3,
        out_specs=vmem(),
        compiler_params=params(),
        cost_estimate=pl.CostEstimate(flops=1 << 20, bytes_accessed=3 << 20, transcendentals=0),
    )(keep, got, middle)


def shifted(value, axis, step):
    count = lax.axis_size(axis)
    return lax.ppermute(value, axis, [(i, (i + step) % count) for i in range(count)])


def gathered_rows(chunks):
    up, down = list(chunks), list(chunks)
    pieces = {0: list(chunks)}
    for step in (1, 2, 3):
        up = [shifted(value, "z", 1) for value in up]
        down = [shifted(value, "z", -1) for value in down]
        pieces[-step], pieces[step] = up, down
    pieces[4] = [shifted(up[0], "z", 1), shifted(down[1], "z", -1)]
    return [value for offset in OFFSETS for value in pieces[offset]]


def local(stream, spatial_gain, spatial_qkv, spatial_out, temporal_gain, temporal_qkv, temporal_out, starts):
    patches, frames, width = stream.shape
    w, xl, y, c, z = (lax.axis_index(name) for name in ("w", "xl", "y", "c", "z"))

    place = (((w * 2 + xl) * 2 + c) * 4 + y).reshape(1)
    first, second, rows = norm_rows(
        place, stream, spatial_gain.reshape(1, width), jnp.transpose(temporal_qkv, (1, 0, 2))
    )

    low = (lax.rem(y, 2) * E, ((w * 2 + xl) * 2 + y // 2) * 256)
    block = lax.dynamic_slice(spatial_out, low, (E, 256))
    parts = []
    for k in range(4):
        pairs = [
            (a * 8 + b, (b // 4) * 8 + (b + 4 * a + k) % 8) for a in range(2) for b in range(8)
        ]
        parts.append(lax.ppermute(block, ("c", "z"), pairs))
    first, second, parts = lax.optimization_barrier((first, second, parts))
    whole_out = join_blocks(z.reshape(1), parts)
    whole_out = lax.all_gather(whole_out, ("w", "xl", "y", "c"), axis=0, tiled=False)
    whole_out = whole_out.reshape(8, 2, 2, 4, E, 256)

    pieces = gathered_rows((first, second))

    sends = split_shares(jnp.stack([z, y]).astype(jnp.int32), pieces)
    got = [sends[0]] + [shifted(sends[k], "y", k) for k in range(1, 4)]

    weight = jnp.transpose(spatial_qkv, (1, 0, 2))
    mix = spatial_attend(z.reshape(1), weight, pieces)
    mix, *got = lax.optimization_barrier((mix, *got))
    quarter = join_shares(y.reshape(1), got)
    mix, quarter, whole_out = lax.optimization_barrier((mix, quarter, whole_out))
    quarter = lax.all_gather(quarter[None], ("w", "xl", "c"), axis=0, tiled=True)
    mix = lax.all_to_all(mix, "z", 0, 0, tiled=True)

    middle, send = middle_rows(mix, whole_out, rows, temporal_gain.reshape(1, width))

    half = lax.dynamic_slice(temporal_out, (c * E, 0), (E, width))
    send, half = lax.optimization_barrier((send, half))
    up, down = half, half
    halves = [half]
    for step in (1, 2, 3):
        up, down = shifted(up, "z", 1), shifted(down, "z", -1)
        halves += [up, down]
    halves += [shifted(up[:64], "z", 1), shifted(down[64:], "z", -1)]

    window = lax.all_to_all(send, ("xl", "y", "c"), 0, 0, tiled=True)
    window, *halves[1:5] = lax.optimization_barrier((window, *halves[1:5]))
    start = lax.dynamic_slice(starts, (w,), (1,))
    mix = temporal_attend(start, window.reshape(512, width), quarter)
    mix = lax.all_to_all(mix, ("xl", "y", "c"), 0, 0, tiled=True)
    keep, give = last_sums(jnp.stack([z, c]).astype(jnp.int32), mix, halves)
    return end_rows(keep, shifted(give, "c", 1), middle)


def solution(mesh):
    names = ("w", "xl", "y", "c", "z")
    fine = Mesh(mesh.devices.reshape(2, 2, 4, 2, NZ), names)
    tm = ("w", "xl", "y", "c")
    placed = (
        P("z", tm, None),
        P(),
        P(None, None, "z"),
        P("z", None),
        P(),
        P(None, None, "z"),
        P("z", None),
        P(),
    )
    return jax.shard_map(
        local, mesh=fine, in_specs=placed, out_specs=P("z", tm, None), check_vma=False
    )
```

```python
import functools
import math

import jax
import jax.numpy as jnp
from jax import lax
from jax.experimental import pallas as pl
from jax.experimental.pallas import tpu as pltpu
from jax.sharding import Mesh
from jax.sharding import PartitionSpec as P

E = 128
SEQ = 64
SCALE = 1.0 / math.sqrt(E)
BF = jnp.bfloat16
F32 = jnp.float32
NZ = 8
VMEM_LIMIT = 28 * 1024 * 1024
OFFSETS = (0, -1, 1, -2, 2, -3, 3, 4)


def params():
    return pltpu.CompilerParams(vmem_limit_bytes=VMEM_LIMIT)


def vmem():
    return pl.BlockSpec(memory_space=pltpu.VMEM)


def smem():
    return pl.BlockSpec(memory_space=pltpu.SMEM)


def normed(values, gain):
    scaled = values * lax.rsqrt(jnp.mean(values * values, axis=-1, keepdims=True) + 1e-05)
    return (scaled * gain).astype(BF)


def softmax(scores):
    top = jnp.max(scores, axis=-1, keepdims=True)
    shifted = jnp.exp2((scores - top) * (SCALE * math.log2(math.e)))
    return (shifted * (1.0 / jnp.sum(shifted, axis=-1, keepdims=True))).astype(BF)


def dot(a, b):
    return jnp.dot(a, b, preferred_element_type=F32)


def dot_t(a, b):
    return lax.dot_general(a, b, (((1,), (1,)), ((), ())), preferred_element_type=F32)


def norm_kernel(place_ref, x_ref, gain_ref, qkv_ref, a_ref, b_ref, rows_ref):
    gain = gain_ref[...]
    values = jnp.transpose(x_ref[...].astype(F32), (1, 0, 2)).reshape(rows_ref.shape)
    half = rows_ref.shape[0] // 2
    rows_ref[...] = values.astype(BF)
    a_ref[:half] = normed(values[:half], gain)
    b_ref[:half] = normed(values[half:], gain)
    b_ref[half:, 1024:] = jnp.zeros((16, 1024), BF)
    for kind in range(3):
        share = qkv_ref[kind]
        ref = (a_ref, b_ref)[kind // 2]
        for group in range(4):
            low = 256 * (4 * (kind % 2) + group)
            ref[half:, low : low + 256] = share[16 * group : 16 * group + 16]


def norm_rows(place, stream, gain, temporal_qkv):
    patches, frames, width = stream.shape
    count = patches * frames
    half = jax.ShapeDtypeStruct((count // 2 + 16, width), BF)
    whole = lambda *shape: pl.BlockSpec(shape, lambda i, at: (0,) * len(shape))
    return pl.pallas_call(
        norm_kernel,
        grid_spec=pltpu.PrefetchScalarGridSpec(
            num_scalar_prefetch=1,
            grid=(1,),
            in_specs=[
                whole(patches, frames, width),
                whole(1, width),
                pl.BlockSpec((3, 64, 256), lambda i, at: (0, at[0], 0)),
            ],
            out_specs=(
                whole(count // 2 + 16, width),
                whole(count // 2 + 16, width),
                whole(count, width),
            ),
        ),
        out_shape=(half, half, jax.ShapeDtypeStruct((count, width), BF)),
        compiler_params=params(),
        cost_estimate=pl.CostEstimate(
            flops=4 * count * width, bytes_accessed=6 * count * width, transcendentals=0
        ),
    )(place, stream, gain, temporal_qkv)


def split_kernel(place_ref, *refs):
    pieces, sends = refs[:-4], refs[-4:]
    z, y = place_ref[0], place_ref[1]
    for k in range(NZ):
        source = lax.rem(z + (OFFSETS[k] + NZ), NZ)
        step = lax.rem(source // 2 + 4 - y, 4)
        pair = lax.rem(source, 2)
        for index, send_ref in enumerate(sends):

            @pl.when(step == index)
            def _():
                for kind in range(3):
                    for group in range(4):
                        low = 256 * (4 * (kind % 2) + group)
                        rows = slice(16 * group, 16 * group + 16)
                        value = pieces[2 * k + kind // 2][:, low : low + 256]
                        send_ref[pair, kind, rows] = value


def split_shares(place, pieces):
    return pl.pallas_call(
        split_kernel,
        grid=(1,),
        out_shape=(jax.ShapeDtypeStruct((2, 3, 64, 256), BF),) * 4,
        in_specs=[smem()] + [pl.BlockSpec((16, 2048), lambda i: (4, 0))] * len(pieces),
        out_specs=(pl.BlockSpec((2, 3, 64, 256), lambda i: (0, 0, 0, 0)),) * 4,
        compiler_params=params(),
        cost_estimate=pl.CostEstimate(flops=0, bytes_accessed=2 << 20, transcendentals=0),
    )(place, *pieces)


def join_kernel(y_ref, *refs):
    out_ref = refs[-1]
    for step in range(4):
        low = pl.multiple_of(64 * lax.rem(y_ref[0] + (4 - step), 4), 64)
        for pair in range(2):
            for kind in range(3):
                out_ref[3 * pair + kind, pl.ds(low, 64), :] = refs[step][pair, kind]


def join_shares(y, got):
    return pl.pallas_call(
        join_kernel,
        out_shape=jax.ShapeDtypeStruct((6, 256, 256), BF),
        in_specs=[smem()] + [vmem()] * 4,
        out_specs=vmem(),
        compiler_params=params(),
        cost_estimate=pl.CostEstimate(flops=0, bytes_accessed=2 << 20, transcendentals=0),
    )(y, *got)


def attend(chains):
    scores = [dot_t(query, key) for query, key, _, _ in chains]
    scores = [
        one if chain[3] is None else jnp.where(chain[3] < 0.0, chain[3], one)
        for one, chain in zip(scores, chains)
    ]
    weights = [softmax(one) for one in scores]
    return [dot(one, chain[2]).astype(BF) for one, chain in zip(weights, chains)]


def spatial_kernel(place_ref, weight_ref, *refs):
    pieces, out_ref, qkv = refs[: 2 * NZ], refs[2 * NZ], refs[2 * NZ + 1]
    place = place_ref[0]
    for frame in range(4):
        low = 32 * (frame % 2)
        rows = jnp.concatenate(
            [pieces[2 * k + frame // 2][low : low + 32, :] for k in range(NZ)], axis=0
        )
        for kind in range(3):
            qkv[kind, 256 * frame : 256 * frame + 256] = dot(rows, weight_ref[kind]).astype(BF)
    for frames in ((0, 1), (2, 3)):
        spots = [(frame, head * E) for frame in frames for head in range(2)]
        chains = []
        for frame, low in spots:
            at, cols = slice(256 * frame, 256 * frame + 256), slice(low, low + E)
            chains.append((qkv[0, at, cols], qkv[1, at, cols], qkv[2, at, cols], None))
        for (frame, low), mixed in zip(spots, attend(chains)):
            for k in range(NZ):
                target = lax.rem(place + (OFFSETS[k] + NZ), NZ)
                out_ref[target, 32 * frame : 32 * frame + 32, low : low + E] = mixed[
                    32 * k : 32 * k + 32
                ]


def spatial_attend(place, weight, pieces):
    return pl.pallas_call(
        spatial_kernel,
        out_shape=jax.ShapeDtypeStruct((NZ, 128, 256), BF),
        in_specs=[smem(), vmem()] + [vmem()] * len(pieces),
        out_specs=vmem(),
        scratch_shapes=[pltpu.VMEM((3, 1024, 256), BF)],
        compiler_params=params(),
        cost_estimate=pl.CostEstimate(
            flops=2 * 1024 * 2048 * 768 * 2, bytes_accessed=8 << 20, transcendentals=8 * 65536
        ),
    )(place, weight, *pieces)


def column_block(read):
    return jnp.concatenate([read(head, k // 4, k % 4) for k in range(NZ) for head in range(2)], axis=0)


def join_blocks_kernel(z_ref, *refs):
    out_ref = refs[-1]
    for step in range(4):
        out_ref[lax.rem(z_ref[0] + (4 - step), 4)] = refs[step][...]


def join_blocks(z, parts):
    return pl.pallas_call(
        join_blocks_kernel,
        out_shape=jax.ShapeDtypeStruct((4, 128, 256), BF),
        in_specs=[smem()] + [vmem()] * 4,
        out_specs=vmem(),
        compiler_params=params(),
        cost_estimate=pl.CostEstimate(flops=0, bytes_accessed=512 << 10, transcendentals=0),
    )(z, *parts)


def middle_kernel(mix_ref, weight_ref, rows_ref, gain_ref, middle_ref, send_ref, total):
    mix = jnp.concatenate([mix_ref[k] for k in range(NZ)], axis=1)
    for block in range(8):
        part = column_block(lambda *at: weight_ref[(block, *at)])
        total[:, 256 * block : 256 * block + 256] = dot(mix, part)
    middle = (total[...] + rows_ref[...].astype(F32)).astype(BF)
    middle_ref[...] = middle
    values = middle.astype(F32)
    scaled = values * lax.rsqrt(jnp.mean(values * values, axis=-1, keepdims=True) + 1e-05)
    scaled = scaled * gain_ref[...]
    for group in range(4):
        chunk = jnp.concatenate(
            [scaled[32 * f + 8 * group : 32 * f + 8 * group + 8] for f in range(4)], axis=0
        ).astype(BF)
        for y in range(4):
            send_ref[(group // 2) * 8 + y * 2 + group % 2] = chunk


def middle_rows(mix, weight, rows, gain):
    width = rows.shape[1]
    return pl.pallas_call(
        middle_kernel,
        out_shape=(
            jax.ShapeDtypeStruct((128, width), BF),
            jax.ShapeDtypeStruct((16, 32, width), BF),
        ),
        in_specs=[vmem()] * 4,
        out_specs=(vmem(), vmem()),
        scratch_shapes=[pltpu.VMEM((128, width), F32)],
        compiler_params=params(),
        cost_estimate=pl.CostEstimate(
            flops=2 * 128 * 2048 * 2048, bytes_accessed=12 << 20, transcendentals=0
        ),
    )(mix, weight, rows, gain)


def temporal_kernel(start_ref, rows_ref, weight_ref, out_ref, qkv, bias):
    count = rows_ref.shape[0]
    start = start_ref[0]
    late = lax.broadcasted_iota(jnp.int32, (count, count), 0)
    early = lax.broadcasted_iota(jnp.int32, (count, count), 1)
    same = (late & 7) == (early & 7)
    allowed = same & (early <= late) & ((early >= 8 * start) == (late >= 8 * start))
    bias[...] = jnp.where(allowed, 0.0, -1e30)
    for block in range(6):
        qkv[block] = dot(rows_ref[...], weight_ref[:, block].reshape(2048, 256)).astype(BF)
    size = 256
    for pair in range(2):
        for low in range(0, count, size):
            chains = []
            high = low + size
            for head in range(2):
                cols = slice(head * E, head * E + E)
                chains.append(
                    (
                        qkv[3 * pair, low:high, cols],
                        qkv[3 * pair + 1, :high, cols],
                        qkv[3 * pair + 2, :high, cols],
                        bias[low:high, :high],
                    )
                )
            for head, mixed in enumerate(attend(chains)):
                for spot in range(low // 32, high // 32):
                    rows = mixed[32 * spot - low : 32 * spot - low + 32]
                    at = (spot // 2 * 2 + head, spot % 2, slice(None), slice(E * pair, E * pair + E))
                    out_ref[at] = rows


def temporal_attend(start, rows, weight):
    count, width = rows.shape
    return pl.pallas_call(
        temporal_kernel,
        out_shape=jax.ShapeDtypeStruct((16, 2, 32, 256), BF),
        in_specs=[smem(), vmem(), vmem()],
        out_specs=vmem(),
        scratch_shapes=[
            pltpu.VMEM((6, count, 256), BF),
            pltpu.VMEM((count, count), F32),
        ],
        compiler_params=params(),
        cost_estimate=pl.CostEstimate(
            flops=2 * 512 * 2048 * 1536, bytes_accessed=9 << 20, transcendentals=131072
        ),
    )(start, rows, weight)


def last_kernel(place_ref, mix_ref, *refs):
    pieces, (keep_ref, give_ref, total) = refs[: NZ + 1], refs[NZ + 1 :]
    z, c = place_ref[0], place_ref[1]
    blocks = []
    for k in range(NZ):
        source = lax.rem(z + (OFFSETS[k] + NZ), NZ)
        cols = pl.ds(pl.multiple_of(lax.rem(source, 2) * E, E), E)
        blocks.append(
            jnp.concatenate(
                [
                    mix_ref[xl * 8 + source // 2 * 2 + core, frames, :, cols]
                    for frames in range(2)
                    for xl in range(2)
                    for core in range(2)
                ],
                axis=0,
            )
        )
    mix = jnp.concatenate(blocks, axis=1)
    for low in range(0, 2048, 512):
        part = jnp.concatenate([piece[:, low : low + 512] for piece in pieces], axis=0)
        total[:, :, low : low + 512] = dot(mix, part).reshape(2, 128, 512)
    keep_ref[...] = total[c]
    give_ref[...] = total[1 - c].astype(BF)


def last_sums(place, mix, pieces):
    width = pieces[0].shape[1]
    return pl.pallas_call(
        last_kernel,
        out_shape=(
            jax.ShapeDtypeStruct((128, width), F32),
            jax.ShapeDtypeStruct((128, width), BF),
        ),
        in_specs=[smem()] + [vmem()] * (NZ + 2),
        out_specs=(vmem(), vmem()),
        scratch_shapes=[pltpu.VMEM((2, 128, width), F32)],
        compiler_params=params(),
        cost_estimate=pl.CostEstimate(
            flops=2 * 128 * 2048 * 2048, bytes_accessed=8 << 20, transcendentals=0
        ),
    )(place, mix, *pieces)


def end_kernel(keep_ref, got_ref, middle_ref, out_ref):
    for group in range(4):
        at = slice(32 * group, 32 * group + 32)
        rows = (keep_ref[at] + got_ref[at].astype(F32)).reshape(4, 8, -1)
        middle = jnp.stack(
            [
                middle_ref[32 * f : 32 * f + 32].astype(F32)[8 * group : 8 * group + 8]
                for f in range(4)
            ],
            axis=0,
        )
        out = jnp.transpose(rows + middle, (1, 0, 2)).astype(BF)
        out_ref[8 * group : 8 * group + 8] = out


def end_rows(keep, got, middle):
    return pl.pallas_call(
        end_kernel,
        out_shape=jax.ShapeDtypeStruct((32, 4, middle.shape[1]), BF),
        in_specs=[vmem()] * 3,
        out_specs=vmem(),
        compiler_params=params(),
        cost_estimate=pl.CostEstimate(flops=1 << 20, bytes_accessed=3 << 20, transcendentals=0),
    )(keep, got, middle)


def shifted(value, axis, step):
    count = lax.axis_size(axis)
    return lax.ppermute(value, axis, [(i, (i + step) % count) for i in range(count)])


def gathered_rows(chunks):
    up, down = list(chunks), list(chunks)
    pieces = {0: list(chunks)}
    for step in (1, 2, 3):
        up = [shifted(value, "z", 1) for value in up]
        down = [shifted(value, "z", -1) for value in down]
        pieces[-step], pieces[step] = up, down
    pieces[4] = [shifted(up[0], "z", 1), shifted(down[1], "z", -1)]
    return [value for offset in OFFSETS for value in pieces[offset]]


def local(stream, spatial_gain, spatial_qkv, spatial_out, temporal_gain, temporal_qkv, temporal_out, starts):
    patches, frames, width = stream.shape
    w, xl, y, c, z = (lax.axis_index(name) for name in ("w", "xl", "y", "c", "z"))

    place = (((w * 2 + xl) * 2 + c) * 4 + y).reshape(1)
    first, second, rows = norm_rows(
        place, stream, spatial_gain.reshape(1, width), jnp.transpose(temporal_qkv, (1, 0, 2))
    )

    low = (lax.rem(y, 2) * E, ((w * 2 + xl) * 2 + y // 2) * 256)
    block = lax.dynamic_slice(spatial_out, low, (E, 256))
    parts = []
    for k in range(4):
        pairs = [
            (a * 8 + b, (b // 4) * 8 + (b + 4 * a + k) % 8) for a in range(2) for b in range(8)
        ]
        parts.append(lax.ppermute(block, ("c", "z"), pairs))
    first, second, parts = lax.optimization_barrier((first, second, parts))
    whole_out = join_blocks(z.reshape(1), parts)
    whole_out = lax.all_gather(whole_out, ("w", "xl", "y", "c"), axis=0, tiled=False)
    whole_out = whole_out.reshape(8, 2, 2, 4, E, 256)

    pieces = gathered_rows((first, second))

    sends = split_shares(jnp.stack([z, y]).astype(jnp.int32), pieces)
    got = [sends[0]] + [shifted(sends[k], "y", k) for k in range(1, 4)]

    weight = jnp.transpose(spatial_qkv, (1, 0, 2))
    mix = spatial_attend(z.reshape(1), weight, pieces)
    mix, *got = lax.optimization_barrier((mix, *got))
    quarter = join_shares(y.reshape(1), got)
    mix, quarter, whole_out = lax.optimization_barrier((mix, quarter, whole_out))
    quarter = lax.all_gather(quarter[None], ("w", "xl", "c"), axis=0, tiled=True)
    mix = lax.all_to_all(mix, "z", 0, 0, tiled=True)

    middle, send = middle_rows(mix, whole_out, rows, temporal_gain.reshape(1, width))

    half = lax.dynamic_slice(temporal_out, (c * E, 0), (E, width))
    send, half = lax.optimization_barrier((send, half))
    up, down = half, half
    halves = [half]
    for step in (1, 2, 3):
        up, down = shifted(up, "z", 1), shifted(down, "z", -1)
        if step == 1:
            up, down, quarter = lax.optimization_barrier((up, down, quarter))
        halves += [up, down]
    halves += [shifted(up[:64], "z", 1), shifted(down[64:], "z", -1)]

    window = lax.all_to_all(send, ("xl", "y", "c"), 0, 0, tiled=True)
    window, *halves[1:5] = lax.optimization_barrier((window, *halves[1:5]))
    start = lax.dynamic_slice(starts, (w,), (1,))
    mix = temporal_attend(start, window.reshape(512, width), quarter)
    mix = lax.all_to_all(mix, ("xl", "y", "c"), 0, 0, tiled=True)
    keep, give = last_sums(jnp.stack([z, c]).astype(jnp.int32), mix, halves)
    return end_rows(keep, shifted(give, "c", 1), middle)


def solution(mesh):
    names = ("w", "xl", "y", "c", "z")
    fine = Mesh(mesh.devices.reshape(2, 2, 4, 2, NZ), names)
    tm = ("w", "xl", "y", "c")
    placed = (
        P("z", tm, None),
        P(),
        P(None, None, "z"),
        P("z", None),
        P(),
        P(None, None, "z"),
        P("z", None),
        P(),
    )
    return jax.shard_map(
        local, mesh=fine, in_specs=placed, out_specs=P("z", tm, None), check_vma=False
    )
```

```python
import functools
import math

import jax
import jax.numpy as jnp
from jax import lax
from jax.experimental import pallas as pl
from jax.experimental.pallas import tpu as pltpu
from jax.sharding import Mesh
from jax.sharding import PartitionSpec as P

E = 128
SEQ = 64
SCALE = 1.0 / math.sqrt(E)
BF = jnp.bfloat16
F32 = jnp.float32
NZ = 8
VMEM_LIMIT = 28 * 1024 * 1024
OFFSETS = (0, -1, 1, -2, 2, -3, 3, 4)


def params():
    return pltpu.CompilerParams(vmem_limit_bytes=VMEM_LIMIT)


def vmem():
    return pl.BlockSpec(memory_space=pltpu.VMEM)


def smem():
    return pl.BlockSpec(memory_space=pltpu.SMEM)


def normed(values, gain):
    scaled = values * lax.rsqrt(jnp.mean(values * values, axis=-1, keepdims=True) + 1e-05)
    return (scaled * gain).astype(BF)


def softmax(scores):
    top = jnp.max(scores, axis=-1, keepdims=True)
    shifted = jnp.exp2((scores - top) * (SCALE * math.log2(math.e)))
    return (shifted * (1.0 / jnp.sum(shifted, axis=-1, keepdims=True))).astype(BF)


def dot(a, b):
    return jnp.dot(a, b, preferred_element_type=F32)


def dot_t(a, b):
    return lax.dot_general(a, b, (((1,), (1,)), ((), ())), preferred_element_type=F32)


def norm_kernel(place_ref, x_ref, gain_ref, qkv_ref, a_ref, b_ref, rows_ref):
    gain = gain_ref[...]
    values = jnp.transpose(x_ref[...].astype(F32), (1, 0, 2)).reshape(rows_ref.shape)
    half = rows_ref.shape[0] // 2
    rows_ref[...] = values.astype(BF)
    a_ref[:half] = normed(values[:half], gain)
    b_ref[:half] = normed(values[half:], gain)
    b_ref[half:, 1024:] = jnp.zeros((16, 1024), BF)
    for kind in range(3):
        share = qkv_ref[kind]
        ref = (a_ref, b_ref)[kind // 2]
        for group in range(4):
            low = 256 * (4 * (kind % 2) + group)
            ref[half:, low : low + 256] = share[16 * group : 16 * group + 16]


def norm_rows(place, stream, gain, temporal_qkv):
    patches, frames, width = stream.shape
    count = patches * frames
    half = jax.ShapeDtypeStruct((count // 2 + 16, width), BF)
    whole = lambda *shape: pl.BlockSpec(shape, lambda i, at: (0,) * len(shape))
    return pl.pallas_call(
        norm_kernel,
        grid_spec=pltpu.PrefetchScalarGridSpec(
            num_scalar_prefetch=1,
            grid=(1,),
            in_specs=[
                whole(patches, frames, width),
                whole(1, width),
                pl.BlockSpec((3, 64, 256), lambda i, at: (0, at[0], 0)),
            ],
            out_specs=(
                whole(count // 2 + 16, width),
                whole(count // 2 + 16, width),
                whole(count, width),
            ),
        ),
        out_shape=(half, half, jax.ShapeDtypeStruct((count, width), BF)),
        compiler_params=params(),
        cost_estimate=pl.CostEstimate(
            flops=4 * count * width, bytes_accessed=6 * count * width, transcendentals=0
        ),
    )(place, stream, gain, temporal_qkv)


def split_kernel(place_ref, *refs):
    pieces, sends = refs[:-4], refs[-4:]
    z, y = place_ref[0], place_ref[1]
    for k in range(NZ):
        source = lax.rem(z + (OFFSETS[k] + NZ), NZ)
        step = lax.rem(source // 2 + 4 - y, 4)
        pair = lax.rem(source, 2)
        for index, send_ref in enumerate(sends):

            @pl.when(step == index)
            def _():
                for kind in range(3):
                    for group in range(4):
                        low = 256 * (4 * (kind % 2) + group)
                        rows = slice(16 * group, 16 * group + 16)
                        value = pieces[2 * k + kind // 2][:, low : low + 256]
                        send_ref[pair, kind, rows] = value


def split_shares(place, pieces):
    return pl.pallas_call(
        split_kernel,
        grid=(1,),
        out_shape=(jax.ShapeDtypeStruct((2, 3, 64, 256), BF),) * 4,
        in_specs=[smem()] + [pl.BlockSpec((16, 2048), lambda i: (4, 0))] * len(pieces),
        out_specs=(pl.BlockSpec((2, 3, 64, 256), lambda i: (0, 0, 0, 0)),) * 4,
        compiler_params=params(),
        cost_estimate=pl.CostEstimate(flops=0, bytes_accessed=2 << 20, transcendentals=0),
    )(place, *pieces)


def join_kernel(y_ref, *refs):
    out_ref = refs[-1]
    for step in range(4):
        low = pl.multiple_of(64 * lax.rem(y_ref[0] + (4 - step), 4), 64)
        for pair in range(2):
            for kind in range(3):
                out_ref[3 * pair + kind, pl.ds(low, 64), :] = refs[step][pair, kind]


def join_shares(y, got):
    return pl.pallas_call(
        join_kernel,
        out_shape=jax.ShapeDtypeStruct((6, 256, 256), BF),
        in_specs=[smem()] + [vmem()] * 4,
        out_specs=vmem(),
        compiler_params=params(),
        cost_estimate=pl.CostEstimate(flops=0, bytes_accessed=2 << 20, transcendentals=0),
    )(y, *got)


def attend(chains):
    scores = [dot_t(query, key) for query, key, _, _ in chains]
    scores = [
        one if chain[3] is None else jnp.where(chain[3] < 0.0, chain[3], one)
        for one, chain in zip(scores, chains)
    ]
    weights = [softmax(one) for one in scores]
    return [dot(one, chain[2]).astype(BF) for one, chain in zip(weights, chains)]


def spatial_kernel(place_ref, weight_ref, *refs):
    pieces, out_ref, qkv = refs[: 2 * NZ], refs[2 * NZ], refs[2 * NZ + 1]
    place = place_ref[0]
    for frame in range(4):
        low = 32 * (frame % 2)
        rows = jnp.concatenate(
            [pieces[2 * k + frame // 2][low : low + 32, :] for k in range(NZ)], axis=0
        )
        for kind in range(3):
            qkv[kind, 256 * frame : 256 * frame + 256] = dot(rows, weight_ref[kind]).astype(BF)
    for frames in ((0, 1), (2, 3)):
        spots = [(frame, head * E) for frame in frames for head in range(2)]
        chains = []
        for frame, low in spots:
            at, cols = slice(256 * frame, 256 * frame + 256), slice(low, low + E)
            chains.append((qkv[0, at, cols], qkv[1, at, cols], qkv[2, at, cols], None))
        for (frame, low), mixed in zip(spots, attend(chains)):
            for k in range(NZ):
                target = lax.rem(place + (OFFSETS[k] + NZ), NZ)
                out_ref[target, 32 * frame : 32 * frame + 32, low : low + E] = mixed[
                    32 * k : 32 * k + 32
                ]


def spatial_attend(place, weight, pieces):
    return pl.pallas_call(
        spatial_kernel,
        out_shape=jax.ShapeDtypeStruct((NZ, 128, 256), BF),
        in_specs=[smem(), vmem()] + [vmem()] * len(pieces),
        out_specs=vmem(),
        scratch_shapes=[pltpu.VMEM((3, 1024, 256), BF)],
        compiler_params=params(),
        cost_estimate=pl.CostEstimate(
            flops=2 * 1024 * 2048 * 768 * 2, bytes_accessed=8 << 20, transcendentals=8 * 65536
        ),
    )(place, weight, *pieces)


def column_block(read):
    return jnp.concatenate([read(head, k // 4, k % 4) for k in range(NZ) for head in range(2)], axis=0)


def join_blocks_kernel(z_ref, *refs):
    out_ref = refs[-1]
    for step in range(4):
        out_ref[lax.rem(z_ref[0] + (4 - step), 4)] = refs[step][...]


def join_blocks(z, parts):
    return pl.pallas_call(
        join_blocks_kernel,
        out_shape=jax.ShapeDtypeStruct((4, 128, 256), BF),
        in_specs=[smem()] + [vmem()] * 4,
        out_specs=vmem(),
        compiler_params=params(),
        cost_estimate=pl.CostEstimate(flops=0, bytes_accessed=512 << 10, transcendentals=0),
    )(z, *parts)


def middle_kernel(mix_ref, weight_ref, rows_ref, gain_ref, middle_ref, send_ref, total):
    mix = jnp.concatenate([mix_ref[k] for k in range(NZ)], axis=1)
    for block in range(8):
        part = column_block(lambda *at: weight_ref[(block, *at)])
        total[:, 256 * block : 256 * block + 256] = dot(mix, part)
    middle = (total[...] + rows_ref[...].astype(F32)).astype(BF)
    middle_ref[...] = middle
    values = middle.astype(F32)
    scaled = values * lax.rsqrt(jnp.mean(values * values, axis=-1, keepdims=True) + 1e-05)
    scaled = scaled * gain_ref[...]
    for group in range(4):
        chunk = jnp.concatenate(
            [scaled[32 * f + 8 * group : 32 * f + 8 * group + 8] for f in range(4)], axis=0
        ).astype(BF)
        for y in range(4):
            send_ref[(group // 2) * 8 + y * 2 + group % 2] = chunk


def middle_rows(mix, weight, rows, gain):
    width = rows.shape[1]
    return pl.pallas_call(
        middle_kernel,
        out_shape=(
            jax.ShapeDtypeStruct((128, width), BF),
            jax.ShapeDtypeStruct((16, 32, width), BF),
        ),
        in_specs=[vmem()] * 4,
        out_specs=(vmem(), vmem()),
        scratch_shapes=[pltpu.VMEM((128, width), F32)],
        compiler_params=params(),
        cost_estimate=pl.CostEstimate(
            flops=2 * 128 * 2048 * 2048, bytes_accessed=12 << 20, transcendentals=0
        ),
    )(mix, weight, rows, gain)


def mask_kernel(start_ref, bias):
    count = bias.shape[0]
    start = start_ref[0]
    late = lax.broadcasted_iota(jnp.int32, (count, count), 0)
    early = lax.broadcasted_iota(jnp.int32, (count, count), 1)
    same = (late & 7) == (early & 7)
    allowed = same & (early <= late) & ((early >= 8 * start) == (late >= 8 * start))
    bias[...] = jnp.where(allowed, 0.0, -1e30)


def frame_mask(start, count):
    return pl.pallas_call(
        mask_kernel,
        out_shape=jax.ShapeDtypeStruct((count, count), F32),
        in_specs=[smem()],
        out_specs=vmem(),
        compiler_params=params(),
        cost_estimate=pl.CostEstimate(flops=16 << 20, bytes_accessed=16 << 20, transcendentals=0),
    )(start)


def temporal_kernel(rows_ref, weight_ref, bias, out_ref, qkv):
    count = rows_ref.shape[0]
    for block in range(6):
        qkv[block] = dot(rows_ref[...], weight_ref[:, block].reshape(2048, 256)).astype(BF)
    size = 256
    for pair in range(2):
        for low in range(0, count, size):
            chains = []
            high = low + size
            for head in range(2):
                cols = slice(head * E, head * E + E)
                chains.append(
                    (
                        qkv[3 * pair, low:high, cols],
                        qkv[3 * pair + 1, :high, cols],
                        qkv[3 * pair + 2, :high, cols],
                        bias[low:high, :high],
                    )
                )
            for head, mixed in enumerate(attend(chains)):
                for spot in range(low // 32, high // 32):
                    rows = mixed[32 * spot - low : 32 * spot - low + 32]
                    at = (spot // 2 * 2 + head, spot % 2, slice(None), slice(E * pair, E * pair + E))
                    out_ref[at] = rows


def temporal_attend(rows, weight, bias):
    count, width = rows.shape
    return pl.pallas_call(
        temporal_kernel,
        out_shape=jax.ShapeDtypeStruct((16, 2, 32, 256), BF),
        in_specs=[vmem()] * 3,
        out_specs=vmem(),
        scratch_shapes=[
            pltpu.VMEM((6, count, 256), BF),
        ],
        compiler_params=params(),
        cost_estimate=pl.CostEstimate(
            flops=2 * 512 * 2048 * 1536, bytes_accessed=9 << 20, transcendentals=131072
        ),
    )(rows, weight, bias)


def last_kernel(place_ref, mix_ref, *refs):
    pieces, (keep_ref, give_ref, total) = refs[: NZ + 1], refs[NZ + 1 :]
    z, c = place_ref[0], place_ref[1]
    blocks = []
    for k in range(NZ):
        source = lax.rem(z + (OFFSETS[k] + NZ), NZ)
        cols = pl.ds(pl.multiple_of(lax.rem(source, 2) * E, E), E)
        blocks.append(
            jnp.concatenate(
                [
                    mix_ref[xl * 8 + source // 2 * 2 + core, frames, :, cols]
                    for frames in range(2)
                    for xl in range(2)
                    for core in range(2)
                ],
                axis=0,
            )
        )
    mix = jnp.concatenate(blocks, axis=1)
    for low in range(0, 2048, 512):
        part = jnp.concatenate([piece[:, low : low + 512] for piece in pieces], axis=0)
        total[:, :, low : low + 512] = dot(mix, part).reshape(2, 128, 512)
    keep_ref[...] = total[c]
    give_ref[...] = total[1 - c].astype(BF)


def last_sums(place, mix, pieces):
    width = pieces[0].shape[1]
    return pl.pallas_call(
        last_kernel,
        out_shape=(
            jax.ShapeDtypeStruct((128, width), F32),
            jax.ShapeDtypeStruct((128, width), BF),
        ),
        in_specs=[smem()] + [vmem()] * (NZ + 2),
        out_specs=(vmem(), vmem()),
        scratch_shapes=[pltpu.VMEM((2, 128, width), F32)],
        compiler_params=params(),
        cost_estimate=pl.CostEstimate(
            flops=2 * 128 * 2048 * 2048, bytes_accessed=8 << 20, transcendentals=0
        ),
    )(place, mix, *pieces)


def end_kernel(keep_ref, got_ref, middle_ref, out_ref):
    for group in range(4):
        at = slice(32 * group, 32 * group + 32)
        rows = (keep_ref[at] + got_ref[at].astype(F32)).reshape(4, 8, -1)
        middle = jnp.stack(
            [
                middle_ref[32 * f : 32 * f + 32].astype(F32)[8 * group : 8 * group + 8]
                for f in range(4)
            ],
            axis=0,
        )
        out = jnp.transpose(rows + middle, (1, 0, 2)).astype(BF)
        out_ref[8 * group : 8 * group + 8] = out


def end_rows(keep, got, middle):
    return pl.pallas_call(
        end_kernel,
        out_shape=jax.ShapeDtypeStruct((32, 4, middle.shape[1]), BF),
        in_specs=[vmem()] * 3,
        out_specs=vmem(),
        compiler_params=params(),
        cost_estimate=pl.CostEstimate(flops=1 << 20, bytes_accessed=3 << 20, transcendentals=0),
    )(keep, got, middle)


def shifted(value, axis, step):
    count = lax.axis_size(axis)
    return lax.ppermute(value, axis, [(i, (i + step) % count) for i in range(count)])


def gathered_rows(chunks):
    up, down = list(chunks), list(chunks)
    pieces = {0: list(chunks)}
    for step in (1, 2, 3):
        up = [shifted(value, "z", 1) for value in up]
        down = [shifted(value, "z", -1) for value in down]
        pieces[-step], pieces[step] = up, down
    pieces[4] = [shifted(up[0], "z", 1), shifted(down[1], "z", -1)]
    return [value for offset in OFFSETS for value in pieces[offset]]


def local(stream, spatial_gain, spatial_qkv, spatial_out, temporal_gain, temporal_qkv, temporal_out, starts):
    patches, frames, width = stream.shape
    w, xl, y, c, z = (lax.axis_index(name) for name in ("w", "xl", "y", "c", "z"))

    place = (((w * 2 + xl) * 2 + c) * 4 + y).reshape(1)
    first, second, rows = norm_rows(
        place, stream, spatial_gain.reshape(1, width), jnp.transpose(temporal_qkv, (1, 0, 2))
    )

    low = (lax.rem(y, 2) * E, ((w * 2 + xl) * 2 + y // 2) * 256)
    block = lax.dynamic_slice(spatial_out, low, (E, 256))
    parts = []
    for k in range(4):
        pairs = [
            (a * 8 + b, (b // 4) * 8 + (b + 4 * a + k) % 8) for a in range(2) for b in range(8)
        ]
        parts.append(lax.ppermute(block, ("c", "z"), pairs))
    first, second, parts = lax.optimization_barrier((first, second, parts))
    whole_out = join_blocks(z.reshape(1), parts)
    whole_out = lax.all_gather(whole_out, ("w", "xl", "y", "c"), axis=0, tiled=False)
    whole_out = whole_out.reshape(8, 2, 2, 4, E, 256)

    pieces = gathered_rows((first, second))

    sends = split_shares(jnp.stack([z, y]).astype(jnp.int32), pieces)
    got = [sends[0]] + [shifted(sends[k], "y", k) for k in range(1, 4)]

    weight = jnp.transpose(spatial_qkv, (1, 0, 2))
    mix = spatial_attend(z.reshape(1), weight, pieces)
    mix, *got = lax.optimization_barrier((mix, *got))
    quarter = join_shares(y.reshape(1), got)
    mix, quarter, whole_out = lax.optimization_barrier((mix, quarter, whole_out))
    quarter = lax.all_gather(quarter[None], ("w", "xl", "c"), axis=0, tiled=True)
    mix = lax.all_to_all(mix, "z", 0, 0, tiled=True)

    middle, send = middle_rows(mix, whole_out, rows, temporal_gain.reshape(1, width))

    start = lax.dynamic_slice(starts, (w,), (1,))
    half = lax.dynamic_slice(temporal_out, (c * E, 0), (E, width))
    send, half = lax.optimization_barrier((send, half))
    up, down = half, half
    halves = [half]
    for step in (1, 2, 3):
        up, down = shifted(up, "z", 1), shifted(down, "z", -1)
        if step == 1:
            up, down, quarter, start = lax.optimization_barrier((up, down, quarter, start))
            bias = frame_mask(start, 512)
            up, down, bias = lax.optimization_barrier((up, down, bias))
        halves += [up, down]
    halves += [shifted(up[:64], "z", 1), shifted(down[64:], "z", -1)]

    window = lax.all_to_all(send, ("xl", "y", "c"), 0, 0, tiled=True)
    window, bias, *halves[1:5] = lax.optimization_barrier((window, bias, *halves[1:5]))
    mix = temporal_attend(window.reshape(512, width), quarter, bias)
    mix = lax.all_to_all(mix, ("xl", "y", "c"), 0, 0, tiled=True)
    keep, give = last_sums(jnp.stack([z, c]).astype(jnp.int32), mix, halves)
    return end_rows(keep, shifted(give, "c", 1), middle)


def solution(mesh):
    names = ("w", "xl", "y", "c", "z")
    fine = Mesh(mesh.devices.reshape(2, 2, 4, 2, NZ), names)
    tm = ("w", "xl", "y", "c")
    placed = (
        P("z", tm, None),
        P(),
        P(None, None, "z"),
        P("z", None),
        P(),
        P(None, None, "z"),
        P("z", None),
        P(),
    )
    return jax.shard_map(
        local, mesh=fine, in_specs=placed, out_specs=P("z", tm, None), check_vma=False
    )
```

```python
import functools
import math

import jax
import jax.numpy as jnp
from jax import lax
from jax.experimental import pallas as pl
from jax.experimental.pallas import tpu as pltpu
from jax.sharding import Mesh
from jax.sharding import PartitionSpec as P

E = 128
SEQ = 64
SCALE = 1.0 / math.sqrt(E)
BF = jnp.bfloat16
F32 = jnp.float32
NZ = 8
VMEM_LIMIT = 18 * 1024 * 1024
OFFSETS = (0, -1, 1, -2, 2, -3, 3, 4)


def params():
    return pltpu.CompilerParams(vmem_limit_bytes=VMEM_LIMIT)


def vmem():
    return pl.BlockSpec(memory_space=pltpu.VMEM)


def smem():
    return pl.BlockSpec(memory_space=pltpu.SMEM)


def normed(values, gain):
    scaled = values * lax.rsqrt(jnp.mean(values * values, axis=-1, keepdims=True) + 1e-05)
    return (scaled * gain).astype(BF)


def softmax(scores):
    top = jnp.max(scores, axis=-1, keepdims=True)
    shifted = jnp.exp2((scores - top) * (SCALE * math.log2(math.e)))
    return (shifted * (1.0 / jnp.sum(shifted, axis=-1, keepdims=True))).astype(BF)


def dot(a, b):
    return jnp.dot(a, b, preferred_element_type=F32)


def dot_t(a, b):
    return lax.dot_general(a, b, (((1,), (1,)), ((), ())), preferred_element_type=F32)


def norm_kernel(place_ref, x_ref, gain_ref, qkv_ref, a_ref, b_ref, rows_ref):
    gain = gain_ref[...]
    values = jnp.transpose(x_ref[...].astype(F32), (1, 0, 2)).reshape(rows_ref.shape)
    half = rows_ref.shape[0] // 2
    rows_ref[...] = values.astype(BF)
    a_ref[:half] = normed(values[:half], gain)
    b_ref[:half] = normed(values[half:], gain)
    b_ref[half:, 1024:] = jnp.zeros((16, 1024), BF)
    for kind in range(3):
        share = qkv_ref[kind]
        ref = (a_ref, b_ref)[kind // 2]
        for group in range(4):
            low = 256 * (4 * (kind % 2) + group)
            ref[half:, low : low + 256] = share[16 * group : 16 * group + 16]


def norm_rows(place, stream, gain, temporal_qkv):
    patches, frames, width = stream.shape
    count = patches * frames
    half = jax.ShapeDtypeStruct((count // 2 + 16, width), BF)
    whole = lambda *shape: pl.BlockSpec(shape, lambda i, at: (0,) * len(shape))
    return pl.pallas_call(
        norm_kernel,
        grid_spec=pltpu.PrefetchScalarGridSpec(
            num_scalar_prefetch=1,
            grid=(1,),
            in_specs=[
                whole(patches, frames, width),
                whole(1, width),
                pl.BlockSpec((3, 64, 256), lambda i, at: (0, at[0], 0)),
            ],
            out_specs=(
                whole(count // 2 + 16, width),
                whole(count // 2 + 16, width),
                whole(count, width),
            ),
        ),
        out_shape=(half, half, jax.ShapeDtypeStruct((count, width), BF)),
        compiler_params=params(),
        cost_estimate=pl.CostEstimate(
            flops=4 * count * width, bytes_accessed=6 * count * width, transcendentals=0
        ),
    )(place, stream, gain, temporal_qkv)


def split_kernel(place_ref, *refs):
    pieces, sends = refs[:-4], refs[-4:]
    z, y = place_ref[0], place_ref[1]
    for k in range(NZ):
        source = lax.rem(z + (OFFSETS[k] + NZ), NZ)
        step = lax.rem(source // 2 + 4 - y, 4)
        pair = lax.rem(source, 2)
        for index, send_ref in enumerate(sends):

            @pl.when(step == index)
            def _():
                for kind in range(3):
                    for group in range(4):
                        low = 256 * (4 * (kind % 2) + group)
                        rows = slice(16 * group, 16 * group + 16)
                        value = pieces[2 * k + kind // 2][:, low : low + 256]
                        send_ref[pair, kind, rows] = value


def split_shares(place, pieces):
    return pl.pallas_call(
        split_kernel,
        grid=(1,),
        out_shape=(jax.ShapeDtypeStruct((2, 3, 64, 256), BF),) * 4,
        in_specs=[smem()] + [pl.BlockSpec((16, 2048), lambda i: (4, 0))] * len(pieces),
        out_specs=(pl.BlockSpec((2, 3, 64, 256), lambda i: (0, 0, 0, 0)),) * 4,
        compiler_params=params(),
        cost_estimate=pl.CostEstimate(flops=0, bytes_accessed=2 << 20, transcendentals=0),
    )(place, *pieces)


def join_kernel(y_ref, *refs):
    out_ref = refs[-1]
    for step in range(4):
        low = pl.multiple_of(64 * lax.rem(y_ref[0] + (4 - step), 4), 64)
        for pair in range(2):
            for kind in range(3):
                out_ref[3 * pair + kind, pl.ds(low, 64), :] = refs[step][pair, kind]


def join_shares(y, got):
    return pl.pallas_call(
        join_kernel,
        out_shape=jax.ShapeDtypeStruct((6, 256, 256), BF),
        in_specs=[smem()] + [vmem()] * 4,
        out_specs=vmem(),
        compiler_params=params(),
        cost_estimate=pl.CostEstimate(flops=0, bytes_accessed=2 << 20, transcendentals=0),
    )(y, *got)


def attend(chains):
    scores = [dot_t(query, key) for query, key, _, _ in chains]
    scores = [
        one if chain[3] is None else jnp.where(chain[3] < 0.0, chain[3], one)
        for one, chain in zip(scores, chains)
    ]
    weights = [softmax(one) for one in scores]
    return [dot(one, chain[2]).astype(BF) for one, chain in zip(weights, chains)]


def spatial_kernel(place_ref, weight_ref, *refs):
    pieces, out_ref, qkv = refs[: 2 * NZ], refs[2 * NZ], refs[2 * NZ + 1]
    place = place_ref[0]
    for frame in range(4):
        low = 32 * (frame % 2)
        rows = jnp.concatenate(
            [pieces[2 * k + frame // 2][low : low + 32, :] for k in range(NZ)], axis=0
        )
        for kind in range(3):
            qkv[kind, 256 * frame : 256 * frame + 256] = dot(rows, weight_ref[kind]).astype(BF)
    for frames in ((0, 1), (2, 3)):
        spots = [(frame, head * E) for frame in frames for head in range(2)]
        chains = []
        for frame, low in spots:
            at, cols = slice(256 * frame, 256 * frame + 256), slice(low, low + E)
            chains.append((qkv[0, at, cols], qkv[1, at, cols], qkv[2, at, cols], None))
        for (frame, low), mixed in zip(spots, attend(chains)):
            for k in range(NZ):
                target = lax.rem(place + (OFFSETS[k] + NZ), NZ)
                out_ref[target, 32 * frame : 32 * frame + 32, low : low + E] = mixed[
                    32 * k : 32 * k + 32
                ]


def spatial_attend(place, weight, pieces):
    return pl.pallas_call(
        spatial_kernel,
        out_shape=jax.ShapeDtypeStruct((NZ, 128, 256), BF),
        in_specs=[smem(), vmem()] + [vmem()] * len(pieces),
        out_specs=vmem(),
        scratch_shapes=[pltpu.VMEM((3, 1024, 256), BF)],
        compiler_params=params(),
        cost_estimate=pl.CostEstimate(
            flops=2 * 1024 * 2048 * 768 * 2, bytes_accessed=8 << 20, transcendentals=8 * 65536
        ),
    )(place, weight, *pieces)


def column_block(read):
    return jnp.concatenate([read(head, k // 4, k % 4) for k in range(NZ) for head in range(2)], axis=0)


def join_blocks_kernel(z_ref, *refs):
    out_ref = refs[-1]
    for step in range(4):
        out_ref[lax.rem(z_ref[0] + (4 - step), 4)] = refs[step][...]


def join_blocks(z, parts):
    return pl.pallas_call(
        join_blocks_kernel,
        out_shape=jax.ShapeDtypeStruct((4, 128, 256), BF),
        in_specs=[smem()] + [vmem()] * 4,
        out_specs=vmem(),
        compiler_params=params(),
        cost_estimate=pl.CostEstimate(flops=0, bytes_accessed=512 << 10, transcendentals=0),
    )(z, *parts)


def middle_kernel(mix_ref, weight_ref, rows_ref, gain_ref, middle_ref, send_ref, total):
    mix = jnp.concatenate([mix_ref[k] for k in range(NZ)], axis=1)
    for block in range(8):
        part = column_block(lambda *at: weight_ref[(block, *at)])
        total[:, 256 * block : 256 * block + 256] = dot(mix, part)
    middle = (total[...] + rows_ref[...].astype(F32)).astype(BF)
    middle_ref[...] = middle
    values = middle.astype(F32)
    scaled = values * lax.rsqrt(jnp.mean(values * values, axis=-1, keepdims=True) + 1e-05)
    scaled = scaled * gain_ref[...]
    for group in range(4):
        chunk = jnp.concatenate(
            [scaled[32 * f + 8 * group : 32 * f + 8 * group + 8] for f in range(4)], axis=0
        ).astype(BF)
        for y in range(4):
            send_ref[(group // 2) * 8 + y * 2 + group % 2] = chunk


def middle_rows(mix, weight, rows, gain):
    width = rows.shape[1]
    return pl.pallas_call(
        middle_kernel,
        out_shape=(
            jax.ShapeDtypeStruct((128, width), BF),
            jax.ShapeDtypeStruct((16, 32, width), BF),
        ),
        in_specs=[vmem()] * 4,
        out_specs=(vmem(), vmem()),
        scratch_shapes=[pltpu.VMEM((128, width), F32)],
        compiler_params=params(),
        cost_estimate=pl.CostEstimate(
            flops=2 * 128 * 2048 * 2048, bytes_accessed=12 << 20, transcendentals=0
        ),
    )(mix, weight, rows, gain)


def temporal_kernel(start_ref, rows_ref, weight_ref, out_ref, qkv, bias):
    count = rows_ref.shape[0]
    start = start_ref[0]
    late = lax.broadcasted_iota(jnp.int32, (count, count), 0)
    early = lax.broadcasted_iota(jnp.int32, (count, count), 1)
    same = (late & 7) == (early & 7)
    allowed = same & (early <= late) & ((early >= 8 * start) == (late >= 8 * start))
    bias[...] = jnp.where(allowed, 0.0, -1e30)
    for block in range(6):
        qkv[block] = dot(rows_ref[...], weight_ref[:, block].reshape(2048, 256)).astype(BF)
    size = 256
    for pair in range(2):
        for low in range(0, count, size):
            chains = []
            high = low + size
            for head in range(2):
                cols = slice(head * E, head * E + E)
                chains.append(
                    (
                        qkv[3 * pair, low:high, cols],
                        qkv[3 * pair + 1, :high, cols],
                        qkv[3 * pair + 2, :high, cols],
                        bias[low:high, :high],
                    )
                )
            for head, mixed in enumerate(attend(chains)):
                for spot in range(low // 32, high // 32):
                    rows = mixed[32 * spot - low : 32 * spot - low + 32]
                    at = (spot // 2 * 2 + head, spot % 2, slice(None), slice(E * pair, E * pair + E))
                    out_ref[at] = rows


def temporal_attend(start, rows, weight):
    count, width = rows.shape
    return pl.pallas_call(
        temporal_kernel,
        out_shape=jax.ShapeDtypeStruct((16, 2, 32, 256), BF),
        in_specs=[smem(), vmem(), vmem()],
        out_specs=vmem(),
        scratch_shapes=[
            pltpu.VMEM((6, count, 256), BF),
            pltpu.VMEM((count, count), F32),
        ],
        compiler_params=params(),
        cost_estimate=pl.CostEstimate(
            flops=2 * 512 * 2048 * 1536, bytes_accessed=9 << 20, transcendentals=131072
        ),
    )(start, rows, weight)


def last_kernel(place_ref, mix_ref, *refs):
    pieces, (keep_ref, give_ref, total) = refs[: NZ + 1], refs[NZ + 1 :]
    z, c = place_ref[0], place_ref[1]
    blocks = []
    for k in range(NZ):
        source = lax.rem(z + (OFFSETS[k] + NZ), NZ)
        cols = pl.ds(pl.multiple_of(lax.rem(source, 2) * E, E), E)
        blocks.append(
            jnp.concatenate(
                [
                    mix_ref[xl * 8 + source // 2 * 2 + core, frames, :, cols]
                    for frames in range(2)
                    for xl in range(2)
                    for core in range(2)
                ],
                axis=0,
            )
        )
    mix = jnp.concatenate(blocks, axis=1)
    for low in range(0, 2048, 512):
        part = jnp.concatenate([piece[:, low : low + 512] for piece in pieces], axis=0)
        total[:, :, low : low + 512] = dot(mix, part).reshape(2, 128, 512)
    keep_ref[...] = total[c]
    give_ref[...] = total[1 - c].astype(BF)


def last_sums(place, mix, pieces):
    width = pieces[0].shape[1]
    return pl.pallas_call(
        last_kernel,
        out_shape=(
            jax.ShapeDtypeStruct((128, width), F32),
            jax.ShapeDtypeStruct((128, width), BF),
        ),
        in_specs=[smem()] + [vmem()] * (NZ + 2),
        out_specs=(vmem(), vmem()),
        scratch_shapes=[pltpu.VMEM((2, 128, width), F32)],
        compiler_params=params(),
        cost_estimate=pl.CostEstimate(
            flops=2 * 128 * 2048 * 2048, bytes_accessed=8 << 20, transcendentals=0
        ),
    )(place, mix, *pieces)


def end_kernel(keep_ref, got_ref, middle_ref, out_ref):
    for group in range(4):
        at = slice(32 * group, 32 * group + 32)
        rows = (keep_ref[at] + got_ref[at].astype(F32)).reshape(4, 8, -1)
        middle = jnp.stack(
            [
                middle_ref[32 * f : 32 * f + 32].astype(F32)[8 * group : 8 * group + 8]
                for f in range(4)
            ],
            axis=0,
        )
        out = jnp.transpose(rows + middle, (1, 0, 2)).astype(BF)
        out_ref[8 * group : 8 * group + 8] = out


def end_rows(keep, got, middle):
    return pl.pallas_call(
        end_kernel,
        out_shape=jax.ShapeDtypeStruct((32, 4, middle.shape[1]), BF),
        in_specs=[vmem()] * 3,
        out_specs=vmem(),
        compiler_params=params(),
        cost_estimate=pl.CostEstimate(flops=1 << 20, bytes_accessed=3 << 20, transcendentals=0),
    )(keep, got, middle)


def shifted(value, axis, step):
    count = lax.axis_size(axis)
    return lax.ppermute(value, axis, [(i, (i + step) % count) for i in range(count)])


def gathered_rows(chunks):
    up, down = list(chunks), list(chunks)
    pieces = {0: list(chunks)}
    for step in (1, 2, 3):
        up = [shifted(value, "z", 1) for value in up]
        down = [shifted(value, "z", -1) for value in down]
        pieces[-step], pieces[step] = up, down
    pieces[4] = [shifted(up[0], "z", 1), shifted(down[1], "z", -1)]
    return [value for offset in OFFSETS for value in pieces[offset]]


def local(stream, spatial_gain, spatial_qkv, spatial_out, temporal_gain, temporal_qkv, temporal_out, starts):
    patches, frames, width = stream.shape
    w, xl, y, c, z = (lax.axis_index(name) for name in ("w", "xl", "y", "c", "z"))

    place = (((w * 2 + xl) * 2 + c) * 4 + y).reshape(1)
    first, second, rows = norm_rows(
        place, stream, spatial_gain.reshape(1, width), jnp.transpose(temporal_qkv, (1, 0, 2))
    )

    low = (lax.rem(y, 2) * E, ((w * 2 + xl) * 2 + y // 2) * 256)
    block = lax.dynamic_slice(spatial_out, low, (E, 256))
    parts = []
    for k in range(4):
        pairs = [
            (a * 8 + b, (b // 4) * 8 + (b + 4 * a + k) % 8) for a in range(2) for b in range(8)
        ]
        parts.append(lax.ppermute(block, ("c", "z"), pairs))
    first, second, parts = lax.optimization_barrier((first, second, parts))
    whole_out = join_blocks(z.reshape(1), parts)
    whole_out = lax.all_gather(whole_out, ("w", "xl", "y", "c"), axis=0, tiled=False)
    whole_out = whole_out.reshape(8, 2, 2, 4, E, 256)

    pieces = gathered_rows((first, second))

    sends = split_shares(jnp.stack([z, y]).astype(jnp.int32), pieces)
    got = [sends[0]] + [shifted(sends[k], "y", k) for k in range(1, 4)]

    weight = jnp.transpose(spatial_qkv, (1, 0, 2))
    mix = spatial_attend(z.reshape(1), weight, pieces)
    mix, *got = lax.optimization_barrier((mix, *got))
    quarter = join_shares(y.reshape(1), got)
    mix, quarter, whole_out = lax.optimization_barrier((mix, quarter, whole_out))
    quarter = lax.all_gather(quarter[None], ("w", "xl", "c"), axis=0, tiled=True)
    mix = lax.all_to_all(mix, "z", 0, 0, tiled=True)

    middle, send = middle_rows(mix, whole_out, rows, temporal_gain.reshape(1, width))

    half = lax.dynamic_slice(temporal_out, (c * E, 0), (E, width))
    send, half = lax.optimization_barrier((send, half))
    up, down = half, half
    halves = [half]
    for step in (1, 2, 3):
        up, down = shifted(up, "z", 1), shifted(down, "z", -1)
        halves += [up, down]
    halves += [shifted(up[:64], "z", 1), shifted(down[64:], "z", -1)]

    window = lax.all_to_all(send, ("xl", "y", "c"), 0, 0, tiled=True)
    window, *halves[1:5] = lax.optimization_barrier((window, *halves[1:5]))
    start = lax.dynamic_slice(starts, (w,), (1,))
    mix = temporal_attend(start, window.reshape(512, width), quarter)
    mix = lax.all_to_all(mix, ("xl", "y", "c"), 0, 0, tiled=True)
    keep, give = last_sums(jnp.stack([z, c]).astype(jnp.int32), mix, halves)
    return end_rows(keep, shifted(give, "c", 1), middle)


def solution(mesh):
    names = ("w", "xl", "y", "c", "z")
    fine = Mesh(mesh.devices.reshape(2, 2, 4, 2, NZ), names)
    tm = ("w", "xl", "y", "c")
    placed = (
        P("z", tm, None),
        P(),
        P(None, None, "z"),
        P("z", None),
        P(),
        P(None, None, "z"),
        P("z", None),
        P(),
    )
    return jax.shard_map(
        local, mesh=fine, in_specs=placed, out_specs=P("z", tm, None), check_vma=False
    )
```
